32 devices in a mesh: grp: 4 (over y, core), ctx: 8 (over z, x).
Axes of the slice: x: 2, y: 2, z: 4, core: 2. Of those that a mesh axis runs over, the one named last changes fastest.
Arguments:
- tokens: bfloat16 [16, 4224, 512], P('grp', 'ctx'), may hold values from -6 to 6
- query_counts: int32 [16], P('grp'), may hold values from 1 to 128, as said below
- cotangent: bfloat16 [16, 4224, 512], P('grp', 'ctx'), may hold values from -6 to 6
- query_weight: bfloat16 [512, 512], replicated, may hold values from -0.25 to 0.25
- key_weight: bfloat16 [512, 512], replicated, may hold values from -0.25 to 0.25
- value_weight: bfloat16 [512, 512], replicated, may hold values from -0.25 to 0.25
- output_weight: bfloat16 [512, 512], replicated, may hold values from -4 to 4
- inner_weight: bfloat16 [512, 1024], replicated, may hold values from -0.25 to 0.25
- inner_bias: bfloat16 [1024], replicated, may hold values from -1.5 to 1.5
- outer_weight: bfloat16 [1024, 512], replicated, may hold values from -0.1875 to 0.1875
- outer_bias: bfloat16 [512], replicated, may hold values from -1.5 to 1.5
- first_gain: bfloat16 [512], replicated, may hold values from 0.25 to 1.75
- first_shift: bfloat16 [512], replicated, may hold values from -1.5 to 1.5
- second_gain: bfloat16 [512], replicated, may hold values from 0.25 to 1.75
- second_shift: bfloat16 [512], replicated, may hold values from -1.5 to 1.5
Outputs:
- layer_out: bfloat16 [16, 4224, 512], P('grp', 'ctx')
- grad_tokens: float32 [16, 4224, 512], P('grp', 'ctx')
- grad_query: float32 [512, 512], replicated
- grad_key: float32 [512, 512], replicated
- grad_value: float32 [512, 512], replicated
- grad_output: float32 [512, 512], replicated
- grad_inner: float32 [512, 1024], replicated
- grad_inner_bias: float32 [1024], replicated
- grad_outer: float32 [1024, 512], replicated
- grad_outer_bias: float32 [512], replicated
- grad_first_gain: float32 [512], replicated
- grad_first_shift: float32 [512], replicated
- grad_second_gain: float32 [512], replicated
- grad_second_shift: float32 [512], replicated
The draws below stay inside these ranges and needn't reach their ends.
Inputs may be any that keep to these rules, and one draw needn't show every extreme that they name: `query_counts`: for every g, among neighbourhoods g * 4 to g * 4 + 3 at least one has exactly 128 live queries.
All inputs are finite; a program needn't handle non-finite values.
Results may differ from the reference program's by a relative error of at most 0.013.
Values may be sent and summed in bfloat16 or wider, within the bound.
No kernel may reach another device: no remote copies, remote signals or barrier semaphores. Data moves between devices by JAX's collectives and lax.ppermute only.
A program may use at most 832 MiB of HBM per device.

```python
import jax
import jax.numpy as jnp
from jax import lax

D = 512
HEADS = 4
FF = 1024
CTX = 4096
QUERIES = 128
NB = 4
HD = 128
CTX_DEV = 512
QS_DEV = 16
ROWS = 4224
NEIGH = 16
N_CTX = 8


def draw_query_counts(key, part):
    key = jax.random.fold_in(key, 7)
    count_key, choose_key = jax.random.split(key)
    groups = NEIGH // NB
    counts = jax.random.randint(count_key, (groups, NB), 1, QUERIES + 1)
    chosen = jax.random.randint(choose_key, (groups, 1), 0, NB)
    full_mask = jnp.arange(NB)[None, :] == chosen
    return jnp.where(full_mask, QUERIES, counts).reshape(NEIGH).astype(jnp.int32)


def block_levels(stream_key, extent, cuts, smallest, high):
    factor_of = 1.0
    for position, shards_of in cuts:
        draws = jax.random.uniform(jax.random.fold_in(jax.random.fold_in(stream_key, 6), position), (shards_of,), jnp.float32, smallest / len(cuts), high / len(cuts))
        factor_of = factor_of * jnp.repeat(jnp.exp(draws), extent[position] // shards_of).reshape((-1,) + (1,) * (len(extent) - 1 - position))
    return factor_of


def scatter_about(key, shape, scale, most, pieces=(), kind=jnp.bfloat16):
    drawn = scale * jax.random.normal(key, shape, jnp.float32)
    if pieces:
        drawn = drawn * block_levels(key, shape, pieces, -0.22, 0.18)
    return jnp.clip(drawn, -most, most).astype(kind)


def setup_inputs(seed: int = 0) -> dict:
    arg_keys = jax.random.split(jax.random.key(seed), 16)
    return {
        "tokens": scatter_about(arg_keys[0], (NEIGH, ROWS, D), 1.0, 6.0, ((0, 4), (1, 8))),
        "query_counts": draw_query_counts(jax.random.fold_in(arg_keys[15], 71), 0),
        "cotangent": scatter_about(arg_keys[2], (NEIGH, ROWS, D), 1.0, 6.0, ((0, 4), (1, 8))),
        "query_weight": scatter_about(arg_keys[3], (D, D), D ** -0.5, 0.25),
        "key_weight": scatter_about(arg_keys[4], (D, D), D ** -0.5, 0.25),
        "value_weight": scatter_about(arg_keys[5], (D, D), D ** -0.5, 0.25),
        "output_weight": scatter_about(arg_keys[6], (D, D), (max(4 * D // CTX, 2)) ** -0.5, 4.0),
        "inner_weight": scatter_about(arg_keys[7], (D, FF), D ** -0.5, 0.25),
        "inner_bias": scatter_about(arg_keys[8], (FF,), 0.3, 1.5),
        "outer_weight": scatter_about(arg_keys[9], (FF, D), FF ** -0.5, 0.1875),
        "outer_bias": scatter_about(arg_keys[10], (D,), 0.3, 1.5),
        "first_gain": jnp.clip(1.0 + 0.15 * jax.random.normal(arg_keys[11], (D,), jnp.float32), 0.25, 1.75).astype(jnp.bfloat16),
        "first_shift": scatter_about(arg_keys[12], (D,), 0.3, 1.5),
        "second_gain": jnp.clip(1.0 + 0.15 * jax.random.normal(arg_keys[13], (D,), jnp.float32), 0.25, 1.75).astype(jnp.bfloat16),
        "second_shift": scatter_about(arg_keys[14], (D,), 0.3, 1.5),
    }


@jax.custom_vjp
def low(v):
    return lax.optimization_barrier(v.astype(jnp.bfloat16)).astype(jnp.float32)

@jax.custom_vjp
def low_back(v):
    return v

def low_keep(v):
    return (low(v), None)

def low_pass(kept, grad):
    return (grad,)

def back_keep(v):
    return (v, None)

def back_low(kept, grad):
    return (low(grad),)
low.defvjp(low_keep, low_pass)
low_back.defvjp(back_keep, back_low)
EPSILON = 1e-05

def matmul(left, right):
    return jnp.dot(left, right, precision=lax.Precision.HIGHEST, preferred_element_type=jnp.float32)

def layer_norm(values, gain, shift):
    center = values - lax.optimization_barrier(jnp.mean(values, axis=-1, keepdims=True))
    spread = lax.optimization_barrier(jnp.mean(center * center, axis=-1, keepdims=True))
    return center * lax.rsqrt(spread + EPSILON) * gain + shift

def one_head(operands):
    query_head, key_head, value_head = operands
    scores = low_back(matmul(query_head, key_head.T) * HD ** (-0.5))
    log_total = jax.nn.logsumexp(scores, axis=-1, keepdims=True)
    soft = jnp.exp(scores - log_total)
    return low_back(matmul(low(soft), value_head))

def neighbourhood(tokens_one, live_one, weights):
    query_weight, key_weight, value_weight, output_weight, inner_weight, inner_bias, outer_weight, outer_bias, first_gain, first_shift, second_gain, second_shift = weights
    blocks = tokens_one.reshape(N_CTX, CTX_DEV + QS_DEV, D)
    context_rows = blocks[:, :CTX_DEV].reshape(CTX, D)
    queries_all = low(low_back(matmul(tokens_one, query_weight)))
    keys_all = low(low_back(matmul(context_rows, key_weight)))
    values_all = low(low_back(matmul(context_rows, value_weight)))
    query_heads = queries_all.reshape(ROWS, HEADS, HD).transpose(1, 0, 2)
    key_heads = keys_all.reshape(CTX, HEADS, HD).transpose(1, 0, 2)
    value_heads = values_all.reshape(CTX, HEADS, HD).transpose(1, 0, 2)
    mixed = lax.map(jax.checkpoint(one_head), (query_heads, key_heads, value_heads))
    attended = low(mixed.transpose(1, 0, 2).reshape(ROWS, D))
    branch = low_back(matmul(attended, output_weight))
    hidden = layer_norm(tokens_one + branch, first_gain, first_shift)
    inner = low_back(matmul(low(hidden), inner_weight) + inner_bias)
    activated = low(jax.nn.gelu(inner, approximate=False))
    outer = low_back(matmul(activated, outer_weight) + outer_bias)
    result = layer_norm(hidden + outer, second_gain, second_shift)
    return result * live_one[:, None]

def reference(tokens, query_counts, cotangent, query_weight, key_weight, value_weight, output_weight, inner_weight, inner_bias, outer_weight, outer_bias, first_gain, first_shift, second_gain, second_shift):
    weights = tuple((item.astype(jnp.float32) for item in (query_weight, key_weight, value_weight, output_weight, inner_weight, inner_bias, outer_weight, outer_bias, first_gain, first_shift, second_gain, second_shift)))
    tokens_float = tokens.astype(jnp.float32)
    slot_local = jnp.arange(CTX_DEV + QS_DEV, dtype=jnp.int32) - CTX_DEV
    member_ids = jnp.arange(N_CTX, dtype=jnp.int32)
    slot_index = member_ids[:, None] * QS_DEV + slot_local[None, :]
    is_context = jnp.broadcast_to(slot_local[None, :] < 0, (N_CTX, CTX_DEV + QS_DEV))
    live_bool = jnp.logical_or(is_context[None], slot_index[None] < query_counts.astype(jnp.int32)[:, None, None])
    live = live_bool.astype(jnp.float32).reshape(NEIGH, ROWS)

    def forward(tokens_in, weights_in):

        def step(carry, operands):
            out_rows = jax.checkpoint(neighbourhood)(operands[0], operands[1], weights_in)
            return (carry, out_rows)
        _, stacked = lax.scan(step, jnp.zeros((), jnp.float32), (tokens_in, live))
        return stacked
    layer, pullback = jax.vjp(forward, tokens_float, weights)
    token_grads, weight_grads = pullback(cotangent.astype(jnp.float32))
    return (layer.astype(jnp.bfloat16), token_grads) + tuple(weight_grads)
```

```python
from functools import partial

import jax
import jax.numpy as jnp
from jax import lax
from jax.experimental import pallas as pl
from jax.experimental.pallas import tpu as pltpu
from jax.sharding import PartitionSpec as P

HEADS = 4
CTX = 4096
QUERIES = 128
NBLK = 4
HD = 128


EPSILON = 1e-05


def product(left, right):
    return jnp.dot(left, right, preferred_element_type=jnp.float32)


def contract_rows(left, right):
    return lax.dot_general(
        left, right, (((0,), (0,)), ((), ())), preferred_element_type=jnp.float32
    )


def contract_last(left, right):
    return lax.dot_general(
        left, right, (((1,), (1,)), ((), ())), preferred_element_type=jnp.float32
    )


def norm_forward(values, gain, shift):
    center = values - jnp.mean(values, axis=-1, keepdims=True)
    inverse = lax.rsqrt(jnp.mean(center * center, axis=-1, keepdims=True) + EPSILON)
    normed = center * inverse
    return (normed * gain + shift, normed, inverse)


def norm_backward(upstream, normed, inverse, gain):
    scaled = upstream * gain
    plain_mean = jnp.mean(scaled, axis=-1, keepdims=True)
    cross_mean = jnp.mean(scaled * normed, axis=-1, keepdims=True)
    value_grad = inverse * (scaled - plain_mean - normed * cross_mean)
    return (value_grad, jnp.sum(upstream * normed, axis=0), jnp.sum(upstream, axis=0))


def spread_plan(
    tokens,
    query_counts,
    cotangent,
    query_weight,
    key_weight,
    value_weight,
    output_weight,
    inner_weight,
    inner_bias,
    outer_weight,
    outer_bias,
    first_gain,
    first_shift,
    second_gain,
    second_shift,
):
    member = lax.axis_index("ctx")
    ctx_count = lax.axis_size("ctx")
    context_dev = CTX // ctx_count
    query_dev = QUERIES // ctx_count
    nb_dev = tokens.shape[0]
    rows_dev = tokens.shape[1]
    width = tokens.shape[2]
    heads_count = HEADS
    head_width = HD
    block_count = nb_dev // NBLK
    scale = head_width ** (-0.5)
    total_rows = nb_dev * rows_dev
    tokens_flat = tokens.reshape(total_rows, width)
    context_rows = tokens[:, :context_dev]
    context_flat = context_rows.reshape(nb_dev * context_dev, width)
    queries = (
        product(tokens_flat, query_weight).astype(jnp.bfloat16).reshape(nb_dev, rows_dev, width)
    )
    keys_own = (
        product(context_flat, key_weight).astype(jnp.bfloat16).reshape(nb_dev, context_dev, width)
    )
    values_own = (
        product(context_flat, value_weight).astype(jnp.bfloat16).reshape(nb_dev, context_dev, width)
    )
    sources = (keys_own, values_own)

    def to_blocks(array):
        return array.reshape((block_count, NBLK) + array.shape[1:])

    def fetch(source):
        keys_mine, values_mine = source
        keys_flat, values_flat = (
            lax.all_gather(keys_mine, "ctx", axis=1, tiled=True),
            lax.all_gather(values_mine, "ctx", axis=1, tiled=True),
        )
        return (keys_flat, values_flat, keys_mine, values_mine)

    def split_heads(array):
        return array.reshape(array.shape[0], array.shape[1], heads_count, head_width)

    def attend(carry, operands):
        queries_blk, source = operands
        keys_flat, values_flat, keys_mine, values_mine = fetch(source)
        query_heads = split_heads(queries_blk)
        scores = (
            jnp.einsum(
                "nrhd,nkhd->nhrk",
                query_heads,
                split_heads(keys_flat),
                preferred_element_type=jnp.float32,
            )
            * scale
        )
        log_total = jax.nn.logsumexp(scores, axis=-1, keepdims=True)
        soft_low = jnp.exp(scores - log_total).astype(jnp.bfloat16)
        mixed = jnp.einsum(
            "nhrk,nkhd->nrhd",
            soft_low,
            split_heads(values_flat),
            preferred_element_type=jnp.float32,
        )
        attended_blk = mixed.reshape(NBLK, rows_dev, width).astype(jnp.bfloat16)
        return (carry, (attended_blk, log_total[..., 0]))

    zero = jnp.zeros((), jnp.float32)
    _, (attended_b, lse_b) = lax.scan(
        attend, zero, (to_blocks(queries), jax.tree.map(to_blocks, sources))
    )
    attended_flat = attended_b.reshape(total_rows, width)
    slot_local = jnp.arange(rows_dev, dtype=jnp.int32) - context_dev
    slot_global = member * query_dev + slot_local
    live_rows = jnp.logical_or(
        slot_local[None, :] < 0, slot_global[None, :] < query_counts[:, None]
    )
    live_flat = live_rows.astype(jnp.float32).reshape(total_rows, 1)
    inner_bias_f = inner_bias.astype(jnp.float32)
    outer_bias_f = outer_bias.astype(jnp.float32)
    first_gain_f = first_gain.astype(jnp.float32)
    second_gain_f = second_gain.astype(jnp.float32)
    first_sum = tokens_flat.astype(jnp.float32) + product(attended_flat, output_weight)
    hidden, normed_one, inverse_one = norm_forward(
        first_sum, first_gain_f, first_shift.astype(jnp.float32)
    )
    hidden_low = hidden.astype(jnp.bfloat16)
    inner = product(hidden_low, inner_weight) + inner_bias_f
    gelu_value, gelu_back = jax.vjp(partial(jax.nn.gelu, approximate=False), inner)
    activated = gelu_value.astype(jnp.bfloat16)
    second_sum = hidden + product(activated, outer_weight) + outer_bias_f
    result, normed_two, inverse_two = norm_forward(
        second_sum, second_gain_f, second_shift.astype(jnp.float32)
    )
    layer_out = (result * live_flat).astype(jnp.bfloat16).reshape(nb_dev, rows_dev, width)
    upstream = cotangent.reshape(total_rows, width).astype(jnp.float32) * live_flat
    second_grad, grad_second_gain, grad_second_shift = norm_backward(
        upstream, normed_two, inverse_two, second_gain_f
    )
    outer_grad = second_grad.astype(jnp.bfloat16)
    grad_outer = contract_rows(activated, outer_grad)
    grad_outer_bias = jnp.sum(outer_grad.astype(jnp.float32), axis=0)
    inner_grad = gelu_back(contract_last(outer_grad, outer_weight))[0].astype(jnp.bfloat16)
    grad_inner = contract_rows(hidden_low, inner_grad)
    grad_inner_bias = jnp.sum(inner_grad.astype(jnp.float32), axis=0)
    hidden_grad = second_grad + contract_last(inner_grad, inner_weight)
    first_grad, grad_first_gain, grad_first_shift = norm_backward(
        hidden_grad, normed_one, inverse_one, first_gain_f
    )
    branch_grad = first_grad.astype(jnp.bfloat16)
    grad_output = contract_rows(attended_flat, branch_grad)
    attended_grad = (
        contract_last(branch_grad, output_weight)
        .astype(jnp.bfloat16)
        .reshape(nb_dev, rows_dev, width)
    )

    def attend_back(carry, operands):
        queries_blk, grads_blk, lse_blk, source = operands
        keys_flat, values_flat, keys_mine, values_mine = fetch(source)
        query_heads = split_heads(queries_blk)
        grad_heads = split_heads(grads_blk)
        key_heads = split_heads(keys_flat)
        value_heads = split_heads(values_flat)
        scores = (
            jnp.einsum(
                "nrhd,nkhd->nhrk", query_heads, key_heads, preferred_element_type=jnp.float32
            )
            * scale
        )
        soft = jnp.exp(scores - lse_blk[..., None])
        soft_grad = jnp.einsum(
            "nrhd,nkhd->nhrk", grad_heads, value_heads, preferred_element_type=jnp.float32
        )
        row_delta = jnp.sum(soft * soft_grad, axis=-1)
        score_grad = (soft * (soft_grad - row_delta[..., None])).astype(jnp.bfloat16)
        query_grad = (
            jnp.einsum("nhrk,nkhd->nrhd", score_grad, key_heads, preferred_element_type=jnp.float32)
            * scale
        )
        query_grad = query_grad.reshape(NBLK, rows_dev, width).astype(jnp.bfloat16)
        soft_low = soft.astype(jnp.bfloat16)
        key_part = (
            jnp.einsum(
                "nhrk,nrhd->nkhd", score_grad, query_heads, preferred_element_type=jnp.float32
            )
            * scale
        )
        value_part = jnp.einsum(
            "nhrk,nrhd->nkhd", soft_low, grad_heads, preferred_element_type=jnp.float32
        )
        key_sum, value_sum = (
            lax.psum_scatter(
                key_part.reshape(NBLK, -1, width), "ctx", scatter_dimension=1, tiled=True
            ),
            lax.psum_scatter(
                value_part.reshape(NBLK, -1, width), "ctx", scatter_dimension=1, tiled=True
            ),
        )
        key_grad = key_sum.astype(jnp.bfloat16)
        value_grad = value_sum.astype(jnp.bfloat16)
        return (carry, (query_grad, key_grad, value_grad))

    _, (query_grad_b, key_grad_b, value_grad_b) = lax.scan(
        attend_back,
        zero,
        (to_blocks(queries), to_blocks(attended_grad), lse_b, jax.tree.map(to_blocks, sources)),
    )
    query_grad = query_grad_b.reshape(total_rows, width)
    key_grad = key_grad_b.reshape(nb_dev * context_dev, width)
    value_grad = value_grad_b.reshape(nb_dev * context_dev, width)
    grad_query = contract_rows(tokens_flat, query_grad)
    grad_key = contract_rows(context_flat, key_grad)
    grad_value = contract_rows(context_flat, value_grad)
    token_grad = (first_grad + contract_last(query_grad, query_weight)).reshape(
        nb_dev, rows_dev, width
    )
    context_back = (
        contract_last(key_grad, key_weight) + contract_last(value_grad, value_weight)
    ).reshape(nb_dev, context_dev, width)
    grad_tokens = jnp.concatenate(
        [token_grad[:, :context_dev] + context_back, token_grad[:, context_dev:]], axis=1
    )
    finals = lax.psum(
        (
            grad_query,
            grad_key,
            grad_value,
            grad_output,
            grad_inner,
            grad_inner_bias,
            grad_outer,
            grad_outer_bias,
            grad_first_gain,
            grad_first_shift,
            grad_second_gain,
            grad_second_shift,
        ),
        ("grp", "ctx"),
    )
    return (layer_out, grad_tokens) + tuple(finals)


BF16, F32 = jnp.bfloat16, jnp.float32
MIB = 2**20
AXES = ("grp", "ctx")
LANES = 128


def one_chip_each(mesh):
    return mesh.shape["grp"] % 2 == 0 and mesh.shape["ctx"] == 2 * NBLK


def dot(left, right, over_left, over_right):
    return lax.dot_general(
        left, right, (((over_left,), (over_right,)), ((), ())), preferred_element_type=F32
    )


def kernel_call(body, grid, ins, outs, scratch, flops, moved, *operands, exps=0):
    return pl.pallas_call(
        body,
        grid=grid,
        in_specs=[pl.BlockSpec(shape, index) for shape, index in ins],
        out_specs=[pl.BlockSpec(shape, index) for shape, index, _, _ in outs],
        out_shape=[jax.ShapeDtypeStruct(shape, kind) for _, _, shape, kind in outs],
        scratch_shapes=scratch,
        cost_estimate=pl.CostEstimate(flops=flops, bytes_accessed=moved, transcendentals=exps),
        compiler_params=pltpu.CompilerParams(vmem_limit_bytes=60 * MIB),
    )(*operands)


def project_kernel(context, scale, own, other, wq, wk, wv, q_out, k_out, v_out):
    rows = own[0]
    queries = (dot(rows, wq[...], 1, 0) * scale).astype(BF16)
    for h in range(HEADS):
        q_out[h] = queries[:, h * HD : (h + 1) * HD]
    for side, keys_of in enumerate((rows[:context], other[0])):
        keys = dot(keys_of, wk[...], 1, 0).astype(BF16)
        values = dot(keys_of, wv[...], 1, 0).astype(BF16)
        for h in range(HEADS):
            k_out[h, side, 0] = keys[:, h * HD : (h + 1) * HD]
            v_out[h, side, 0] = values[:, h * HD : (h + 1) * HD]


def project(own, other, wq, wk, wv, scale):
    blocks, rows, width = own.shape
    context = other.shape[1]
    whole = (width, width)
    block = lambda b: (b, 0, 0)
    fixed = lambda b: (0, 0)
    key_spec = (
        (HEADS, 2, 1, context, HD),
        lambda b: (0, 0, b, 0, 0),
        (HEADS, 2, blocks, context, HD),
        BF16,
    )
    q, k, v = kernel_call(
        partial(project_kernel, context, scale),
        (blocks,),
        [((1, rows, width), block), ((1, context, width), block)] + [(whole, fixed)] * 3,
        [
            ((HEADS, rows, HD), lambda b: (0, b, 0), (HEADS, blocks * rows, HD), BF16),
            key_spec,
            key_spec,
        ],
        [],
        2 * blocks * width * width * (rows + 4 * context),
        4 * blocks * width * (rows + 3 * context),
        own,
        other,
        wq,
        wk,
        wv,
    )
    flat = (HEADS, 2 * blocks * context, HD)
    return q, k.reshape(flat), v.reshape(flat)


def forward_kernel(
    steps, row_blocks, chunk, q_ref, k_ref, v_ref, p_ref, o_ref, inv_ref, s_even, s_odd, top_even, top_odd, v_wide
):
    t = pl.program_id(0)
    rows, hd = q_ref.shape[-2:]
    keys = k_ref.shape[-2]

    @pl.when(t == 0)
    def _():
        v_wide[:, hd:] = jnp.ones((keys, hd), BF16)

    @pl.when((t > 0) & (lax.rem(t - 1, row_blocks) == 0))
    def _():
        v_wide[:, :hd] = v_ref[0]

    def body(score, weigh, s_now, s_before, top_now, top_before):
        if score:
            q = q_ref[0]
            high = None
        if weigh:
            peak = jnp.max(top_before[...], axis=-1, keepdims=True)
            total = jnp.zeros((rows, 2 * hd), F32)
        for c in range(keys // chunk):
            at = slice(c * chunk, (c + 1) * chunk)
            if score:
                scores = dot(q, k_ref[0, at, :], 1, 1)
                s_now[:, at] = scores
                for j in range(chunk // LANES):
                    part = scores[:, j * LANES : (j + 1) * LANES]
                    high = part if high is None else jnp.maximum(high, part)
            if weigh:
                soft = jnp.exp2(s_before[:, at] - peak).astype(BF16)
                p_ref[0, 0, :, at] = soft
                total = total + dot(soft, v_wide[at, :], 1, 0)
        if score:
            top_now[...] = high
        if weigh:
            inverse = 1.0 / total[:, hd:]
            o_ref[...] = total[:, :hd] * inverse
            inv_ref[0] = inverse

    even = (s_even, s_odd, top_even, top_odd)
    odd = (s_odd, s_even, top_odd, top_even)
    inside = (t > 0) & (t < steps)
    pl.when(inside & (lax.rem(t, 2) == 0))(lambda: body(True, True, *even))
    pl.when(inside & (lax.rem(t, 2) == 1))(lambda: body(True, True, *odd))
    pl.when(t == 0)(lambda: body(True, False, *even))
    pl.when(t == steps)(lambda: body(False, True, *(odd if steps % 2 else even)))


def attention_forward(q, k, v, row_blocks, chunk=512):
    heads, total, hd = q.shape
    keys = k.shape[1]
    rows = total // row_blocks
    steps = heads * row_blocks
    ahead = lambda t: jnp.minimum(t, steps - 1)
    behind = lambda t: jnp.maximum(t - 1, 0)
    return kernel_call(
        partial(forward_kernel, steps, row_blocks, chunk),
        (steps + 1,),
        [
            ((1, rows, hd), lambda t: (ahead(t) // row_blocks, ahead(t) % row_blocks, 0)),
            ((1, keys, hd), lambda t: (ahead(t) // row_blocks, 0, 0)),
            ((1, keys, hd), lambda t: (behind(t) // row_blocks, 0, 0)),
        ],
        [
            (
                (1, 1, rows, keys),
                lambda t: (behind(t) // row_blocks, behind(t) % row_blocks, 0, 0),
                (heads, row_blocks, rows, keys),
                BF16,
            ),
            (
                (rows, hd),
                lambda t: (behind(t) % row_blocks, behind(t) // row_blocks),
                (total, heads * hd),
                F32,
            ),
            (
                (1, rows, hd),
                lambda t: (behind(t) // row_blocks, behind(t) % row_blocks, 0),
                (heads, total, hd),
                F32,
            ),
        ],
        [
            pltpu.VMEM((rows, keys), F32),
            pltpu.VMEM((rows, keys), F32),
            pltpu.VMEM((rows, LANES), F32),
            pltpu.VMEM((rows, LANES), F32),
            pltpu.VMEM((keys, 2 * hd), BF16),
        ],
        8 * heads * total * keys * hd,
        2 * heads * total * keys,
        q,
        k,
        v,
        exps=heads * total * keys,
    )


def gelu_pair(inner):
    size = jnp.abs(inner) * (0.5**0.5)
    rate = 1.0 / (1.0 + 0.3275911 * size)
    bell = jnp.exp(-(size * size))
    tail = rate * (
        0.254829592
        + rate * (-0.284496736 + rate * (1.421413741 + rate * (-1.453152027 + rate * 1.061405429)))
    )
    tail = 0.5 * tail * bell
    below = jnp.where(inner < 0, tail, 1.0 - tail)
    return inner * below, below + inner * bell * 0.3989422804014327


def dense_kernel(
    x_ref, o_ref, inv_ref, cot_ref, wo, w1, b1, w2, b2, g1, s1, g2, s2,
    out_ref, first_ref, grad_ref, delta_ref, go_ref, gi_ref, gu_ref, vec_ref,
):
    @pl.when(pl.program_id(0) == 0)
    def _():
        for ref in (go_ref, gi_ref, gu_ref, vec_ref):
            ref[...] = jnp.zeros_like(ref)

    width = x_ref.shape[1]
    attended = o_ref[...]
    attended_low = attended.astype(BF16)
    gain_one, gain_two = g1[...].astype(F32), g2[...].astype(F32)
    first_sum = x_ref[...].astype(F32) + dot(attended_low, wo[...], 1, 0)
    hidden, normed_one, inverse_one = norm_forward(first_sum, gain_one, s1[...].astype(F32))
    hidden_low = hidden.astype(BF16)
    inner = dot(hidden_low, w1[...], 1, 0) + b1[...].astype(F32)
    activated, slope = gelu_pair(inner)
    activated = activated.astype(BF16)
    second_sum = hidden + dot(activated, w2[...], 1, 0) + b2[...].astype(F32)
    result, normed_two, inverse_two = norm_forward(second_sum, gain_two, s2[...].astype(F32))
    out_ref[...] = result.astype(BF16)
    upstream = cot_ref[...].astype(F32)
    second_grad, gain_two_sum, shift_two_sum = norm_backward(
        upstream, normed_two, inverse_two, gain_two
    )
    outer_grad = second_grad.astype(BF16)
    gu_ref[...] += dot(activated, outer_grad, 0, 0)
    inner_grad = (dot(outer_grad, w2[...], 1, 1) * slope).astype(BF16)
    gi_ref[...] += dot(hidden_low, inner_grad, 0, 0)
    hidden_grad = second_grad + dot(inner_grad, w1[...], 1, 1)
    first_grad, gain_one_sum, shift_one_sum = norm_backward(
        hidden_grad, normed_one, inverse_one, gain_one
    )
    first_ref[...] = first_grad
    branch_grad = first_grad.astype(BF16)
    go_ref[...] += dot(attended_low, branch_grad, 0, 0)
    attended_grad = dot(branch_grad, wo[...], 1, 1)
    for h in range(HEADS):
        at = slice(h * HD, (h + 1) * HD)
        scaled = (attended_grad[:, at] * inv_ref[h]).astype(BF16)
        grad_ref[h] = scaled
        delta = jnp.sum(scaled.astype(F32) * attended[:, at], axis=-1, keepdims=True)
        delta_ref[h] = jnp.broadcast_to(delta, delta_ref.shape[1:])
    inner_sum = jnp.sum(inner_grad.astype(F32), axis=0)
    sums = (
        gain_one_sum,
        shift_one_sum,
        gain_two_sum,
        shift_two_sum,
        jnp.sum(outer_grad.astype(F32), axis=0),
        inner_sum[:width],
        inner_sum[width:],
    )
    for j, part in enumerate(sums):
        vec_ref[j : j + 1, :] += part[None, :]


def dense(x, attended, inverse, cot, weights, row_blocks):
    total, width = x.shape
    rows = total // row_blocks
    hidden = weights[1].shape[1]
    block = lambda b: (b, 0)
    fixed = lambda b: (0, 0)
    by_head = lambda b: (0, b, 0)
    whole = lambda *shape: (shape, fixed, shape, F32)
    return kernel_call(
        dense_kernel,
        (row_blocks,),
        [
            ((rows, width), block),
            ((rows, width), block),
            ((HEADS, rows, HD), by_head),
            ((rows, width), block),
        ]
        + [(w.shape, fixed) for w in weights],
        [
            ((rows, width), block, (total, width), BF16),
            ((rows, width), block, (total, width), F32),
            ((HEADS, rows, HD), by_head, (HEADS, total, HD), BF16),
            ((HEADS, rows, HD), by_head, (HEADS, total, HD), F32),
            whole(width, width),
            whole(width, hidden),
            whole(hidden, width),
            whole(8, width),
        ],
        [],
        6 * total * width * (width + 2 * hidden),
        20 * total * width + 8 * width * (width + 2 * hidden),
        x,
        attended,
        inverse,
        cot,
        *weights,
    )


def backward_kernel(
    row_blocks, chunks, scale_q, scale_k,
    q_ref, g_ref, k_ref, v_ref, d_ref, p_ref, dq_ref, dk_ref, dv_ref, ds, dq_sum, q_t, g_t,
):
    c = pl.program_id(1)
    rows, chunk = p_ref.shape[2:]

    @pl.when(c == 0)
    def _():
        q_t[...] = q_ref[0].T
        g_t[...] = g_ref[0].T
        dq_sum[...] = jnp.zeros_like(dq_sum)

    keys, values = k_ref[0], v_ref[0]
    dv_t = jnp.zeros((HD, chunk), F32)
    for i in range(row_blocks):
        at = slice(i * rows, (i + 1) * rows)
        soft = p_ref[0, i]
        soft_grad = dot(g_ref[0, at, :], values, 1, 1)
        delta = jnp.concatenate([d_ref[0, at, :]] * (chunk // LANES), axis=1)
        score_grad = (soft.astype(F32) * (soft_grad - delta)).astype(BF16)
        ds[at, :] = score_grad
        dq_sum[at, :] += dot(score_grad, keys, 1, 0)
        dv_t += dot(g_t[:, at], soft, 1, 0)
    dv_ref[0] = dv_t.T.astype(BF16)
    dk_t = dot(q_t[...], ds[...], 1, 0)
    dk_ref[0] = (dk_t.T * scale_k).astype(BF16)

    @pl.when(c == chunks - 1)
    def _():
        dq_ref[0] = (dq_sum[...] * scale_q).astype(BF16)


def attention_backward(q, g, k, v, delta, p, scale_q, scale_k, chunk=1024):
    heads, total, hd = q.shape
    keys = k.shape[1]
    row_blocks, rows = p.shape[1:3]
    chunks = keys // chunk
    head = lambda h, c: (h, 0, 0)
    key = lambda h, c: (h, c, 0)
    key_out = ((1, chunk, hd), key, (heads, keys, hd), BF16)
    return kernel_call(
        partial(backward_kernel, row_blocks, chunks, scale_q, scale_k),
        (heads, chunks),
        [
            ((1, total, hd), head),
            ((1, total, hd), head),
            ((1, chunk, hd), key),
            ((1, chunk, hd), key),
            ((1, total, hd), head),
            ((1, row_blocks, rows, chunk), lambda h, c: (h, 0, 0, c)),
        ],
        [((1, total, hd), head, (heads, total, hd), BF16), key_out, key_out],
        [
            pltpu.VMEM((total, chunk), BF16),
            pltpu.VMEM((total, hd), F32),
            pltpu.VMEM((hd, total), BF16),
            pltpu.VMEM((hd, total), BF16),
        ],
        12 * heads * total * keys * hd,
        2 * heads * total * keys,
        q,
        g,
        k,
        v,
        delta,
        p,
    )


def finish_kernel(
    context, x_ref, first_ref, dq_ref, dk_own, dk_other, dv_own, dv_other, wq, wk, wv,
    token_ref, late_ref,
):
    width = x_ref.shape[2]

    @pl.when(pl.program_id(0) == 0)
    def _():
        late_ref[...] = jnp.zeros_like(late_ref)

    def joined(ref, other=None):
        parts = [ref[h, 0] if other is None else ref[h, 0, 0] for h in range(HEADS)]
        if other is not None:
            parts = [
                (part.astype(F32) + other[h, 0].astype(F32)).astype(BF16)
                for h, part in enumerate(parts)
            ]
        return jnp.concatenate(parts, axis=1)

    rows = x_ref[0]
    above = rows[:context]
    query_grad = joined(dq_ref)
    key_grad = joined(dk_own, dk_other)
    value_grad = joined(dv_own, dv_other)
    base = first_ref[0] + dot(query_grad, wq[...], 1, 1)
    back = dot(key_grad, wk[...], 1, 1) + dot(value_grad, wv[...], 1, 1)
    token_ref[0, :context] = (base[:context] + back).astype(BF16)
    token_ref[0, context:] = base[context:].astype(BF16)
    late_ref[:width] += dot(rows, query_grad, 0, 0)
    late_ref[width : 2 * width] += dot(above, key_grad, 0, 0)
    late_ref[2 * width :] += dot(above, value_grad, 0, 0)


def finish(x, first_grad, dq, dk, dk_other, dv, dv_other, wq, wk, wv):
    blocks, rows, width = x.shape
    context = dk.shape[1] // (2 * blocks)
    block = lambda b: (b, 0, 0)
    fixed = lambda b: (0, 0)
    sided = (HEADS, 2 * blocks, context, HD)
    own = ((HEADS, 1, 1, context, HD), lambda b: (0, 0, b, 0, 0))
    other = ((HEADS, 1, context, HD), lambda b: (0, b, 0, 0))
    both = lambda array: array.reshape(HEADS, 2, blocks, context, HD)
    return kernel_call(
        partial(finish_kernel, context),
        (blocks,),
        [
            ((1, rows, width), block),
            ((1, rows, width), block),
            ((HEADS, 1, rows, HD), lambda b: (0, b, 0, 0)),
            own,
            other,
            own,
            other,
        ]
        + [((width, width), fixed)] * 3,
        [
            ((1, rows, width), block, (blocks, rows, width), BF16),
            ((3 * width, width), fixed, (3 * width, width), F32),
        ],
        [],
        4 * blocks * width * width * (rows + 2 * context),
        8 * blocks * width * (rows + 2 * context),
        x,
        first_grad.reshape(blocks, rows, width),
        dq.reshape(HEADS, blocks, rows, HD),
        both(dk),
        dk_other,
        both(dv),
        dv_other,
        wq,
        wk,
        wv,
    )


def sum_over_all(part, groups, members, name):
    grp, ctx = lax.axis_index("grp"), lax.axis_index("ctx")

    def partner(flip_grp, flip_ctx):
        return [
            (g * members + c, (g ^ flip_grp) * members + (c ^ flip_ctx))
            for g in range(groups)
            for c in range(members)
        ]

    ways = [(1, 0)]
    ways += [(1 << b, 0) for b in range(1, groups.bit_length() - 1)]
    ways += [(0, 1 << b) for b in range(members.bit_length() - 1)]
    bits = [
        lax.rem((grp if flip_grp else ctx) // max(flip_grp, flip_ctx), 2)
        for flip_grp, flip_ctx in ways
    ]
    for way, bit in zip(ways, bits, strict=True):
        half = part.shape[0] // 2
        sent = lax.dynamic_slice_in_dim(part, (1 - bit) * half, half).astype(BF16)
        kept = lax.dynamic_slice_in_dim(part, bit * half, half)
        part = kept + lax.ppermute(sent, AXES, partner(*way)).astype(F32)
    part = part.astype(BF16)
    for way, bit in reversed(list(zip(ways, bits, strict=True))):
        came = lax.ppermute(part, AXES, partner(*way))
        part = jnp.where(
            bit == 0, jnp.concatenate([part, came]), jnp.concatenate([came, part])
        )
    return part.astype(F32)


def gathered_plan(
    tokens,
    query_counts,
    cotangent,
    query_weight,
    key_weight,
    value_weight,
    output_weight,
    inner_weight,
    inner_bias,
    outer_weight,
    outer_bias,
    first_gain,
    first_shift,
    second_gain,
    second_shift,
):
    blocks, rows, width = tokens.shape
    groups, members = lax.axis_size("grp"), lax.axis_size("ctx")
    member = lax.axis_index("ctx")
    place = member // 2
    context = CTX // members
    slots = QUERIES // members

    def route(r, back=False):
        pairs = []
        for g in range(groups):
            for c in range(members):
                to = (g - g % 2 + c % 2) * members + ((c // 2 + r) % blocks) * 2 + g % 2
                pairs.append((to, g * members + c) if back else (g * members + c, to))
        return pairs

    across = [
        (g * members + c, (g ^ 1) * members + c) for g in range(groups) for c in range(members)
    ]

    def outward(array):
        return [
            lax.ppermute(
                lax.dynamic_index_in_dim(array, lax.rem(place + r, blocks), 0, keepdims=False),
                AXES,
                route(r),
            )
            for r in range(blocks)
        ]

    def homeward(array):
        came = [lax.ppermute(array[r], AXES, route(r, True)) for r in range(blocks)]
        twice = jnp.stack(came + came)
        return lax.dynamic_slice_in_dim(twice, blocks - place, blocks)

    slot = member * slots + jnp.arange(rows, dtype=jnp.int32) - context
    live = (jnp.arange(rows) < context)[None, :] | (slot[None, :] < query_counts[:, None])
    live = live[:, :, None]

    own = outward(tokens)
    other = jnp.stack([lax.ppermute(block[:context], AXES, across) for block in own])
    own = jnp.stack(own)
    masked, own, other = lax.optimization_barrier(
        (jnp.where(live, cotangent, 0).astype(BF16), own, other)
    )
    cot = jnp.stack(outward(masked)).reshape(blocks * rows, width)

    scale = HD**-0.5
    log2e = 1.4426950408889634
    q, k, v = project(own, other, query_weight, key_weight, value_weight, scale * log2e)
    p, attended, inverse = attention_forward(q, k, v, blocks)
    lifted = lambda vector: vector.reshape(1, -1)
    weights = (
        output_weight,
        inner_weight,
        lifted(inner_bias),
        outer_weight,
        lifted(outer_bias),
        lifted(first_gain),
        lifted(first_shift),
        lifted(second_gain),
        lifted(second_shift),
    )
    out, first_grad, grads, delta, grad_output, grad_inner, grad_outer, vectors = dense(
        own.reshape(blocks * rows, width), attended, inverse, cot, weights, blocks
    )
    layer_out = homeward(out.reshape(blocks, rows, width))
    layer_out = jnp.where(live, layer_out, 0).astype(BF16)
    early = jnp.concatenate(
        [
            grad_output,
            grad_inner[:, :width],
            grad_inner[:, width:],
            grad_outer,
            vectors,
            jnp.zeros((504, width), F32),
        ]
    )
    early = sum_over_all(early, groups, members, "early")

    dq, dk, dv = attention_backward(q, grads, k, v, delta, p, scale, 1.0 / log2e)
    half = blocks * context
    dk_other = lax.ppermute(dk[:, half:], AXES, across).reshape(HEADS, blocks, context, HD)
    dv_other = lax.ppermute(dv[:, half:], AXES, across).reshape(HEADS, blocks, context, HD)
    token_grad, late = finish(
        own, first_grad, dq, dk, dk_other, dv, dv_other, query_weight, key_weight, value_weight
    )
    grad_tokens = homeward(token_grad).astype(F32)
    late = sum_over_all(late, groups, members, "late")

    vectors = early[5 * width :]
    return (
        layer_out,
        grad_tokens,
        late[:width],
        late[width : 2 * width],
        late[2 * width :],
        early[:width],
        jnp.concatenate([early[width : 2 * width], early[2 * width : 3 * width]], axis=1),
        jnp.concatenate([vectors[5], vectors[6]]),
        early[3 * width : 5 * width],
        vectors[4],
        vectors[0],
        vectors[1],
        vectors[2],
        vectors[3],
    )


def solution(mesh):
    return jax.shard_map(
        gathered_plan if one_chip_each(mesh) else spread_plan,
        mesh=mesh,
        in_specs=(
            P("grp", "ctx", None),
            P("grp"),
            P("grp", "ctx", None),
            P(),
            P(),
            P(),
            P(),
            P(),
            P(),
            P(),
            P(),
            P(),
            P(),
            P(),
            P(),
        ),
        out_specs=(
            P("grp", "ctx", None),
            P("grp", "ctx", None),
            P(),
            P(),
            P(),
            P(),
            P(),
            P(),
            P(),
            P(),
            P(),
            P(),
            P(),
            P(),
        ),
        check_vma=False,
    )
```

```python
from functools import partial

import jax
import jax.numpy as jnp
from jax import lax
from jax.experimental import pallas as pl
from jax.experimental.pallas import tpu as pltpu
from jax.sharding import PartitionSpec as P

HEADS = 4
CTX = 4096
QUERIES = 128
NBLK = 4
HD = 128


EPSILON = 1e-05


def product(left, right):
    return jnp.dot(left, right, preferred_element_type=jnp.float32)


def contract_rows(left, right):
    return lax.dot_general(
        left, right, (((0,), (0,)), ((), ())), preferred_element_type=jnp.float32
    )


def contract_last(left, right):
    return lax.dot_general(
        left, right, (((1,), (1,)), ((), ())), preferred_element_type=jnp.float32
    )


def norm_forward(values, gain, shift):
    center = values - jnp.mean(values, axis=-1, keepdims=True)
    inverse = lax.rsqrt(jnp.mean(center * center, axis=-1, keepdims=True) + EPSILON)
    normed = center * inverse
    return (normed * gain + shift, normed, inverse)


def norm_backward(upstream, normed, inverse, gain):
    scaled = upstream * gain
    plain_mean = jnp.mean(scaled, axis=-1, keepdims=True)
    cross_mean = jnp.mean(scaled * normed, axis=-1, keepdims=True)
    value_grad = inverse * (scaled - plain_mean - normed * cross_mean)
    return (value_grad, jnp.sum(upstream * normed, axis=0), jnp.sum(upstream, axis=0))


def spread_plan(
    tokens,
    query_counts,
    cotangent,
    query_weight,
    key_weight,
    value_weight,
    output_weight,
    inner_weight,
    inner_bias,
    outer_weight,
    outer_bias,
    first_gain,
    first_shift,
    second_gain,
    second_shift,
):
    member = lax.axis_index("ctx")
    ctx_count = lax.axis_size("ctx")
    context_dev = CTX // ctx_count
    query_dev = QUERIES // ctx_count
    nb_dev = tokens.shape[0]
    rows_dev = tokens.shape[1]
    width = tokens.shape[2]
    heads_count = HEADS
    head_width = HD
    block_count = nb_dev // NBLK
    scale = head_width ** (-0.5)
    total_rows = nb_dev * rows_dev
    tokens_flat = tokens.reshape(total_rows, width)
    context_rows = tokens[:, :context_dev]
    context_flat = context_rows.reshape(nb_dev * context_dev, width)
    queries = (
        product(tokens_flat, query_weight).astype(jnp.bfloat16).reshape(nb_dev, rows_dev, width)
    )
    keys_own = (
        product(context_flat, key_weight).astype(jnp.bfloat16).reshape(nb_dev, context_dev, width)
    )
    values_own = (
        product(context_flat, value_weight).astype(jnp.bfloat16).reshape(nb_dev, context_dev, width)
    )
    sources = (keys_own, values_own)

    def to_blocks(array):
        return array.reshape((block_count, NBLK) + array.shape[1:])

    def fetch(source):
        keys_mine, values_mine = source
        keys_flat, values_flat = (
            lax.all_gather(keys_mine, "ctx", axis=1, tiled=True),
            lax.all_gather(values_mine, "ctx", axis=1, tiled=True),
        )
        return (keys_flat, values_flat, keys_mine, values_mine)

    def split_heads(array):
        return array.reshape(array.shape[0], array.shape[1], heads_count, head_width)

    def attend(carry, operands):
        queries_blk, source = operands
        keys_flat, values_flat, keys_mine, values_mine = fetch(source)
        query_heads = split_heads(queries_blk)
        scores = (
            jnp.einsum(
                "nrhd,nkhd->nhrk",
                query_heads,
                split_heads(keys_flat),
                preferred_element_type=jnp.float32,
            )
            * scale
        )
        log_total = jax.nn.logsumexp(scores, axis=-1, keepdims=True)
        soft_low = jnp.exp(scores - log_total).astype(jnp.bfloat16)
        mixed = jnp.einsum(
            "nhrk,nkhd->nrhd",
            soft_low,
            split_heads(values_flat),
            preferred_element_type=jnp.float32,
        )
        attended_blk = mixed.reshape(NBLK, rows_dev, width).astype(jnp.bfloat16)
        return (carry, (attended_blk, log_total[..., 0]))

    zero = jnp.zeros((), jnp.float32)
    _, (attended_b, lse_b) = lax.scan(
        attend, zero, (to_blocks(queries), jax.tree.map(to_blocks, sources))
    )
    attended_flat = attended_b.reshape(total_rows, width)
    slot_local = jnp.arange(rows_dev, dtype=jnp.int32) - context_dev
    slot_global = member * query_dev + slot_local
    live_rows = jnp.logical_or(
        slot_local[None, :] < 0, slot_global[None, :] < query_counts[:, None]
    )
    live_flat = live_rows.astype(jnp.float32).reshape(total_rows, 1)
    inner_bias_f = inner_bias.astype(jnp.float32)
    outer_bias_f = outer_bias.astype(jnp.float32)
    first_gain_f = first_gain.astype(jnp.float32)
    second_gain_f = second_gain.astype(jnp.float32)
    first_sum = tokens_flat.astype(jnp.float32) + product(attended_flat, output_weight)
    hidden, normed_one, inverse_one = norm_forward(
        first_sum, first_gain_f, first_shift.astype(jnp.float32)
    )
    hidden_low = hidden.astype(jnp.bfloat16)
    inner = product(hidden_low, inner_weight) + inner_bias_f
    gelu_value, gelu_back = jax.vjp(partial(jax.nn.gelu, approximate=False), inner)
    activated = gelu_value.astype(jnp.bfloat16)
    second_sum = hidden + product(activated, outer_weight) + outer_bias_f
    result, normed_two, inverse_two = norm_forward(
        second_sum, second_gain_f, second_shift.astype(jnp.float32)
    )
    layer_out = (result * live_flat).astype(jnp.bfloat16).reshape(nb_dev, rows_dev, width)
    upstream = cotangent.reshape(total_rows, width).astype(jnp.float32) * live_flat
    second_grad, grad_second_gain, grad_second_shift = norm_backward(
        upstream, normed_two, inverse_two, second_gain_f
    )
    outer_grad = second_grad.astype(jnp.bfloat16)
    grad_outer = contract_rows(activated, outer_grad)
    grad_outer_bias = jnp.sum(outer_grad.astype(jnp.float32), axis=0)
    inner_grad = gelu_back(contract_last(outer_grad, outer_weight))[0].astype(jnp.bfloat16)
    grad_inner = contract_rows(hidden_low, inner_grad)
    grad_inner_bias = jnp.sum(inner_grad.astype(jnp.float32), axis=0)
    hidden_grad = second_grad + contract_last(inner_grad, inner_weight)
    first_grad, grad_first_gain, grad_first_shift = norm_backward(
        hidden_grad, normed_one, inverse_one, first_gain_f
    )
    branch_grad = first_grad.astype(jnp.bfloat16)
    grad_output = contract_rows(attended_flat, branch_grad)
    attended_grad = (
        contract_last(branch_grad, output_weight)
        .astype(jnp.bfloat16)
        .reshape(nb_dev, rows_dev, width)
    )

    def attend_back(carry, operands):
        queries_blk, grads_blk, lse_blk, source = operands
        keys_flat, values_flat, keys_mine, values_mine = fetch(source)
        query_heads = split_heads(queries_blk)
        grad_heads = split_heads(grads_blk)
        key_heads = split_heads(keys_flat)
        value_heads = split_heads(values_flat)
        scores = (
            jnp.einsum(
                "nrhd,nkhd->nhrk", query_heads, key_heads, preferred_element_type=jnp.float32
            )
            * scale
        )
        soft = jnp.exp(scores - lse_blk[..., None])
        soft_grad = jnp.einsum(
            "nrhd,nkhd->nhrk", grad_heads, value_heads, preferred_element_type=jnp.float32
        )
        row_delta = jnp.sum(soft * soft_grad, axis=-1)
        score_grad = (soft * (soft_grad - row_delta[..., None])).astype(jnp.bfloat16)
        query_grad = (
            jnp.einsum("nhrk,nkhd->nrhd", score_grad, key_heads, preferred_element_type=jnp.float32)
            * scale
        )
        query_grad = query_grad.reshape(NBLK, rows_dev, width).astype(jnp.bfloat16)
        soft_low = soft.astype(jnp.bfloat16)
        key_part = (
            jnp.einsum(
                "nhrk,nrhd->nkhd", score_grad, query_heads, preferred_element_type=jnp.float32
            )
            * scale
        )
        value_part = jnp.einsum(
            "nhrk,nrhd->nkhd", soft_low, grad_heads, preferred_element_type=jnp.float32
        )
        key_sum, value_sum = (
            lax.psum_scatter(
                key_part.reshape(NBLK, -1, width), "ctx", scatter_dimension=1, tiled=True
            ),
            lax.psum_scatter(
                value_part.reshape(NBLK, -1, width), "ctx", scatter_dimension=1, tiled=True
            ),
        )
        key_grad = key_sum.astype(jnp.bfloat16)
        value_grad = value_sum.astype(jnp.bfloat16)
        return (carry, (query_grad, key_grad, value_grad))

    _, (query_grad_b, key_grad_b, value_grad_b) = lax.scan(
        attend_back,
        zero,
        (to_blocks(queries), to_blocks(attended_grad), lse_b, jax.tree.map(to_blocks, sources)),
    )
    query_grad = query_grad_b.reshape(total_rows, width)
    key_grad = key_grad_b.reshape(nb_dev * context_dev, width)
    value_grad = value_grad_b.reshape(nb_dev * context_dev, width)
    grad_query = contract_rows(tokens_flat, query_grad)
    grad_key = contract_rows(context_flat, key_grad)
    grad_value = contract_rows(context_flat, value_grad)
    token_grad = (first_grad + contract_last(query_grad, query_weight)).reshape(
        nb_dev, rows_dev, width
    )
    context_back = (
        contract_last(key_grad, key_weight) + contract_last(value_grad, value_weight)
    ).reshape(nb_dev, context_dev, width)
    grad_tokens = jnp.concatenate(
        [token_grad[:, :context_dev] + context_back, token_grad[:, context_dev:]], axis=1
    )
    finals = lax.psum(
        (
            grad_query,
            grad_key,
            grad_value,
            grad_output,
            grad_inner,
            grad_inner_bias,
            grad_outer,
            grad_outer_bias,
            grad_first_gain,
            grad_first_shift,
            grad_second_gain,
            grad_second_shift,
        ),
        ("grp", "ctx"),
    )
    return (layer_out, grad_tokens) + tuple(finals)


BF16, F32 = jnp.bfloat16, jnp.float32
MIB = 2**20
AXES = ("grp", "ctx")
LANES = 128
ROWS_STEP = 528


def one_chip_each(mesh):
    return mesh.shape["grp"] % 2 == 0 and mesh.shape["ctx"] == 2 * NBLK


def dot(left, right, over_left, over_right):
    return lax.dot_general(
        left, right, (((over_left,), (over_right,)), ((), ())), preferred_element_type=F32
    )


def kernel_call(body, grid, ins, outs, scratch, flops, moved, *operands, exps=0, into=()):
    given = len(ins)

    def run(*refs):
        body(*refs[:given], *refs[given + len(into) :])

    return pl.pallas_call(
        run,
        grid=grid,
        in_specs=[
            pl.BlockSpec(memory_space=index) if shape is None else pl.BlockSpec(shape, index)
            for shape, index in ins
        ]
        + [pl.BlockSpec(memory_space=pl.ANY)] * len(into),
        out_specs=[
            pl.BlockSpec(memory_space=index) if shape is None else pl.BlockSpec(shape, index)
            for shape, index, _, _ in outs
        ],
        out_shape=[jax.ShapeDtypeStruct(shape, kind) for _, _, shape, kind in outs],
        scratch_shapes=scratch,
        input_output_aliases={given + j: j for j in range(len(into))},
        cost_estimate=pl.CostEstimate(flops=flops, bytes_accessed=moved, transcendentals=exps),
        compiler_params=pltpu.CompilerParams(vmem_limit_bytes=60 * MIB),
    )(*operands, *into)


def project_kernel(context, scale, own, other, wq, wk, wv, q_out, k_out, v_out, x_out):
    rows = own[...]
    x_out[0] = rows
    queries = (dot(rows, wq[...], 1, 0) * scale).astype(BF16)
    for h in range(HEADS):
        q_out[h] = queries[:, h * HD : (h + 1) * HD]
    for side, keys_of in enumerate((rows[:context], other[:context])):
        keys = dot(keys_of, wk[...], 1, 0).astype(BF16)
        values = dot(keys_of, wv[...], 1, 0).astype(BF16)
        for h in range(HEADS):
            k_out[h, side, 0] = keys[:, h * HD : (h + 1) * HD]
            v_out[h, side, 0] = values[:, h * HD : (h + 1) * HD]


def project(own, other, place, blocks, context, kinds, scale, into):
    rows, width = own.shape
    fixed = lambda b: (0, 0)
    key_spec = (
        (HEADS, 2, 1, context, HD),
        lambda b: (0, 0, place, 0, 0),
        (HEADS, 2, blocks, context, HD),
        BF16,
    )
    return kernel_call(
        partial(project_kernel, context, scale),
        (1,),
        [((rows, width), fixed)] * 2 + [((width, width), fixed)] * 3,
        [
            ((HEADS, rows, HD), lambda b: (0, place, 0), (HEADS, blocks * rows, HD), BF16),
            key_spec,
            key_spec,
            ((1, rows, width), lambda b: (place, 0, 0), (blocks, rows, width), BF16),
        ],
        [],
        2 * width * width * (rows + 4 * context),
        4 * width * (rows + 3 * context),
        own,
        other,
        *kinds,
        into=into,
    )


def forward_kernel(sets, steps, row_blocks, chunk, q_ref, *refs):
    k_refs, v_refs, refs = refs[:sets], refs[sets : 2 * sets], refs[2 * sets :]
    p_ref, o_ref, sum_ref, s_even, s_odd, top_even, top_odd, v_wide = refs
    t = pl.program_id(0)
    rows, hd = q_ref.shape[-2:]
    keys = p_ref.shape[-1]

    @pl.when(t == 0)
    def _():
        v_wide[:, hd:] = jnp.ones((keys, hd), BF16)

    @pl.when((t > 0) & (lax.rem(t - 1, row_blocks) == 0))
    def _():
        start = 0
        for v_ref in v_refs:
            v_wide[start : start + v_ref.shape[1], :hd] = v_ref[0]
            start += v_ref.shape[1]

    places = []
    for k_ref in k_refs:
        places += [(k_ref, slice(c, c + chunk)) for c in range(0, k_ref.shape[1], chunk)]

    def body(score, weigh, s_now, s_before, top_now, top_before):
        if score:
            q = q_ref[0]
            high = None
        if weigh:
            peak = jnp.max(top_before[...], axis=-1, keepdims=True)
            total = jnp.zeros((rows, 2 * hd), F32)
        for c, (k_ref, within) in enumerate(places):
            at = slice(c * chunk, (c + 1) * chunk)
            if score:
                scores = dot(q, k_ref[0, within, :], 1, 1)
                s_now[:, at] = scores
                for j in range(chunk // LANES):
                    part = scores[:, j * LANES : (j + 1) * LANES]
                    high = part if high is None else jnp.maximum(high, part)
            if weigh:
                soft = jnp.exp2(s_before[:, at] - peak).astype(BF16)
                p_ref[0, :, at] = soft
                total = total + dot(soft, v_wide[at, :], 1, 0)
        if score:
            top_now[...] = high
        if weigh:
            o_ref[...] = total[:, :hd]
            sum_ref[0] = total[:, hd:]

    even = (s_even, s_odd, top_even, top_odd)
    odd = (s_odd, s_even, top_odd, top_even)
    inside = (t > 0) & (t < steps)
    pl.when(inside & (lax.rem(t, 2) == 0))(lambda: body(True, True, *even))
    pl.when(inside & (lax.rem(t, 2) == 1))(lambda: body(True, True, *odd))
    pl.when(t == 0)(lambda: body(True, False, *even))
    pl.when(t == steps)(lambda: body(False, True, *(odd if steps % 2 else even)))


def attention_forward(q, ks, vs, row_blocks, chunk=512):
    heads, total, hd = q.shape
    keys = sum(k.shape[1] for k in ks)
    rows = total // row_blocks
    steps = heads * row_blocks
    ahead = lambda t: jnp.minimum(t, steps - 1)
    behind = lambda t: jnp.maximum(t - 1, 0)
    by_row = lambda t: (behind(t) // row_blocks, behind(t) % row_blocks, 0)
    per_row = ((1, rows, hd), by_row, (heads, total, hd), F32)
    return kernel_call(
        partial(forward_kernel, len(ks), steps, row_blocks, chunk),
        (steps + 1,),
        [((1, rows, hd), lambda t: (ahead(t) // row_blocks, ahead(t) % row_blocks, 0))]
        + [((1, k.shape[1], hd), lambda t: (ahead(t) // row_blocks, 0, 0)) for k in ks]
        + [((1, v.shape[1], hd), lambda t: (behind(t) // row_blocks, 0, 0)) for v in vs],
        [
            ((1, rows, keys), by_row, (heads, total, keys), BF16),
            (
                (rows, hd),
                lambda t: (behind(t) % row_blocks, behind(t) // row_blocks),
                (total, heads * hd),
                F32,
            ),
            per_row,
        ],
        [
            pltpu.VMEM((rows, keys), F32),
            pltpu.VMEM((rows, keys), F32),
            pltpu.VMEM((rows, LANES), F32),
            pltpu.VMEM((rows, LANES), F32),
            pltpu.VMEM((keys, 2 * hd), BF16),
        ],
        8 * heads * total * keys * hd,
        2 * heads * total * keys,
        q,
        *ks,
        *vs,
        exps=heads * total * keys,
    )


def gelu_pair(inner):
    size = jnp.abs(inner) * (0.5**0.5)
    rate = 1.0 / (1.0 + 0.3275911 * size)
    bell = jnp.exp(-(size * size))
    tail = rate * (
        0.254829592
        + rate * (-0.284496736 + rate * (1.421413741 + rate * (-1.453152027 + rate * 1.061405429)))
    )
    tail = 0.5 * tail * bell
    below = jnp.where(inner < 0, tail, 1.0 - tail)
    return inner * below, below + inner * bell * 0.3989422804014327


def dense_kernel(
    blocks, steps, bit_ref, x_ref, o_ref, total_ref, wo, w1, b1, w2, b2, g1, s1, g2, s2, *refs
):
    cot_refs, refs = refs[:blocks], refs[blocks:]
    out_refs, refs = refs[:blocks], refs[blocks:]
    first_ref, grad_ref, delta_ref, keep_ref, send_ref = refs[:5]
    sums, sending, cot, out, arrived, left = refs[5:]
    t = pl.program_id(0)
    width, hidden_width = w1.shape
    rows, half = x_ref.shape[0], sending.shape[0]
    block = cot.shape[0] // blocks
    load = [
        pltpu.make_async_copy(ref, cot.at[pl.ds(j * block, block)], arrived.at[j])
        for j, ref in enumerate(cot_refs)
    ]
    store = [
        pltpu.make_async_copy(out.at[pl.ds(j * block, block)], ref, left.at[j])
        for j, ref in enumerate(out_refs)
    ]

    @pl.when(t == 0)
    def _():
        for copy in load:
            copy.start()
        sums[...] = jnp.zeros_like(sums)

    for j, copy in enumerate(load):
        pl.when(t == j * block // rows)(copy.wait)
    here = pl.ds(pl.multiple_of(t * rows, 16), rows)
    gain_one, gain_two = g1[...].astype(F32), g2[...].astype(F32)
    inverses = [1.0 / total_ref[h] for h in range(HEADS)]
    attended = jnp.concatenate(
        [o_ref[:, h * HD : (h + 1) * HD] * inverses[h] for h in range(HEADS)], axis=1
    )
    attended_low = attended.astype(BF16)
    first_sum = x_ref[...].astype(F32) + dot(attended_low, wo[...], 1, 0)
    hidden, normed_one, inverse_one = norm_forward(first_sum, gain_one, s1[...].astype(F32))
    hidden_low = hidden.astype(BF16)
    inner = dot(hidden_low, w1[...], 1, 0) + b1[...].astype(F32)
    activated, slope = gelu_pair(inner)
    activated = activated.astype(BF16)
    second_sum = hidden + dot(activated, w2[...], 1, 0) + b2[...].astype(F32)
    result, normed_two, inverse_two = norm_forward(second_sum, gain_two, s2[...].astype(F32))
    out[here, :] = result.astype(BF16)
    upstream = cot[here, :].astype(F32)
    second_grad, gain_two_sum, shift_two_sum = norm_backward(
        upstream, normed_two, inverse_two, gain_two
    )
    outer_grad = second_grad.astype(BF16)
    at = width + hidden_width
    sums[at : at + hidden_width] += dot(activated, outer_grad, 0, 0)
    inner_grad = (dot(outer_grad, w2[...], 1, 1) * slope).astype(BF16)
    inner_sums = dot(hidden_low, inner_grad, 0, 0)
    for j in range(0, hidden_width, width):
        sums[width + j : 2 * width + j] += inner_sums[:, j : j + width]
    hidden_grad = second_grad + dot(inner_grad, w1[...], 1, 1)
    first_grad, gain_one_sum, shift_one_sum = norm_backward(
        hidden_grad, normed_one, inverse_one, gain_one
    )
    branch_grad = first_grad.astype(BF16)
    first_ref[...] = branch_grad
    sums[:width] += dot(attended_low, branch_grad, 0, 0)
    attended_grad = dot(branch_grad, wo[...], 1, 1)
    for h in range(HEADS):
        at = slice(h * HD, (h + 1) * HD)
        scaled = (attended_grad[:, at] * inverses[h]).astype(BF16)
        grad_ref[h] = scaled
        delta = jnp.sum(scaled.astype(F32) * attended[:, at], axis=-1, keepdims=True)
        delta_ref[h] = jnp.broadcast_to(delta, delta_ref.shape[1:])
    inner_sum = jnp.sum(inner_grad.astype(F32), axis=0)
    vectors = [
        gain_one_sum,
        shift_one_sum,
        gain_two_sum,
        shift_two_sum,
        jnp.sum(outer_grad.astype(F32), axis=0),
    ]
    vectors += [inner_sum[j : j + width] for j in range(0, hidden_width, width)]
    at = width + 2 * hidden_width
    for j, part in enumerate(vectors):
        sums[at + j : at + j + 1, :] += part[None, :]

    @pl.when(t == steps - 1)
    def _():
        bit = bit_ref[0]
        keep = pltpu.make_async_copy(
            sums.at[pl.ds(pl.multiple_of(bit * half, 16), half)], keep_ref, arrived.at[0]
        )
        sending[...] = sums[pl.ds(pl.multiple_of((1 - bit) * half, 16), half)].astype(BF16)
        send = pltpu.make_async_copy(sending, send_ref, arrived.at[1])
        copies = [*store, keep, send]
        for copy in copies:
            copy.start()
        for copy in copies:
            copy.wait()


def dense(bit, x, cots, attended, total_of, weights, steps=3):
    blocks, block, width = x.shape
    total = blocks * block
    rows = total // steps
    hidden = weights[1].shape[1]
    by_row = ((rows, width), lambda t: (t, 0))
    by_head = ((HEADS, rows, HD), lambda t: (0, t, 0))
    count = -(-(width + 2 * hidden + 8) // 256) * 256
    *out, first_grad, grads, delta, keep, send = kernel_call(
        partial(dense_kernel, blocks, steps),
        (steps,),
        [(None, pltpu.SMEM), by_row, by_row, by_head]
        + [(w.shape, lambda t: (0, 0)) for w in weights]
        + [(None, pl.ANY)] * blocks,
        [(None, pl.ANY, (block, width), BF16)] * blocks
        + [
            (*by_row, (total, width), BF16),
            (*by_head, (HEADS, total, HD), BF16),
            (*by_head, (HEADS, total, HD), F32),
            (None, pl.ANY, (count // 2, width), F32),
            (None, pl.ANY, (count // 2, width), BF16),
        ],
        [
            pltpu.VMEM((count, width), F32),
            pltpu.VMEM((count // 2, width), BF16),
            pltpu.VMEM((total, width), BF16),
            pltpu.VMEM((total, width), BF16),
            pltpu.SemaphoreType.DMA((blocks,)),
            pltpu.SemaphoreType.DMA((blocks,)),
        ],
        6 * total * width * (width + 2 * hidden),
        32 * total * width + 8 * width * (width + 2 * hidden),
        bit,
        x.reshape(total, width),
        attended,
        total_of,
        *weights,
        *cots,
    )
    return out, first_grad, grads, delta, keep, send


def backward_kernel(scale_k, scale_q, carried, q_ref, g_ref, d_ref, p_ref, k_ref, v_ref, *refs):
    if carried:
        before, refs = refs[0], refs[1:]
    kv_ref, dq_ref, dq_sum, ds, q_t, g_t = refs
    c = pl.program_id(1)

    @pl.when(c == 0)
    def _():
        q_t[...] = q_ref[0].T
        g_t[...] = g_ref[0].T
        dq_sum[...] = before[0] if carried else jnp.zeros_like(dq_sum)

    keys, values = k_ref[0], v_ref[0]
    chunk = keys.shape[0]
    for start in range(0, p_ref.shape[1], ROWS_STEP):
        at = slice(start, start + ROWS_STEP)
        soft_grad = dot(g_ref[0, at, :], values, 1, 1)
        delta = jnp.concatenate([d_ref[0, at, :]] * (chunk // LANES), axis=1)
        score_grad = (p_ref[0, at, :].astype(F32) * (soft_grad - delta)).astype(BF16)
        ds[at, :] = score_grad
        dq_sum[at, :] += dot(score_grad, keys, 1, 0)
    dv = dot(g_t[...], p_ref[0], 1, 0).T
    dk = dot(q_t[...], ds[...], 1, 0).T * scale_k
    kv_ref[0, 0] = dk.astype(BF16)
    kv_ref[1, 0] = dv.astype(BF16)

    @pl.when(c == pl.num_programs(1) - 1)
    def _():
        dq_ref[0] = (dq_sum[...] * scale_q).astype(dq_ref.dtype)


def attention_backward(q, g, d, p, k, v, scale_k, scale_q, chunk, first, chunks, before=None):
    heads, total, hd = q.shape
    row = lambda h, c: (h, 0, 0)
    key = lambda h, c: (h, c + first, 0)
    by_row = ((1, total, hd), row)
    carried = before is not None
    return kernel_call(
        partial(backward_kernel, scale_k, scale_q, carried),
        (heads, chunks),
        [
            by_row,
            by_row,
            by_row,
            ((1, total, chunk), lambda h, c: (h, 0, c + first)),
            ((1, chunk, hd), key),
            ((1, chunk, hd), key),
        ]
        + [by_row] * carried,
        [
            ((2, 1, chunk, hd), lambda h, c: (0, h, c, 0), (2, heads, chunks * chunk, hd), BF16),
            (*by_row, (heads, total, hd), BF16 if carried else F32),
        ],
        [
            pltpu.VMEM((total, hd), F32),
            pltpu.VMEM((total, chunk), BF16),
            pltpu.VMEM((hd, total), BF16),
            pltpu.VMEM((hd, total), BF16),
        ],
        12 * heads * total * chunk * chunks * hd,
        2 * heads * total * chunk * chunks,
        q,
        g,
        d,
        p,
        k,
        v,
        *[before] * carried,
    )


def finish_kernel(context, blocks, first_ref, query_ref, own, other, wq, wk, wv, *refs):
    token_refs, (key_ref, value_ref, tokens, left) = refs[:blocks], refs[blocks:]
    b = pl.program_id(0)

    def joined(one):
        return jnp.concatenate([one(h).astype(BF16) for h in range(HEADS)], axis=1)

    query_grad = joined(lambda h: query_ref[h, 0])
    key_grad, value_grad = (
        joined(lambda h, j=j: own[j, h, 0].astype(F32) + other[j, h, 0].astype(F32))
        for j in range(2)
    )
    key_ref[0] = key_grad
    value_ref[0] = value_grad
    base = first_ref[0].astype(F32) + dot(query_grad, wq[...], 1, 1)
    back = dot(key_grad, wk[...], 1, 1) + dot(value_grad, wv[...], 1, 1)
    tokens[b, :context] = (base[:context] + back).astype(BF16)
    tokens[b, context:] = base[context:].astype(BF16)
    store = [
        pltpu.make_async_copy(tokens.at[j], ref, left.at[j]) for j, ref in enumerate(token_refs)
    ]
    for j, copy in enumerate(store):
        pl.when(b == j)(copy.start)

    @pl.when(b == blocks - 1)
    def _():
        for copy in store:
            copy.wait()


def finish(first_grad, own, other, query_grad, kinds, blocks):
    total, width = first_grad.shape
    rows = total // blocks
    context = own.shape[2] // blocks
    block = lambda b: (b, 0, 0)
    side = ((2, HEADS, 1, context, HD), lambda b: (0, 0, b, 0, 0))
    by_rows = lambda count: ((1, count, width), block, (blocks, count, width), BF16)
    return kernel_call(
        partial(finish_kernel, context, blocks),
        (blocks,),
        [
            ((1, rows, width), block),
            ((HEADS, 1, rows, HD), lambda b: (0, b, 0, 0)),
            side,
            side,
        ]
        + [((width, width), lambda b: (0, 0))] * 3,
        [(None, pl.ANY, (rows, width), BF16)] * blocks + [by_rows(context), by_rows(context)],
        [pltpu.VMEM((blocks, rows, width), BF16), pltpu.SemaphoreType.DMA((blocks,))],
        2 * blocks * width * width * (rows + 2 * context),
        6 * blocks * width * (rows + 2 * context),
        first_grad.reshape(blocks, rows, width),
        query_grad.reshape(HEADS, blocks, rows, HD),
        own.reshape(2, HEADS, blocks, context, HD),
        other.reshape(2, HEADS, blocks, context, HD),
        *kinds,
    )


def weigh_kernel(bit_ref, x_ref, query_ref, key_ref, value_ref, keep_ref, send_ref, sums, sending, left):
    s = pl.program_id(0)
    blocks, rows, width = x_ref.shape
    context = key_ref.shape[1]
    per = query_ref.shape[0]
    columns = per * HD
    x = x_ref[...].reshape(blocks * rows, width)
    above = x_ref[:, :context].reshape(blocks * context, width)
    query_grad = jnp.concatenate([query_ref[h] for h in range(per)], axis=1)
    three = [dot(x, query_grad, 0, 0)]
    for ref in (key_ref, value_ref):
        three.append(dot(above, ref[...].reshape(blocks * context, columns), 0, 0))
    steps = width // columns
    for j in range(steps):

        @pl.when(s == j)
        def _(j=j):
            for i, part in enumerate(three):
                sums[i * width : (i + 1) * width, j * columns : (j + 1) * columns] = part

    @pl.when(s == steps - 1)
    def _():
        bit = bit_ref[0]
        half = sending.shape[0]
        keep = pltpu.make_async_copy(
            sums.at[pl.ds(pl.multiple_of(bit * half, 16), half)], keep_ref, left.at[0]
        )
        keep.start()
        sending[...] = sums[pl.ds(pl.multiple_of((1 - bit) * half, 16), half)].astype(BF16)
        send = pltpu.make_async_copy(sending, send_ref, left.at[1])
        send.start()
        keep.wait()
        send.wait()


def weigh(bit, x, query_grad, key_grad, value_grad, per=2):
    blocks, rows, width = x.shape
    context = key_grad.shape[1]
    by_columns = ((blocks, context, per * HD), lambda s: (0, 0, s))
    half = 3 * width // 2
    return kernel_call(
        weigh_kernel,
        (HEADS // per,),
        [
            (None, pltpu.SMEM),
            (x.shape, lambda s: (0, 0, 0)),
            ((per, blocks * rows, HD), lambda s: (s, 0, 0)),
            by_columns,
            by_columns,
        ],
        [(None, pl.ANY, (half, width), F32), (None, pl.ANY, (half, width), BF16)],
        [
            pltpu.VMEM((3 * width, width), F32),
            pltpu.VMEM((half, width), BF16),
            pltpu.SemaphoreType.DMA((2,)),
        ],
        2 * blocks * width * width * (rows + 2 * context),
        4 * blocks * width * (rows + context),
        bit,
        x,
        query_grad,
        key_grad,
        value_grad,
    )


def summing(groups, members):
    grp, ctx = lax.axis_index("grp"), lax.axis_index("ctx")
    planes, along = groups // 2, members // 2
    places = [(g, c) for g in range(groups) for c in range(members)]
    number = lambda g, c: g * members + c
    stages = (
        (2, grp % 2, lambda g, c, s: (g ^ s, c)),
        (
            2 * planes,
            grp // 2 * 2 + ctx % 2,
            lambda g, c, s: (g ^ (s // 2 * 2), c ^ (s % 2)),
        ),
        (along, ctx // 2, lambda g, c, s: (g, c ^ (2 * s))),
    )

    def swap(array, move, s):
        return lax.ppermute(
            array, AXES, [(number(g, c), number(*move(g, c, s))) for g, c in places]
        )

    def reduce_pieces(stage, part):
        count, index, _ = stage
        piece = part.shape[0] // count
        take = lambda s: lax.dynamic_slice_in_dim(part, (index ^ s) * piece, piece)
        return [take(0)] + [take(s).astype(BF16) for s in range(1, count)]

    def reduce_join(stage, own, came):
        return sum((array.astype(F32) for array in came), own)

    def gather_pieces(stage, part):
        return [part.astype(BF16)] * stage[0]

    def gather_join(stage, own, came):
        count, index, _ = stage
        shares = [own] + came
        step = 1
        while step < count:
            turned = (index // step) % 2 == 1
            shares = [jnp.where(turned, shares[s ^ step], shares[s]) for s in range(count)]
            step *= 2
        return jnp.concatenate(shares)

    def send(stage, pieces):
        return [swap(piece, stage[2], s) for s, piece in enumerate(pieces) if s]

    return [
        (partial(reduce_pieces, stage), partial(send, stage), partial(reduce_join, stage))
        for stage in stages
    ] + [
        (partial(gather_pieces, stage), partial(send, stage), partial(gather_join, stage))
        for stage in reversed(stages)
    ]


def gathered_plan(
    tokens,
    query_counts,
    cotangent,
    query_weight,
    key_weight,
    value_weight,
    output_weight,
    inner_weight,
    inner_bias,
    outer_weight,
    outer_bias,
    first_gain,
    first_shift,
    second_gain,
    second_shift,
):
    blocks, rows, width = tokens.shape
    groups, members = lax.axis_size("grp"), lax.axis_size("ctx")
    member = lax.axis_index("ctx")
    place = member // 2
    context = CTX // members
    slots = QUERIES // members

    far = blocks // 2
    order = [r for r in range(blocks) if r != far] + [far]

    def route(r, back=False):
        pairs = []
        for g in range(groups):
            for c in range(members):
                to = (g - g % 2 + c % 2) * members + ((c // 2 + r) % blocks) * 2 + g % 2
                pairs.append((to, g * members + c) if back else (g * members + c, to))
        return pairs

    across = [
        (g * members + c, (g ^ 1) * members + c) for g in range(groups) for c in range(members)
    ]
    tie = lambda *arrays: lax.optimization_barrier(arrays)

    def block_of(array, r):
        return lax.dynamic_index_in_dim(array, lax.rem(place + r, blocks), 0, keepdims=False)

    def outward(block, r):
        return lax.ppermute(block, AXES, route(r))

    def homeward(block, r):
        return lax.ppermute(block, AXES, route(r, True))

    def put(whole, block, r):
        return lax.dynamic_update_index_in_dim(whole, block, lax.rem(place + r, blocks), 0)

    slot = member * slots + jnp.arange(rows, dtype=jnp.int32) - context
    live = (jnp.arange(rows) < context)[None, :] | (slot[None, :] < query_counts[:, None])
    live = live[:, :, None]
    masked = jnp.where(live, cotangent, 0).astype(BF16)

    scale = HD**-0.5
    log2e = 1.4426950408889634
    kinds = (query_weight, key_weight, value_weight)
    *own, own_far = [outward(block_of(tokens, r), r) for r in order]
    other = [lax.ppermute(block, AXES, across) for block in own]
    qkvx = ()
    for j in range(blocks - 1):
        qkvx = project(own[j], other[j], j, blocks, context, kinds, scale * log2e, qkvx)
    own_far, *qkvx = tie(own_far, *qkvx)
    other_far = lax.ppermute(own_far, AXES, across)
    qkvx = project(
        own_far, other_far, blocks - 1, blocks, context, kinds, scale * log2e, qkvx
    )
    q, k, v, x = qkvx
    k, v = (array.reshape(HEADS, 2 * blocks * context, HD) for array in (k, v))

    *cots, q = tie(*[block_of(masked, r) for r in order], q)
    cots = [outward(block, r) for block, r in zip(cots, order, strict=True)]
    p, attended, totals = attention_forward(q, [k], [v], blocks)
    *cots, p = tie(*cots, p)

    lifted = lambda vector: vector.reshape(1, -1)
    weights = (
        output_weight,
        inner_weight,
        lifted(inner_bias),
        outer_weight,
        lifted(outer_bias),
        lifted(first_gain),
        lifted(first_shift),
        lifted(second_gain),
        lifted(second_shift),
    )
    bit = lax.rem(lax.axis_index("grp"), 2).astype(jnp.int32).reshape(1)
    out, first_grad, grads, delta, keep, given = dense(bit, x, cots, attended, totals, weights)

    stages = summing(groups, members)
    scale_k = 1.0 / log2e
    chunk = blocks * context // 2

    def start(stage, part):
        pieces_of, send, join = stage
        mine, *pieces = pieces_of(part)
        return pieces, lambda pieces: send([mine] + pieces), partial(join, mine)

    *out, given, grads = tie(*out, given, grads)
    came = lax.ppermute(given, AXES, across)
    home = [homeward(out[j], r) for j, r in enumerate(order[:-1])]
    kv_other, dq = attention_backward(q, grads, delta, p, k, v, scale_k, 1.0, chunk, 2, 2)
    *home, came, kv_other, grads = tie(*home, came, kv_other, grads)
    early = keep + came.astype(F32)

    pieces, send, join = start(stages[1], early)
    *pieces, kv_other, far_out, grads = tie(*pieces, kv_other, out[-1], grads)
    kv_came = lax.ppermute(kv_other, AXES, across)
    came = send(pieces)
    home.append(homeward(far_out, far))
    kv_own, dq = attention_backward(q, grads, delta, p, k, v, scale_k, scale, chunk, 0, 2, dq)
    *came, home[-1], kv_came, kv_own = tie(*came, home[-1], kv_came, kv_own)
    early = join(came)

    pieces, send, join = start(stages[2], early)
    *pieces, kv_own = tie(*pieces, kv_own)
    came = send(pieces)
    *token_grad, key_grad, value_grad = finish(first_grad, kv_own, kv_came, dq, kinds, blocks)
    ready = tie(*came, *token_grad)
    came, token_grad = list(ready[: len(came)]), ready[len(came) :]
    early = join(came)

    *token_grad, x = tie(*token_grad, x)
    back = [homeward(token_grad[j], order[j]) for j in range(blocks - 2)]
    keep, given = weigh(bit, x, dq, key_grad, value_grad)
    *back, given, token_three = tie(*back, given, token_grad[-2])
    came = lax.ppermute(given, AXES, across)
    back.append(homeward(token_three, order[-2]))
    late = keep + came.astype(F32)
    pieces, send, join = start(stages[1], late)
    late = join(send(pieces))
    pieces, send, join = start(stages[2], late)
    came = send(pieces)
    *came, back[-1] = tie(*came, back[-1])
    late = join(came)
    shares = (early.shape[0], late.shape[0])
    both = jnp.concatenate([early, late])
    pieces, send, join = start(stages[3], both)
    both = join(send(pieces))
    pieces, send, join = start(stages[4], both)
    *pieces, token_far = tie(*pieces, token_grad[-1])
    came = send(pieces)
    went = homeward(token_far, far)
    *home, live, came[0] = tie(*home, live, came[0])
    layer_out = jnp.zeros((blocks, rows, width), BF16)
    grad_tokens = jnp.zeros((blocks, rows, width), F32)
    for block, r in zip(home, order, strict=True):
        layer_out = put(layer_out, jnp.where(block_of(live, r), block, 0).astype(BF16), r)
    for block, r in zip(back, order, strict=False):
        grad_tokens = put(grad_tokens, block.astype(F32), r)
    *came, went = tie(*came, went)
    both = join(came)
    pieces, send, join = start(stages[5], both)
    both = join(send(pieces)).reshape(-1, sum(shares), width)
    early = both[:, : shares[0]].reshape(-1, width).astype(F32)
    late = both[:, shares[0] :].reshape(-1, width).astype(F32)
    grad_tokens = put(grad_tokens, went.astype(F32), far)

    hidden = inner_weight.shape[1]
    inner_at = [early[at : at + width] for at in range(width, width + hidden, width)]
    vectors = early[width + 2 * hidden :]
    return (
        layer_out,
        grad_tokens,
        late[:width],
        late[width : 2 * width],
        late[2 * width :],
        early[:width],
        jnp.concatenate(inner_at, axis=1),
        vectors[5 : 5 + hidden // width].reshape(hidden),
        early[width + hidden : width + 2 * hidden],
        vectors[4],
        vectors[0],
        vectors[1],
        vectors[2],
        vectors[3],
    )


def solution(mesh):
    return jax.shard_map(
        gathered_plan if one_chip_each(mesh) else spread_plan,
        mesh=mesh,
        in_specs=(
            P("grp", "ctx", None),
            P("grp"),
            P("grp", "ctx", None),
            P(),
            P(),
            P(),
            P(),
            P(),
            P(),
            P(),
            P(),
            P(),
            P(),
            P(),
            P(),
        ),
        out_specs=(
            P("grp", "ctx", None),
            P("grp", "ctx", None),
            P(),
            P(),
            P(),
            P(),
            P(),
            P(),
            P(),
            P(),
            P(),
            P(),
            P(),
            P(),
        ),
        check_vma=False,
    )
```

```python
from functools import partial

import jax
import jax.numpy as jnp
from jax import lax
from jax.experimental import pallas as pl
from jax.experimental.pallas import tpu as pltpu
from jax.sharding import PartitionSpec as P

HEADS = 4
CTX = 4096
QUERIES = 128
NBLK = 4
HD = 128


EPSILON = 1e-05


def product(left, right):
    return jnp.dot(left, right, preferred_element_type=jnp.float32)


def contract_rows(left, right):
    return lax.dot_general(
        left, right, (((0,), (0,)), ((), ())), preferred_element_type=jnp.float32
    )


def contract_last(left, right):
    return lax.dot_general(
        left, right, (((1,), (1,)), ((), ())), preferred_element_type=jnp.float32
    )


def norm_forward(values, gain, shift):
    center = values - jnp.mean(values, axis=-1, keepdims=True)
    inverse = lax.rsqrt(jnp.mean(center * center, axis=-1, keepdims=True) + EPSILON)
    normed = center * inverse
    return (normed * gain + shift, normed, inverse)


def norm_backward(upstream, normed, inverse, gain):
    scaled = upstream * gain
    plain_mean = jnp.mean(scaled, axis=-1, keepdims=True)
    cross_mean = jnp.mean(scaled * normed, axis=-1, keepdims=True)
    value_grad = inverse * (scaled - plain_mean - normed * cross_mean)
    return (value_grad, jnp.sum(upstream * normed, axis=0), jnp.sum(upstream, axis=0))


def spread_plan(
    tokens,
    query_counts,
    cotangent,
    query_weight,
    key_weight,
    value_weight,
    output_weight,
    inner_weight,
    inner_bias,
    outer_weight,
    outer_bias,
    first_gain,
    first_shift,
    second_gain,
    second_shift,
):
    member = lax.axis_index("ctx")
    ctx_count = lax.axis_size("ctx")
    context_dev = CTX // ctx_count
    query_dev = QUERIES // ctx_count
    nb_dev = tokens.shape[0]
    rows_dev = tokens.shape[1]
    width = tokens.shape[2]
    heads_count = HEADS
    head_width = HD
    block_count = nb_dev // NBLK
    scale = head_width ** (-0.5)
    total_rows = nb_dev * rows_dev
    tokens_flat = tokens.reshape(total_rows, width)
    context_rows = tokens[:, :context_dev]
    context_flat = context_rows.reshape(nb_dev * context_dev, width)
    queries = (
        product(tokens_flat, query_weight).astype(jnp.bfloat16).reshape(nb_dev, rows_dev, width)
    )
    keys_own = (
        product(context_flat, key_weight).astype(jnp.bfloat16).reshape(nb_dev, context_dev, width)
    )
    values_own = (
        product(context_flat, value_weight).astype(jnp.bfloat16).reshape(nb_dev, context_dev, width)
    )
    sources = (keys_own, values_own)

    def to_blocks(array):
        return array.reshape((block_count, NBLK) + array.shape[1:])

    def fetch(source):
        keys_mine, values_mine = source
        keys_flat, values_flat = (
            lax.all_gather(keys_mine, "ctx", axis=1, tiled=True),
            lax.all_gather(values_mine, "ctx", axis=1, tiled=True),
        )
        return (keys_flat, values_flat, keys_mine, values_mine)

    def split_heads(array):
        return array.reshape(array.shape[0], array.shape[1], heads_count, head_width)

    def attend(carry, operands):
        queries_blk, source = operands
        keys_flat, values_flat, keys_mine, values_mine = fetch(source)
        query_heads = split_heads(queries_blk)
        scores = (
            jnp.einsum(
                "nrhd,nkhd->nhrk",
                query_heads,
                split_heads(keys_flat),
                preferred_element_type=jnp.float32,
            )
            * scale
        )
        log_total = jax.nn.logsumexp(scores, axis=-1, keepdims=True)
        soft_low = jnp.exp(scores - log_total).astype(jnp.bfloat16)
        mixed = jnp.einsum(
            "nhrk,nkhd->nrhd",
            soft_low,
            split_heads(values_flat),
            preferred_element_type=jnp.float32,
        )
        attended_blk = mixed.reshape(NBLK, rows_dev, width).astype(jnp.bfloat16)
        return (carry, (attended_blk, log_total[..., 0]))

    zero = jnp.zeros((), jnp.float32)
    _, (attended_b, lse_b) = lax.scan(
        attend, zero, (to_blocks(queries), jax.tree.map(to_blocks, sources))
    )
    attended_flat = attended_b.reshape(total_rows, width)
    slot_local = jnp.arange(rows_dev, dtype=jnp.int32) - context_dev
    slot_global = member * query_dev + slot_local
    live_rows = jnp.logical_or(
        slot_local[None, :] < 0, slot_global[None, :] < query_counts[:, None]
    )
    live_flat = live_rows.astype(jnp.float32).reshape(total_rows, 1)
    inner_bias_f = inner_bias.astype(jnp.float32)
    outer_bias_f = outer_bias.astype(jnp.float32)
    first_gain_f = first_gain.astype(jnp.float32)
    second_gain_f = second_gain.astype(jnp.float32)
    first_sum = tokens_flat.astype(jnp.float32) + product(attended_flat, output_weight)
    hidden, normed_one, inverse_one = norm_forward(
        first_sum, first_gain_f, first_shift.astype(jnp.float32)
    )
    hidden_low = hidden.astype(jnp.bfloat16)
    inner = product(hidden_low, inner_weight) + inner_bias_f
    gelu_value, gelu_back = jax.vjp(partial(jax.nn.gelu, approximate=False), inner)
    activated = gelu_value.astype(jnp.bfloat16)
    second_sum = hidden + product(activated, outer_weight) + outer_bias_f
    result, normed_two, inverse_two = norm_forward(
        second_sum, second_gain_f, second_shift.astype(jnp.float32)
    )
    layer_out = (result * live_flat).astype(jnp.bfloat16).reshape(nb_dev, rows_dev, width)
    upstream = cotangent.reshape(total_rows, width).astype(jnp.float32) * live_flat
    second_grad, grad_second_gain, grad_second_shift = norm_backward(
        upstream, normed_two, inverse_two, second_gain_f
    )
    outer_grad = second_grad.astype(jnp.bfloat16)
    grad_outer = contract_rows(activated, outer_grad)
    grad_outer_bias = jnp.sum(outer_grad.astype(jnp.float32), axis=0)
    inner_grad = gelu_back(contract_last(outer_grad, outer_weight))[0].astype(jnp.bfloat16)
    grad_inner = contract_rows(hidden_low, inner_grad)
    grad_inner_bias = jnp.sum(inner_grad.astype(jnp.float32), axis=0)
    hidden_grad = second_grad + contract_last(inner_grad, inner_weight)
    first_grad, grad_first_gain, grad_first_shift = norm_backward(
        hidden_grad, normed_one, inverse_one, first_gain_f
    )
    branch_grad = first_grad.astype(jnp.bfloat16)
    grad_output = contract_rows(attended_flat, branch_grad)
    attended_grad = (
        contract_last(branch_grad, output_weight)
        .astype(jnp.bfloat16)
        .reshape(nb_dev, rows_dev, width)
    )

    def attend_back(carry, operands):
        queries_blk, grads_blk, lse_blk, source = operands
        keys_flat, values_flat, keys_mine, values_mine = fetch(source)
        query_heads = split_heads(queries_blk)
        grad_heads = split_heads(grads_blk)
        key_heads = split_heads(keys_flat)
        value_heads = split_heads(values_flat)
        scores = (
            jnp.einsum(
                "nrhd,nkhd->nhrk", query_heads, key_heads, preferred_element_type=jnp.float32
            )
            * scale
        )
        soft = jnp.exp(scores - lse_blk[..., None])
        soft_grad = jnp.einsum(
            "nrhd,nkhd->nhrk", grad_heads, value_heads, preferred_element_type=jnp.float32
        )
        row_delta = jnp.sum(soft * soft_grad, axis=-1)
        score_grad = (soft * (soft_grad - row_delta[..., None])).astype(jnp.bfloat16)
        query_grad = (
            jnp.einsum("nhrk,nkhd->nrhd", score_grad, key_heads, preferred_element_type=jnp.float32)
            * scale
        )
        query_grad = query_grad.reshape(NBLK, rows_dev, width).astype(jnp.bfloat16)
        soft_low = soft.astype(jnp.bfloat16)
        key_part = (
            jnp.einsum(
                "nhrk,nrhd->nkhd", score_grad, query_heads, preferred_element_type=jnp.float32
            )
            * scale
        )
        value_part = jnp.einsum(
            "nhrk,nrhd->nkhd", soft_low, grad_heads, preferred_element_type=jnp.float32
        )
        key_sum, value_sum = (
            lax.psum_scatter(
                key_part.reshape(NBLK, -1, width), "ctx", scatter_dimension=1, tiled=True
            ),
            lax.psum_scatter(
                value_part.reshape(NBLK, -1, width), "ctx", scatter_dimension=1, tiled=True
            ),
        )
        key_grad = key_sum.astype(jnp.bfloat16)
        value_grad = value_sum.astype(jnp.bfloat16)
        return (carry, (query_grad, key_grad, value_grad))

    _, (query_grad_b, key_grad_b, value_grad_b) = lax.scan(
        attend_back,
        zero,
        (to_blocks(queries), to_blocks(attended_grad), lse_b, jax.tree.map(to_blocks, sources)),
    )
    query_grad = query_grad_b.reshape(total_rows, width)
    key_grad = key_grad_b.reshape(nb_dev * context_dev, width)
    value_grad = value_grad_b.reshape(nb_dev * context_dev, width)
    grad_query = contract_rows(tokens_flat, query_grad)
    grad_key = contract_rows(context_flat, key_grad)
    grad_value = contract_rows(context_flat, value_grad)
    token_grad = (first_grad + contract_last(query_grad, query_weight)).reshape(
        nb_dev, rows_dev, width
    )
    context_back = (
        contract_last(key_grad, key_weight) + contract_last(value_grad, value_weight)
    ).reshape(nb_dev, context_dev, width)
    grad_tokens = jnp.concatenate(
        [token_grad[:, :context_dev] + context_back, token_grad[:, context_dev:]], axis=1
    )
    finals = lax.psum(
        (
            grad_query,
            grad_key,
            grad_value,
            grad_output,
            grad_inner,
            grad_inner_bias,
            grad_outer,
            grad_outer_bias,
            grad_first_gain,
            grad_first_shift,
            grad_second_gain,
            grad_second_shift,
        ),
        ("grp", "ctx"),
    )
    return (layer_out, grad_tokens) + tuple(finals)


BF16, F32 = jnp.bfloat16, jnp.float32
MIB = 2**20
AXES = ("grp", "ctx")
LANES = 128
ROWS_STEP = 528


def one_chip_each(mesh):
    return mesh.shape["grp"] % 2 == 0 and mesh.shape["ctx"] == 2 * NBLK


def dot(left, right, over_left, over_right):
    return lax.dot_general(
        left, right, (((over_left,), (over_right,)), ((), ())), preferred_element_type=F32
    )


def kernel_call(body, grid, ins, outs, scratch, flops, moved, *operands, exps=0, into=()):
    given = len(ins)

    def run(*refs):
        body(*refs[:given], *refs[given + len(into) :])

    return pl.pallas_call(
        run,
        grid=grid,
        in_specs=[
            pl.BlockSpec(memory_space=index) if shape is None else pl.BlockSpec(shape, index)
            for shape, index in ins
        ]
        + [pl.BlockSpec(memory_space=pl.ANY)] * len(into),
        out_specs=[
            pl.BlockSpec(memory_space=index) if shape is None else pl.BlockSpec(shape, index)
            for shape, index, _, _ in outs
        ],
        out_shape=[jax.ShapeDtypeStruct(shape, kind) for _, _, shape, kind in outs],
        scratch_shapes=scratch,
        input_output_aliases={given + j: j for j in range(len(into))},
        cost_estimate=pl.CostEstimate(flops=flops, bytes_accessed=moved, transcendentals=exps),
        compiler_params=pltpu.CompilerParams(vmem_limit_bytes=60 * MIB),
    )(*operands, *into)


def project_kernel(context, scale, own, other, wq, wk, wv, q_out, k_out, v_out, x_out):
    rows = own[...]
    x_out[0] = rows
    queries = (dot(rows, wq[...], 1, 0) * scale).astype(BF16)
    for h in range(HEADS):
        q_out[h] = queries[:, h * HD : (h + 1) * HD]
    for side, keys_of in enumerate((rows[:context], other[:context])):
        keys = dot(keys_of, wk[...], 1, 0).astype(BF16)
        values = dot(keys_of, wv[...], 1, 0).astype(BF16)
        for h in range(HEADS):
            k_out[h, side, 0] = keys[:, h * HD : (h + 1) * HD]
            v_out[h, side, 0] = values[:, h * HD : (h + 1) * HD]


def project(own, other, place, blocks, context, kinds, scale, into):
    rows, width = own.shape
    fixed = lambda b: (0, 0)
    key_spec = (
        (HEADS, 2, 1, context, HD),
        lambda b: (0, 0, place, 0, 0),
        (HEADS, 2, blocks, context, HD),
        BF16,
    )
    return kernel_call(
        partial(project_kernel, context, scale),
        (1,),
        [((rows, width), fixed)] * 2 + [((width, width), fixed)] * 3,
        [
            ((HEADS, rows, HD), lambda b: (0, place, 0), (HEADS, blocks * rows, HD), BF16),
            key_spec,
            key_spec,
            ((1, rows, width), lambda b: (place, 0, 0), (blocks, rows, width), BF16),
        ],
        [],
        2 * width * width * (rows + 4 * context),
        4 * width * (rows + 3 * context),
        own,
        other,
        *kinds,
        into=into,
    )


def forward_kernel(sets, steps, row_blocks, chunk, q_ref, *refs):
    k_refs, v_refs, refs = refs[:sets], refs[sets : 2 * sets], refs[2 * sets :]
    p_ref, o_ref, sum_ref, s_even, s_odd, top_even, top_odd, v_wide = refs
    t = pl.program_id(0)
    rows, hd = q_ref.shape[-2:]
    keys = p_ref.shape[-1]

    @pl.when(t == 0)
    def _():
        v_wide[:, hd:] = jnp.ones((keys, hd), BF16)

    @pl.when((t > 0) & (lax.rem(t - 1, row_blocks) == 0))
    def _():
        start = 0
        for v_ref in v_refs:
            v_wide[start : start + v_ref.shape[1], :hd] = v_ref[0]
            start += v_ref.shape[1]

    places = []
    for k_ref in k_refs:
        places += [(k_ref, slice(c, c + chunk)) for c in range(0, k_ref.shape[1], chunk)]

    def body(score, weigh, s_now, s_before, top_now, top_before):
        if score:
            q = q_ref[0]
            high = None
        if weigh:
            peak = jnp.max(top_before[...], axis=-1, keepdims=True)
            total = jnp.zeros((rows, 2 * hd), F32)
        for c, (k_ref, within) in enumerate(places):
            at = slice(c * chunk, (c + 1) * chunk)
            if score:
                scores = dot(q, k_ref[0, within, :], 1, 1)
                s_now[:, at] = scores
                for j in range(chunk // LANES):
                    part = scores[:, j * LANES : (j + 1) * LANES]
                    high = part if high is None else jnp.maximum(high, part)
            if weigh:
                soft = jnp.exp2(s_before[:, at] - peak).astype(BF16)
                p_ref[0, :, at] = soft
                total = total + dot(soft, v_wide[at, :], 1, 0)
        if score:
            top_now[...] = high
        if weigh:
            o_ref[...] = total[:, :hd]
            sum_ref[0] = total[:, hd:]

    even = (s_even, s_odd, top_even, top_odd)
    odd = (s_odd, s_even, top_odd, top_even)
    inside = (t > 0) & (t < steps)
    pl.when(inside & (lax.rem(t, 2) == 0))(lambda: body(True, True, *even))
    pl.when(inside & (lax.rem(t, 2) == 1))(lambda: body(True, True, *odd))
    pl.when(t == 0)(lambda: body(True, False, *even))
    pl.when(t == steps)(lambda: body(False, True, *(odd if steps % 2 else even)))


def attention_forward(q, ks, vs, row_blocks, chunk=512):
    heads, total, hd = q.shape
    keys = sum(k.shape[1] for k in ks)
    rows = total // row_blocks
    steps = heads * row_blocks
    ahead = lambda t: jnp.minimum(t, steps - 1)
    behind = lambda t: jnp.maximum(t - 1, 0)
    by_row = lambda t: (behind(t) // row_blocks, behind(t) % row_blocks, 0)
    per_row = ((1, rows, hd), by_row, (heads, total, hd), F32)
    return kernel_call(
        partial(forward_kernel, len(ks), steps, row_blocks, chunk),
        (steps + 1,),
        [((1, rows, hd), lambda t: (ahead(t) // row_blocks, ahead(t) % row_blocks, 0))]
        + [((1, k.shape[1], hd), lambda t: (ahead(t) // row_blocks, 0, 0)) for k in ks]
        + [((1, v.shape[1], hd), lambda t: (behind(t) // row_blocks, 0, 0)) for v in vs],
        [
            ((1, rows, keys), by_row, (heads, total, keys), BF16),
            (
                (rows, hd),
                lambda t: (behind(t) % row_blocks, behind(t) // row_blocks),
                (total, heads * hd),
                F32,
            ),
            per_row,
        ],
        [
            pltpu.VMEM((rows, keys), F32),
            pltpu.VMEM((rows, keys), F32),
            pltpu.VMEM((rows, LANES), F32),
            pltpu.VMEM((rows, LANES), F32),
            pltpu.VMEM((keys, 2 * hd), BF16),
        ],
        8 * heads * total * keys * hd,
        2 * heads * total * keys,
        q,
        *ks,
        *vs,
        exps=heads * total * keys,
    )


def gelu_pair(inner):
    size = jnp.abs(inner) * (0.5**0.5)
    rate = 1.0 / (1.0 + 0.3275911 * size)
    bell = jnp.exp(-(size * size))
    tail = rate * (
        0.254829592
        + rate * (-0.284496736 + rate * (1.421413741 + rate * (-1.453152027 + rate * 1.061405429)))
    )
    tail = 0.5 * tail * bell
    below = jnp.where(inner < 0, tail, 1.0 - tail)
    return inner * below, below + inner * bell * 0.3989422804014327


def dense_kernel(
    blocks, steps, bit_ref, x_ref, o_ref, total_ref, wo, w1, b1, w2, b2, g1, s1, g2, s2, *refs
):
    cot_refs, refs = refs[:blocks], refs[blocks:]
    out_refs, refs = refs[:blocks], refs[blocks:]
    first_ref, grad_ref, delta_ref, keep_ref, send_ref = refs[:5]
    sums, sending, cot, out, arrived, left = refs[5:]
    t = pl.program_id(0)
    width, hidden_width = w1.shape
    rows, half = x_ref.shape[0], sending.shape[0]
    block = cot.shape[0] // blocks
    load = [
        pltpu.make_async_copy(ref, cot.at[pl.ds(j * block, block)], arrived.at[j])
        for j, ref in enumerate(cot_refs)
    ]
    store = [
        pltpu.make_async_copy(out.at[pl.ds(j * block, block)], ref, left.at[j])
        for j, ref in enumerate(out_refs)
    ]

    @pl.when(t == 0)
    def _():
        for copy in load:
            copy.start()
        sums[...] = jnp.zeros_like(sums)

    for j, copy in enumerate(load):
        pl.when(t == j * block // rows)(copy.wait)
    here = pl.ds(pl.multiple_of(t * rows, 16), rows)
    gain_one, gain_two = g1[...].astype(F32), g2[...].astype(F32)
    inverses = [1.0 / total_ref[h] for h in range(HEADS)]
    attended = jnp.concatenate(
        [o_ref[:, h * HD : (h + 1) * HD] * inverses[h] for h in range(HEADS)], axis=1
    )
    attended_low = attended.astype(BF16)
    first_sum = x_ref[...].astype(F32) + dot(attended_low, wo[...], 1, 0)
    hidden, normed_one, inverse_one = norm_forward(first_sum, gain_one, s1[...].astype(F32))
    hidden_low = hidden.astype(BF16)
    inner = dot(hidden_low, w1[...], 1, 0) + b1[...].astype(F32)
    activated, slope = gelu_pair(inner)
    activated = activated.astype(BF16)
    second_sum = hidden + dot(activated, w2[...], 1, 0) + b2[...].astype(F32)
    result, normed_two, inverse_two = norm_forward(second_sum, gain_two, s2[...].astype(F32))
    out[here, :] = result.astype(BF16)
    upstream = cot[here, :].astype(F32)
    second_grad, gain_two_sum, shift_two_sum = norm_backward(
        upstream, normed_two, inverse_two, gain_two
    )
    outer_grad = second_grad.astype(BF16)
    at = width + hidden_width
    sums[at : at + hidden_width] += dot(activated, outer_grad, 0, 0)
    inner_grad = (dot(outer_grad, w2[...], 1, 1) * slope).astype(BF16)
    inner_sums = dot(hidden_low, inner_grad, 0, 0)
    for j in range(0, hidden_width, width):
        sums[width + j : 2 * width + j] += inner_sums[:, j : j + width]
    hidden_grad = second_grad + dot(inner_grad, w1[...], 1, 1)
    first_grad, gain_one_sum, shift_one_sum = norm_backward(
        hidden_grad, normed_one, inverse_one, gain_one
    )
    branch_grad = first_grad.astype(BF16)
    first_ref[...] = branch_grad
    sums[:width] += dot(attended_low, branch_grad, 0, 0)
    attended_grad = dot(branch_grad, wo[...], 1, 1)
    for h in range(HEADS):
        at = slice(h * HD, (h + 1) * HD)
        scaled = (attended_grad[:, at] * inverses[h]).astype(BF16)
        grad_ref[h] = scaled
        delta = jnp.sum(scaled.astype(F32) * attended[:, at], axis=-1, keepdims=True)
        delta_ref[h] = jnp.broadcast_to(delta, delta_ref.shape[1:])
    inner_sum = jnp.sum(inner_grad.astype(F32), axis=0)
    vectors = [
        gain_one_sum,
        shift_one_sum,
        gain_two_sum,
        shift_two_sum,
        jnp.sum(outer_grad.astype(F32), axis=0),
    ]
    vectors += [inner_sum[j : j + width] for j in range(0, hidden_width, width)]
    at = width + 2 * hidden_width
    for j, part in enumerate(vectors):
        sums[at + j : at + j + 1, :] += part[None, :]

    @pl.when(t == steps - 1)
    def _():
        bit = bit_ref[0]
        keep = pltpu.make_async_copy(
            sums.at[pl.ds(pl.multiple_of(bit * half, 16), half)], keep_ref, arrived.at[0]
        )
        sending[...] = sums[pl.ds(pl.multiple_of((1 - bit) * half, 16), half)].astype(BF16)
        send = pltpu.make_async_copy(sending, send_ref, arrived.at[1])
        copies = [*store, keep, send]
        for copy in copies:
            copy.start()
        for copy in copies:
            copy.wait()


def dense(bit, x, cots, attended, total_of, weights, steps=3):
    blocks, block, width = x.shape
    total = blocks * block
    rows = total // steps
    hidden = weights[1].shape[1]
    by_row = ((rows, width), lambda t: (t, 0))
    by_head = ((HEADS, rows, HD), lambda t: (0, t, 0))
    count = -(-(width + 2 * hidden + 8) // 512) * 512
    *out, first_grad, grads, delta, keep, send = kernel_call(
        partial(dense_kernel, blocks, steps),
        (steps,),
        [(None, pltpu.SMEM), by_row, by_row, by_head]
        + [(w.shape, lambda t: (0, 0)) for w in weights]
        + [(None, pl.ANY)] * blocks,
        [(None, pl.ANY, (block, width), BF16)] * blocks
        + [
            (*by_row, (total, width), BF16),
            (*by_head, (HEADS, total, HD), BF16),
            (*by_head, (HEADS, total, HD), F32),
            (None, pl.ANY, (count // 2, width), F32),
            (None, pl.ANY, (count // 2, width), BF16),
        ],
        [
            pltpu.VMEM((count, width), F32),
            pltpu.VMEM((count // 2, width), BF16),
            pltpu.VMEM((total, width), BF16),
            pltpu.VMEM((total, width), BF16),
            pltpu.SemaphoreType.DMA((blocks,)),
            pltpu.SemaphoreType.DMA((blocks,)),
        ],
        6 * total * width * (width + 2 * hidden),
        32 * total * width + 8 * width * (width + 2 * hidden),
        bit,
        x.reshape(total, width),
        attended,
        total_of,
        *weights,
        *cots,
    )
    return out, first_grad, grads, delta, keep, send


def backward_kernel(scale_k, scale_q, carried, q_ref, g_ref, d_ref, p_ref, k_ref, v_ref, *refs):
    if carried:
        before, refs = refs[0], refs[1:]
    kv_ref, dq_ref, dq_sum, ds, q_t, g_t = refs
    c = pl.program_id(1)

    @pl.when(c == 0)
    def _():
        q_t[...] = q_ref[0].T
        g_t[...] = g_ref[0].T
        dq_sum[...] = before[0] if carried else jnp.zeros_like(dq_sum)

    keys, values = k_ref[0], v_ref[0]
    chunk = keys.shape[0]
    for start in range(0, p_ref.shape[1], ROWS_STEP):
        at = slice(start, start + ROWS_STEP)
        soft_grad = dot(g_ref[0, at, :], values, 1, 1)
        delta = jnp.concatenate([d_ref[0, at, :]] * (chunk // LANES), axis=1)
        score_grad = (p_ref[0, at, :].astype(F32) * (soft_grad - delta)).astype(BF16)
        ds[at, :] = score_grad
        dq_sum[at, :] += dot(score_grad, keys, 1, 0)
    dv = dot(g_t[...], p_ref[0], 1, 0).T
    dk = dot(q_t[...], ds[...], 1, 0).T * scale_k
    kv_ref[0, 0] = dk.astype(BF16)
    kv_ref[1, 0] = dv.astype(BF16)

    @pl.when(c == pl.num_programs(1) - 1)
    def _():
        dq_ref[0] = (dq_sum[...] * scale_q).astype(dq_ref.dtype)


def attention_backward(q, g, d, p, k, v, scale_k, scale_q, chunk, first, chunks, before=None):
    heads, total, hd = q.shape
    row = lambda h, c: (h, 0, 0)
    key = lambda h, c: (h, c + first, 0)
    by_row = ((1, total, hd), row)
    carried = before is not None
    return kernel_call(
        partial(backward_kernel, scale_k, scale_q, carried),
        (heads, chunks),
        [
            by_row,
            by_row,
            by_row,
            ((1, total, chunk), lambda h, c: (h, 0, c + first)),
            ((1, chunk, hd), key),
            ((1, chunk, hd), key),
        ]
        + [by_row] * carried,
        [
            ((2, 1, chunk, hd), lambda h, c: (0, h, c, 0), (2, heads, chunks * chunk, hd), BF16),
            (*by_row, (heads, total, hd), BF16 if carried else F32),
        ],
        [
            pltpu.VMEM((total, hd), F32),
            pltpu.VMEM((total, chunk), BF16),
            pltpu.VMEM((hd, total), BF16),
            pltpu.VMEM((hd, total), BF16),
        ],
        12 * heads * total * chunk * chunks * hd,
        2 * heads * total * chunk * chunks,
        q,
        g,
        d,
        p,
        k,
        v,
        *[before] * carried,
    )


def side_by_side(parts):
    return jnp.concatenate([part.astype(BF16) for part in parts], axis=1)


def weigh_kernel(
    bit_ref, x_ref, query_ref, own_ref, other_ref, keep_ref, send_ref, sums, sending, left
):
    s = pl.program_id(0)
    blocks, rows, width = x_ref.shape
    context = own_ref.shape[2] // blocks
    per = query_ref.shape[0]
    columns = per * HD
    x = x_ref[...].reshape(blocks * rows, width)
    above = x_ref[:, :context].reshape(blocks * context, width)
    three = [dot(x, side_by_side([query_ref[h] for h in range(per)]), 0, 0)]
    for j in range(2):
        whole = side_by_side(
            [own_ref[j, h].astype(F32) + other_ref[j, h].astype(F32) for h in range(per)]
        )
        three.append(dot(above, whole, 0, 0))
    steps = width // columns
    for j in range(steps):

        @pl.when(s == j)
        def _(j=j):
            for i, part in enumerate(three):
                sums[i * width : (i + 1) * width, j * columns : (j + 1) * columns] = part

    @pl.when(s == steps - 1)
    def _():
        bit = bit_ref[0]
        half = sending.shape[0]
        keep = pltpu.make_async_copy(
            sums.at[pl.ds(pl.multiple_of(bit * half, 16), half)], keep_ref, left.at[0]
        )
        keep.start()
        sending[...] = sums[pl.ds(pl.multiple_of((1 - bit) * half, 16), half)].astype(BF16)
        send = pltpu.make_async_copy(sending, send_ref, left.at[1])
        send.start()
        keep.wait()
        send.wait()


def weigh(bit, x, query_grad, own, other, per=2):
    blocks, rows, width = x.shape
    keys = own.shape[2]
    side = ((2, per, keys, HD), lambda s: (0, s, 0, 0))
    half = 3 * width // 2
    return kernel_call(
        weigh_kernel,
        (HEADS // per,),
        [
            (None, pltpu.SMEM),
            (x.shape, lambda s: (0, 0, 0)),
            ((per, blocks * rows, HD), lambda s: (s, 0, 0)),
            side,
            side,
        ],
        [(None, pl.ANY, (half, width), F32), (None, pl.ANY, (half, width), BF16)],
        [
            pltpu.VMEM((3 * width, width), F32),
            pltpu.VMEM((half, width), BF16),
            pltpu.SemaphoreType.DMA((2,)),
        ],
        2 * width * width * (blocks * rows + 2 * keys),
        2 * width * (2 * blocks * rows + 4 * keys),
        bit,
        x,
        query_grad,
        own,
        other,
    )


def finish_kernel(context, count, first_ref, query_ref, own, other, wq, wk, wv, *refs):
    token_refs, (tokens, left) = refs[:count], refs[count:]
    b = pl.program_id(0)
    query_grad = side_by_side([query_ref[h, 0] for h in range(HEADS)])
    key_grad, value_grad = (
        side_by_side(
            [own[j, h, 0].astype(F32) + other[j, h, 0].astype(F32) for h in range(HEADS)]
        )
        for j in range(2)
    )
    base = first_ref[0].astype(F32) + dot(query_grad, wq[...], 1, 1)
    back = dot(key_grad, wk[...], 1, 1) + dot(value_grad, wv[...], 1, 1)
    tokens[b, :context] = (base[:context] + back).astype(BF16)
    tokens[b, context:] = base[context:].astype(BF16)
    store = [
        pltpu.make_async_copy(tokens.at[j], ref, left.at[j]) for j, ref in enumerate(token_refs)
    ]
    for j, copy in enumerate(store):
        pl.when(b == j)(copy.start)

    @pl.when(b == count - 1)
    def _():
        for copy in store:
            copy.wait()


def finish(ahead, first_grad, own, other, query_grad, kinds, blocks):
    first, last = ahead[0], ahead[-1]
    count = len(ahead)
    at = lambda b: first + b * (last - first)
    total, width = first_grad.shape
    rows = total // blocks
    context = own.shape[2] // blocks
    side = ((2, HEADS, 1, context, HD), lambda b: (0, 0, at(b), 0, 0))
    return kernel_call(
        partial(finish_kernel, context, count),
        (count,),
        [
            ((1, rows, width), lambda b: (at(b), 0, 0)),
            ((HEADS, 1, rows, HD), lambda b: (0, at(b), 0, 0)),
            side,
            side,
        ]
        + [((width, width), lambda b: (0, 0))] * 3,
        [(None, pl.ANY, (rows, width), BF16)] * count,
        [pltpu.VMEM((count, rows, width), BF16), pltpu.SemaphoreType.DMA((count,))],
        2 * count * width * width * (rows + 2 * context),
        6 * count * width * (rows + 2 * context),
        first_grad.reshape(blocks, rows, width),
        query_grad.reshape(HEADS, blocks, rows, HD),
        own.reshape(2, HEADS, blocks, context, HD),
        other.reshape(2, HEADS, blocks, context, HD),
        *kinds,
    )


def unpack_kernel(counts, shares, place_ref, half_ref, *refs):
    outs, (early, late, left) = refs[:7], refs[7:]
    grad_query, grad_key, grad_value, grad_output, grad_inner, grad_outer, vectors = outs
    first, second = shares
    across, along = counts
    share = first + second
    for s in range(across):
        for u in range(along):
            at = (s * along + u) * share
            number = (place_ref[1] ^ s) * along + (place_ref[2] ^ u)
            early[pl.ds(pl.multiple_of(number * first, 16), first)] = half_ref[
                at : at + first
            ].astype(F32)
            late[pl.ds(pl.multiple_of(number * second, 16), second)] = half_ref[
                at + first : at + share
            ].astype(F32)
    width, hidden = grad_inner.shape
    middle = late.shape[0] - width

    def copy_out(pieces):
        copies = [
            pltpu.make_async_copy(source.at[pl.ds(start, size)], ref, left.at[j])
            for j, (source, start, size, ref) in enumerate(pieces)
        ]
        for copy in copies:
            copy.start()
        for copy in copies:
            copy.wait()

    @pl.when(place_ref[0] == 0)
    def _():
        pieces = [(late, 0, width, grad_query), (late, width, middle, grad_key.at[:middle])]
        pieces.append((early, 0, width, grad_output))
        for j in range(0, hidden, width):
            pieces.append((early, width + j, width, grad_inner.at[:, pl.ds(j, width)]))
        copy_out(pieces)

    @pl.when(place_ref[0] == 1)
    def _():
        copy_out(
            [
                (late, 0, width - middle, grad_key.at[middle:]),
                (late, width - middle, width, grad_value),
                (early, 0, hidden, grad_outer),
                (early, hidden, vectors.shape[0], vectors),
            ]
        )


def unpack(places, half, counts, shares, hidden, into=()):
    width = half.shape[1]
    total = counts[0] * counts[1]
    shapes = [(width, width)] * 4 + [(width, hidden), (hidden, width), (16, width)]
    return kernel_call(
        partial(unpack_kernel, counts, shares),
        (1,),
        [(None, pltpu.SMEM), (half.shape, lambda b: (0, 0))],
        [(None, pl.ANY, shape, F32) for shape in shapes],
        [
            pltpu.VMEM((total * shares[0], width), F32),
            pltpu.VMEM((total * shares[1], width), F32),
            pltpu.SemaphoreType.DMA((3 + hidden // width,)),
        ],
        0,
        6 * half.size,
        places,
        half,
        into=into,
    )


def summing(groups, members):
    grp, ctx = lax.axis_index("grp"), lax.axis_index("ctx")
    planes, along = groups // 2, members // 2
    places = [(g, c) for g in range(groups) for c in range(members)]
    number = lambda g, c: g * members + c
    stages = (
        (2, grp % 2, lambda g, c, s: (g ^ s, c)),
        (
            2 * planes,
            grp // 2 * 2 + ctx % 2,
            lambda g, c, s: (g ^ (s // 2 * 2), c ^ (s % 2)),
        ),
        (along, ctx // 2, lambda g, c, s: (g, c ^ (2 * s))),
    )

    def swap(array, move, s):
        return lax.ppermute(
            array, AXES, [(number(g, c), number(*move(g, c, s))) for g, c in places]
        )

    def reduce_pieces(stage, parts):
        count, index, _ = stage
        piece = parts[0].shape[0] // count

        def take(s):
            at = (index ^ s) * piece
            return sum(lax.dynamic_slice_in_dim(part, at, piece).astype(F32) for part in parts)

        return [take(0)] + [take(s).astype(BF16) for s in range(1, count)]

    def reduce_join(stage, own, came):
        return [own, *came]

    def gather_pieces(stage, part):
        return [part.astype(BF16)] * stage[0]

    def gather_join(stage, own, came):
        return jnp.concatenate([own] + came)

    def send(stage, pieces):
        return [swap(piece, stage[2], s) for s, piece in enumerate(pieces) if s]

    return [
        (partial(reduce_pieces, stage), partial(send, stage), partial(reduce_join, stage))
        for stage in stages
    ] + [
        (partial(gather_pieces, stage), partial(send, stage), partial(gather_join, stage))
        for stage in reversed(stages)
    ], stages


def gathered_plan(
    tokens,
    query_counts,
    cotangent,
    query_weight,
    key_weight,
    value_weight,
    output_weight,
    inner_weight,
    inner_bias,
    outer_weight,
    outer_bias,
    first_gain,
    first_shift,
    second_gain,
    second_shift,
):
    blocks, rows, width = tokens.shape
    groups, members = lax.axis_size("grp"), lax.axis_size("ctx")
    member = lax.axis_index("ctx")
    place = member // 2
    context = CTX // members
    slots = QUERIES // members

    far = blocks // 2
    order = [r for r in range(1, blocks) if r != far] + [0, far]

    def route(r, back=False):
        pairs = []
        for g in range(groups):
            for c in range(members):
                to = (g - g % 2 + c % 2) * members + ((c // 2 + r) % blocks) * 2 + g % 2
                pairs.append((to, g * members + c) if back else (g * members + c, to))
        return pairs

    across = [
        (g * members + c, (g ^ 1) * members + c) for g in range(groups) for c in range(members)
    ]
    tie = lambda *arrays: lax.optimization_barrier(arrays)

    def block_of(array, r):
        return lax.dynamic_index_in_dim(array, lax.rem(place + r, blocks), 0, keepdims=False)

    def outward(block, r):
        return lax.ppermute(block, AXES, route(r))

    def homeward(block, r):
        return lax.ppermute(block, AXES, route(r, True))

    def put(whole, block, r):
        return lax.dynamic_update_index_in_dim(whole, block, lax.rem(place + r, blocks), 0)

    slot = member * slots + jnp.arange(rows, dtype=jnp.int32) - context
    live = (jnp.arange(rows) < context)[None, :] | (slot[None, :] < query_counts[:, None])
    live = live[:, :, None]
    masked = jnp.where(live, cotangent, 0).astype(BF16)

    scale = HD**-0.5
    log2e = 1.4426950408889634
    kinds = (query_weight, key_weight, value_weight)
    *own, own_far = [outward(block_of(tokens, r), r) for r in order]
    other = [lax.ppermute(block, AXES, across) for block in own]
    qkvx = ()
    for j in range(blocks - 1):
        qkvx = project(own[j], other[j], j, blocks, context, kinds, scale * log2e, qkvx)
    own_far, *qkvx = tie(own_far, *qkvx)
    other_far = lax.ppermute(own_far, AXES, across)
    qkvx = project(
        own_far, other_far, blocks - 1, blocks, context, kinds, scale * log2e, qkvx
    )
    q, k, v, x = qkvx
    k, v = (array.reshape(HEADS, 2 * blocks * context, HD) for array in (k, v))

    *cots, q = tie(*[block_of(masked, r) for r in order], q)
    cots = [outward(block, r) for block, r in zip(cots, order, strict=True)]
    p, attended, totals = attention_forward(q, [k], [v], blocks)
    *cots, p = tie(*cots, p)

    lifted = lambda vector: vector.reshape(1, -1)
    weights = (
        output_weight,
        inner_weight,
        lifted(inner_bias),
        outer_weight,
        lifted(outer_bias),
        lifted(first_gain),
        lifted(first_shift),
        lifted(second_gain),
        lifted(second_shift),
    )
    bit = lax.rem(lax.axis_index("grp"), 2).astype(jnp.int32).reshape(1)
    out, first_grad, grads, delta, keep, given = dense(bit, x, cots, attended, totals, weights)

    stages, stages_of = summing(groups, members)
    scale_k = 1.0 / log2e
    chunk = blocks * context // 2

    added = lambda parts: sum(part.astype(F32) for part in parts)

    def start(stage, part):
        pieces_of, send, join = stage
        mine, *pieces = pieces_of(part)
        return pieces, lambda pieces: send([mine] + pieces), partial(join, mine)

    *out, given, grads = tie(*out, given, grads)
    came = lax.ppermute(given, AXES, across)
    home = [homeward(out[j], r) for j, r in enumerate(order[:-1])]
    kv_other, dq = attention_backward(q, grads, delta, p, k, v, scale_k, 1.0, chunk, 2, 2)
    *home, came, kv_other, grads = tie(*home, came, kv_other, grads)
    pieces, send, early_join = start(stages[1], [keep, came])
    *pieces, kv_other, far_out, grads = tie(*pieces, kv_other, out[-1], grads)
    kv_came = lax.ppermute(kv_other, AXES, across)
    early_came = send(pieces)
    home.append(homeward(far_out, far))
    kv_own, dq = attention_backward(q, grads, delta, p, k, v, scale_k, scale, chunk, 0, 2, dq)
    *early_came, home[-1], kv_came, kv_own = tie(*early_came, home[-1], kv_came, kv_own)

    token_of = lambda places, after: finish(
        places, after, kv_own, kv_came, dq, kinds, blocks
    )
    three = token_of([1], first_grad)[0]
    three, first_grad = tie(three, first_grad)
    three = homeward(three, order[1])
    one, two = token_of([2, 0], first_grad)
    one, two, x = tie(one, two, x)
    keep, given = weigh(bit, x, dq, kv_own, kv_came)
    three, given, first_grad = tie(three, given, first_grad)
    came = lax.ppermute(given, AXES, across)
    last = token_of([3], first_grad)[0]
    came, last = tie(came, last)

    pieces, send, join = start(stages[1], [keep, came])
    *pieces, two = tie(*pieces, two)
    came = send(pieces)
    two = homeward(two, order[0])
    *came, two = tie(*came, two)
    late = added(join(came))
    early = added(early_join(early_came))

    along = members // 2
    shares = (early.shape[0] // along, late.shape[0] // along)
    both = jnp.concatenate(
        [early.reshape(along, shares[0], width), late.reshape(along, shares[1], width)], axis=1
    ).reshape(-1, width)
    pieces, send, join = start(stages[2], [both])
    came = send(pieces)
    grad_tokens = jnp.zeros((blocks, rows, width), F32)
    grad_tokens = put(grad_tokens, three.astype(F32), order[1])
    *came, grad_tokens, one = tie(*came, grad_tokens, one)
    both = added(join(came))

    pieces, send, join = start(stages[3], both)
    *home, live, one, pieces[0] = tie(*home, live, one, pieces[0])
    came = send(pieces)
    one = homeward(one, order[2])
    grad_tokens = put(grad_tokens, two.astype(F32), order[0])
    *came, one, grad_tokens = tie(*came, one, grad_tokens)
    both = join(came)

    pieces, send, join = start(stages[4], both)
    *pieces, last = tie(*pieces, last)
    came = send(pieces)
    last = homeward(last, far)
    grad_tokens = put(grad_tokens, one.astype(F32), order[2])
    layer_out = jnp.zeros((blocks, rows, width), BF16)
    for block, r in zip(home, order, strict=True):
        layer_out = put(layer_out, jnp.where(block_of(live, r), block, 0).astype(BF16), r)
    *came, last, layer_out, grad_tokens = tie(*came, last, layer_out, grad_tokens)
    both = join(came)
    hidden = inner_weight.shape[1]
    counts = (groups, members // 2)
    mine = [index.astype(jnp.int32) for _, index, _ in stages_of]
    came = lax.ppermute(both, AXES, across)
    sums = unpack(jnp.stack(mine), both, counts, shares, hidden)
    grad_tokens = put(grad_tokens, last.astype(F32), far)
    came, grad_tokens, *sums = tie(came, grad_tokens, *sums)
    theirs = jnp.stack([1 - mine[0], *mine[1:]])
    *sums, vectors = unpack(theirs, came, counts, shares, hidden, sums)
    return (
        layer_out,
        grad_tokens,
        *sums[:5],
        vectors[5 : 5 + hidden // width].reshape(hidden),
        sums[5],
        vectors[4],
        vectors[0],
        vectors[1],
        vectors[2],
        vectors[3],
    )


def solution(mesh):
    return jax.shard_map(
        gathered_plan if one_chip_each(mesh) else spread_plan,
        mesh=mesh,
        in_specs=(
            P("grp", "ctx", None),
            P("grp"),
            P("grp", "ctx", None),
            P(),
            P(),
            P(),
            P(),
            P(),
            P(),
            P(),
            P(),
            P(),
            P(),
            P(),
            P(),
        ),
        out_specs=(
            P("grp", "ctx", None),
            P("grp", "ctx", None),
            P(),
            P(),
            P(),
            P(),
            P(),
            P(),
            P(),
            P(),
            P(),
            P(),
            P(),
            P(),
        ),
        check_vma=False,
    )
```

```python
from functools import partial

import jax
import jax.numpy as jnp
from jax import lax
from jax.experimental import pallas as pl
from jax.experimental.pallas import tpu as pltpu
from jax.sharding import PartitionSpec as P

HEADS = 4
CTX = 4096
QUERIES = 128
NBLK = 4
HD = 128


EPSILON = 1e-05


def product(left, right):
    return jnp.dot(left, right, preferred_element_type=jnp.float32)


def contract_rows(left, right):
    return lax.dot_general(
        left, right, (((0,), (0,)), ((), ())), preferred_element_type=jnp.float32
    )


def contract_last(left, right):
    return lax.dot_general(
        left, right, (((1,), (1,)), ((), ())), preferred_element_type=jnp.float32
    )


def norm_forward(values, gain, shift):
    center = values - jnp.mean(values, axis=-1, keepdims=True)
    inverse = lax.rsqrt(jnp.mean(center * center, axis=-1, keepdims=True) + EPSILON)
    normed = center * inverse
    return (normed * gain + shift, normed, inverse)


def norm_backward(upstream, normed, inverse, gain):
    scaled = upstream * gain
    plain_mean = jnp.mean(scaled, axis=-1, keepdims=True)
    cross_mean = jnp.mean(scaled * normed, axis=-1, keepdims=True)
    value_grad = inverse * (scaled - plain_mean - normed * cross_mean)
    return (value_grad, jnp.sum(upstream * normed, axis=0), jnp.sum(upstream, axis=0))


def spread_plan(
    tokens,
    query_counts,
    cotangent,
    query_weight,
    key_weight,
    value_weight,
    output_weight,
    inner_weight,
    inner_bias,
    outer_weight,
    outer_bias,
    first_gain,
    first_shift,
    second_gain,
    second_shift,
):
    member = lax.axis_index("ctx")
    ctx_count = lax.axis_size("ctx")
    context_dev = CTX // ctx_count
    query_dev = QUERIES // ctx_count
    nb_dev = tokens.shape[0]
    rows_dev = tokens.shape[1]
    width = tokens.shape[2]
    heads_count = HEADS
    head_width = HD
    block_count = nb_dev // NBLK
    scale = head_width ** (-0.5)
    total_rows = nb_dev * rows_dev
    tokens_flat = tokens.reshape(total_rows, width)
    context_rows = tokens[:, :context_dev]
    context_flat = context_rows.reshape(nb_dev * context_dev, width)
    queries = (
        product(tokens_flat, query_weight).astype(jnp.bfloat16).reshape(nb_dev, rows_dev, width)
    )
    keys_own = (
        product(context_flat, key_weight).astype(jnp.bfloat16).reshape(nb_dev, context_dev, width)
    )
    values_own = (
        product(context_flat, value_weight).astype(jnp.bfloat16).reshape(nb_dev, context_dev, width)
    )
    sources = (keys_own, values_own)

    def to_blocks(array):
        return array.reshape((block_count, NBLK) + array.shape[1:])

    def fetch(source):
        keys_mine, values_mine = source
        keys_flat, values_flat = (
            lax.all_gather(keys_mine, "ctx", axis=1, tiled=True),
            lax.all_gather(values_mine, "ctx", axis=1, tiled=True),
        )
        return (keys_flat, values_flat, keys_mine, values_mine)

    def split_heads(array):
        return array.reshape(array.shape[0], array.shape[1], heads_count, head_width)

    def attend(carry, operands):
        queries_blk, source = operands
        keys_flat, values_flat, keys_mine, values_mine = fetch(source)
        query_heads = split_heads(queries_blk)
        scores = (
            jnp.einsum(
                "nrhd,nkhd->nhrk",
                query_heads,
                split_heads(keys_flat),
                preferred_element_type=jnp.float32,
            )
            * scale
        )
        log_total = jax.nn.logsumexp(scores, axis=-1, keepdims=True)
        soft_low = jnp.exp(scores - log_total).astype(jnp.bfloat16)
        mixed = jnp.einsum(
            "nhrk,nkhd->nrhd",
            soft_low,
            split_heads(values_flat),
            preferred_element_type=jnp.float32,
        )
        attended_blk = mixed.reshape(NBLK, rows_dev, width).astype(jnp.bfloat16)
        return (carry, (attended_blk, log_total[..., 0]))

    zero = jnp.zeros((), jnp.float32)
    _, (attended_b, lse_b) = lax.scan(
        attend, zero, (to_blocks(queries), jax.tree.map(to_blocks, sources))
    )
    attended_flat = attended_b.reshape(total_rows, width)
    slot_local = jnp.arange(rows_dev, dtype=jnp.int32) - context_dev
    slot_global = member * query_dev + slot_local
    live_rows = jnp.logical_or(
        slot_local[None, :] < 0, slot_global[None, :] < query_counts[:, None]
    )
    live_flat = live_rows.astype(jnp.float32).reshape(total_rows, 1)
    inner_bias_f = inner_bias.astype(jnp.float32)
    outer_bias_f = outer_bias.astype(jnp.float32)
    first_gain_f = first_gain.astype(jnp.float32)
    second_gain_f = second_gain.astype(jnp.float32)
    first_sum = tokens_flat.astype(jnp.float32) + product(attended_flat, output_weight)
    hidden, normed_one, inverse_one = norm_forward(
        first_sum, first_gain_f, first_shift.astype(jnp.float32)
    )
    hidden_low = hidden.astype(jnp.bfloat16)
    inner = product(hidden_low, inner_weight) + inner_bias_f
    gelu_value, gelu_back = jax.vjp(partial(jax.nn.gelu, approximate=False), inner)
    activated = gelu_value.astype(jnp.bfloat16)
    second_sum = hidden + product(activated, outer_weight) + outer_bias_f
    result, normed_two, inverse_two = norm_forward(
        second_sum, second_gain_f, second_shift.astype(jnp.float32)
    )
    layer_out = (result * live_flat).astype(jnp.bfloat16).reshape(nb_dev, rows_dev, width)
    upstream = cotangent.reshape(total_rows, width).astype(jnp.float32) * live_flat
    second_grad, grad_second_gain, grad_second_shift = norm_backward(
        upstream, normed_two, inverse_two, second_gain_f
    )
    outer_grad = second_grad.astype(jnp.bfloat16)
    grad_outer = contract_rows(activated, outer_grad)
    grad_outer_bias = jnp.sum(outer_grad.astype(jnp.float32), axis=0)
    inner_grad = gelu_back(contract_last(outer_grad, outer_weight))[0].astype(jnp.bfloat16)
    grad_inner = contract_rows(hidden_low, inner_grad)
    grad_inner_bias = jnp.sum(inner_grad.astype(jnp.float32), axis=0)
    hidden_grad = second_grad + contract_last(inner_grad, inner_weight)
    first_grad, grad_first_gain, grad_first_shift = norm_backward(
        hidden_grad, normed_one, inverse_one, first_gain_f
    )
    branch_grad = first_grad.astype(jnp.bfloat16)
    grad_output = contract_rows(attended_flat, branch_grad)
    attended_grad = (
        contract_last(branch_grad, output_weight)
        .astype(jnp.bfloat16)
        .reshape(nb_dev, rows_dev, width)
    )

    def attend_back(carry, operands):
        queries_blk, grads_blk, lse_blk, source = operands
        keys_flat, values_flat, keys_mine, values_mine = fetch(source)
        query_heads = split_heads(queries_blk)
        grad_heads = split_heads(grads_blk)
        key_heads = split_heads(keys_flat)
        value_heads = split_heads(values_flat)
        scores = (
            jnp.einsum(
                "nrhd,nkhd->nhrk", query_heads, key_heads, preferred_element_type=jnp.float32
            )
            * scale
        )
        soft = jnp.exp(scores - lse_blk[..., None])
        soft_grad = jnp.einsum(
            "nrhd,nkhd->nhrk", grad_heads, value_heads, preferred_element_type=jnp.float32
        )
        row_delta = jnp.sum(soft * soft_grad, axis=-1)
        score_grad = (soft * (soft_grad - row_delta[..., None])).astype(jnp.bfloat16)
        query_grad = (
            jnp.einsum("nhrk,nkhd->nrhd", score_grad, key_heads, preferred_element_type=jnp.float32)
            * scale
        )
        query_grad = query_grad.reshape(NBLK, rows_dev, width).astype(jnp.bfloat16)
        soft_low = soft.astype(jnp.bfloat16)
        key_part = (
            jnp.einsum(
                "nhrk,nrhd->nkhd", score_grad, query_heads, preferred_element_type=jnp.float32
            )
            * scale
        )
        value_part = jnp.einsum(
            "nhrk,nrhd->nkhd", soft_low, grad_heads, preferred_element_type=jnp.float32
        )
        key_sum, value_sum = (
            lax.psum_scatter(
                key_part.reshape(NBLK, -1, width), "ctx", scatter_dimension=1, tiled=True
            ),
            lax.psum_scatter(
                value_part.reshape(NBLK, -1, width), "ctx", scatter_dimension=1, tiled=True
            ),
        )
        key_grad = key_sum.astype(jnp.bfloat16)
        value_grad = value_sum.astype(jnp.bfloat16)
        return (carry, (query_grad, key_grad, value_grad))

    _, (query_grad_b, key_grad_b, value_grad_b) = lax.scan(
        attend_back,
        zero,
        (to_blocks(queries), to_blocks(attended_grad), lse_b, jax.tree.map(to_blocks, sources)),
    )
    query_grad = query_grad_b.reshape(total_rows, width)
    key_grad = key_grad_b.reshape(nb_dev * context_dev, width)
    value_grad = value_grad_b.reshape(nb_dev * context_dev, width)
    grad_query = contract_rows(tokens_flat, query_grad)
    grad_key = contract_rows(context_flat, key_grad)
    grad_value = contract_rows(context_flat, value_grad)
    token_grad = (first_grad + contract_last(query_grad, query_weight)).reshape(
        nb_dev, rows_dev, width
    )
    context_back = (
        contract_last(key_grad, key_weight) + contract_last(value_grad, value_weight)
    ).reshape(nb_dev, context_dev, width)
    grad_tokens = jnp.concatenate(
        [token_grad[:, :context_dev] + context_back, token_grad[:, context_dev:]], axis=1
    )
    finals = lax.psum(
        (
            grad_query,
            grad_key,
            grad_value,
            grad_output,
            grad_inner,
            grad_inner_bias,
            grad_outer,
            grad_outer_bias,
            grad_first_gain,
            grad_first_shift,
            grad_second_gain,
            grad_second_shift,
        ),
        ("grp", "ctx"),
    )
    return (layer_out, grad_tokens) + tuple(finals)


BF16, F32 = jnp.bfloat16, jnp.float32
MIB = 2**20
AXES = ("grp", "ctx")
LANES = 128
VECTORS = 16
ROWS_STEP = 528


def one_chip_each(mesh):
    return mesh.shape["grp"] % 2 == 0 and mesh.shape["ctx"] == 2 * NBLK


def dot(left, right, over_left, over_right):
    return lax.dot_general(
        left, right, (((over_left,), (over_right,)), ((), ())), preferred_element_type=F32
    )


def kernel_call(body, grid, ins, outs, scratch, flops, moved, *operands, exps=0, into=()):
    given = len(ins)

    def run(*refs):
        body(*refs[:given], *refs[given + len(into) :])

    return pl.pallas_call(
        run,
        grid=grid,
        in_specs=[
            pl.BlockSpec(memory_space=index) if shape is None else pl.BlockSpec(shape, index)
            for shape, index in ins
        ]
        + [pl.BlockSpec(memory_space=pl.ANY)] * len(into),
        out_specs=[
            pl.BlockSpec(memory_space=index) if shape is None else pl.BlockSpec(shape, index)
            for shape, index, _, _ in outs
        ],
        out_shape=[jax.ShapeDtypeStruct(shape, kind) for _, _, shape, kind in outs],
        scratch_shapes=scratch,
        input_output_aliases={given + j: j for j in range(len(into))},
        cost_estimate=pl.CostEstimate(flops=flops, bytes_accessed=moved, transcendentals=exps),
        compiler_params=pltpu.CompilerParams(vmem_limit_bytes=60 * MIB),
    )(*operands, *into)


def project_kernel(context, scale, with_own, *refs):
    if with_own:
        own, wq, refs = refs[0], refs[1], refs[2:]
        rows = own[...]
    others = len(refs) - 6 if with_own else len(refs) - 4
    other_refs, (wk, wv), refs = refs[:others], refs[others : others + 2], refs[others + 2 :]
    k_out, v_out = refs[:2]
    sides = []
    if with_own:
        q_out, x_out = refs[2:]
        x_out[0] = rows
        queries = (dot(rows, wq[...], 1, 0) * scale).astype(BF16)
        for h in range(HEADS):
            q_out[h] = queries[:, h * HD : (h + 1) * HD]
        sides.append(rows[:context])
    sides += [ref[:context] for ref in other_refs]
    for side, keys_of in enumerate(sides):
        keys = dot(keys_of, wk[...], 1, 0).astype(BF16)
        values = dot(keys_of, wv[...], 1, 0).astype(BF16)
        for h in range(HEADS):
            k_out[h, side, 0] = keys[:, h * HD : (h + 1) * HD]
            v_out[h, side, 0] = values[:, h * HD : (h + 1) * HD]


def project(own, other, place, blocks, context, kinds, scale, into):
    given = [array for array in (own, other) if array is not None]
    rows, width = given[0].shape
    fixed = lambda b: (0, 0)
    whole = ((width, width), fixed)
    sides = len(given)
    key_spec = (
        (HEADS, sides, 1, context, HD),
        lambda b: (0, int(own is None), place, 0, 0),
        (HEADS, 2, blocks, context, HD),
        BF16,
    )
    row_specs = [
        ((HEADS, rows, HD), lambda b: (0, place, 0), (HEADS, blocks * rows, HD), BF16),
        ((1, rows, width), lambda b: (place, 0, 0), (blocks, rows, width), BF16),
    ]
    row_in = [((rows, width), fixed)]
    with_own = own is not None
    wq, wk, wv = kinds
    return kernel_call(
        partial(project_kernel, context, scale, with_own),
        (1,),
        (row_in + [whole]) * with_own + row_in * (other is not None) + [whole] * 2,
        [key_spec] * 2 + row_specs * with_own,
        [],
        2 * width * width * (rows + 4 * context),
        4 * width * (rows + 3 * context),
        *([own, wq] if with_own else []),
        *([other] if other is not None else []),
        wk,
        wv,
        into=into,
    )


def forward_kernel(sets, steps, row_blocks, chunk, q_ref, *refs):
    k_refs, v_refs, refs = refs[:sets], refs[sets : 2 * sets], refs[2 * sets :]
    p_ref, o_ref, sum_ref, s_even, s_odd, top_even, top_odd, v_wide = refs
    t = pl.program_id(0)
    rows, hd = q_ref.shape[-2:]
    keys = p_ref.shape[-1]

    @pl.when(t == 0)
    def _():
        v_wide[:, hd:] = jnp.ones((keys, hd), BF16)

    @pl.when((t > 0) & (lax.rem(t - 1, row_blocks) == 0))
    def _():
        start = 0
        for v_ref in v_refs:
            v_wide[start : start + v_ref.shape[1], :hd] = v_ref[0]
            start += v_ref.shape[1]

    places = []
    for k_ref in k_refs:
        places += [(k_ref, slice(c, c + chunk)) for c in range(0, k_ref.shape[1], chunk)]

    def body(score, weigh, s_now, s_before, top_now, top_before):
        if score:
            q = q_ref[0]
            high = None
        if weigh:
            peak = jnp.max(top_before[...], axis=-1, keepdims=True)
            total = jnp.zeros((rows, 2 * hd), F32)
        for c, (k_ref, within) in enumerate(places):
            at = slice(c * chunk, (c + 1) * chunk)
            if score:
                scores = dot(q, k_ref[0, within, :], 1, 1)
                s_now[:, at] = scores
                for j in range(chunk // LANES):
                    part = scores[:, j * LANES : (j + 1) * LANES]
                    high = part if high is None else jnp.maximum(high, part)
            if weigh:
                soft = jnp.exp2(s_before[:, at] - peak).astype(BF16)
                p_ref[0, :, at] = soft
                total = total + dot(soft, v_wide[at, :], 1, 0)
        if score:
            top_now[...] = high
        if weigh:
            o_ref[...] = total[:, :hd]
            sum_ref[0] = total[:, hd:]

    even = (s_even, s_odd, top_even, top_odd)
    odd = (s_odd, s_even, top_odd, top_even)
    inside = (t > 0) & (t < steps)
    pl.when(inside & (lax.rem(t, 2) == 0))(lambda: body(True, True, *even))
    pl.when(inside & (lax.rem(t, 2) == 1))(lambda: body(True, True, *odd))
    pl.when(t == 0)(lambda: body(True, False, *even))
    pl.when(t == steps)(lambda: body(False, True, *(odd if steps % 2 else even)))


def attention_forward(q, ks, vs, row_blocks, chunk=512):
    heads, total, hd = q.shape
    keys = sum(k.shape[1] for k in ks)
    rows = total // row_blocks
    steps = heads * row_blocks
    ahead = lambda t: jnp.minimum(t, steps - 1)
    behind = lambda t: jnp.maximum(t - 1, 0)
    by_row = lambda t: (behind(t) // row_blocks, behind(t) % row_blocks, 0)
    per_row = ((1, rows, hd), by_row, (heads, total, hd), F32)
    return kernel_call(
        partial(forward_kernel, len(ks), steps, row_blocks, chunk),
        (steps + 1,),
        [((1, rows, hd), lambda t: (ahead(t) // row_blocks, ahead(t) % row_blocks, 0))]
        + [((1, k.shape[1], hd), lambda t: (ahead(t) // row_blocks, 0, 0)) for k in ks]
        + [((1, v.shape[1], hd), lambda t: (behind(t) // row_blocks, 0, 0)) for v in vs],
        [
            ((1, rows, keys), by_row, (heads, total, keys), BF16),
            (
                (rows, hd),
                lambda t: (behind(t) % row_blocks, behind(t) // row_blocks),
                (total, heads * hd),
                F32,
            ),
            per_row,
        ],
        [
            pltpu.VMEM((rows, keys), F32),
            pltpu.VMEM((rows, keys), F32),
            pltpu.VMEM((rows, LANES), F32),
            pltpu.VMEM((rows, LANES), F32),
            pltpu.VMEM((keys, 2 * hd), BF16),
        ],
        8 * heads * total * keys * hd,
        2 * heads * total * keys,
        q,
        *ks,
        *vs,
        exps=heads * total * keys,
    )


def gelu_pair(inner):
    size = jnp.abs(inner) * (0.5**0.5)
    rate = 1.0 / (1.0 + 0.3275911 * size)
    bell = jnp.exp(-(size * size))
    tail = rate * (
        0.254829592
        + rate * (-0.284496736 + rate * (1.421413741 + rate * (-1.453152027 + rate * 1.061405429)))
    )
    tail = 0.5 * tail * bell
    below = jnp.where(inner < 0, tail, 1.0 - tail)
    return inner * below, below + inner * bell * 0.3989422804014327


def dense_kernel(
    blocks, steps, bit_ref, x_ref, o_ref, total_ref, wo, w1, b1, w2, b2, g1, s1, g2, s2, *refs
):
    cot_refs, refs = refs[:blocks], refs[blocks:]
    out_refs, refs = refs[:blocks], refs[blocks:]
    first_ref, grad_ref, delta_ref, keep_ref, send_ref = refs[:5]
    sums, sending, cot, out, arrived, left = refs[5:]
    t = pl.program_id(0)
    width, hidden_width = w1.shape
    rows, half = x_ref.shape[0], (width + 2 * hidden_width) // 2
    vector_rows = sums.shape[0] - 2 * half
    block = cot.shape[0] // blocks
    load = [
        pltpu.make_async_copy(ref, cot.at[pl.ds(j * block, block)], arrived.at[j])
        for j, ref in enumerate(cot_refs)
    ]
    store = [
        pltpu.make_async_copy(out.at[pl.ds(j * block, block)], ref, left.at[j])
        for j, ref in enumerate(out_refs)
    ]

    @pl.when(t == 0)
    def _():
        for copy in load:
            copy.start()
        sums[...] = jnp.zeros_like(sums)

    for j, copy in enumerate(load):
        pl.when(t == j * block // rows)(copy.wait)
    here = pl.ds(pl.multiple_of(t * rows, 16), rows)
    gain_one, gain_two = g1[...].astype(F32), g2[...].astype(F32)
    inverses = [1.0 / total_ref[h] for h in range(HEADS)]
    attended = jnp.concatenate(
        [o_ref[:, h * HD : (h + 1) * HD] * inverses[h] for h in range(HEADS)], axis=1
    )
    attended_low = attended.astype(BF16)
    first_sum = x_ref[...].astype(F32) + dot(attended_low, wo[...], 1, 0)
    hidden, normed_one, inverse_one = norm_forward(first_sum, gain_one, s1[...].astype(F32))
    hidden_low = hidden.astype(BF16)
    inner = dot(hidden_low, w1[...], 1, 0) + b1[...].astype(F32)
    activated, slope = gelu_pair(inner)
    activated = activated.astype(BF16)
    second_sum = hidden + dot(activated, w2[...], 1, 0) + b2[...].astype(F32)
    result, normed_two, inverse_two = norm_forward(second_sum, gain_two, s2[...].astype(F32))
    out[here, :] = result.astype(BF16)
    for j, copy in enumerate(store):
        pl.when(t == ((j + 1) * block - 1) // rows)(copy.start)
    upstream = cot[here, :].astype(F32)
    second_grad, gain_two_sum, shift_two_sum = norm_backward(
        upstream, normed_two, inverse_two, gain_two
    )
    outer_grad = second_grad.astype(BF16)
    at = width + hidden_width
    sums[at : at + hidden_width] += dot(activated, outer_grad, 0, 0)
    inner_grad = (dot(outer_grad, w2[...], 1, 1) * slope).astype(BF16)
    inner_sums = dot(hidden_low, inner_grad, 0, 0)
    for j in range(0, hidden_width, width):
        sums[width + j : 2 * width + j] += inner_sums[:, j : j + width]
    hidden_grad = second_grad + dot(inner_grad, w1[...], 1, 1)
    first_grad, gain_one_sum, shift_one_sum = norm_backward(
        hidden_grad, normed_one, inverse_one, gain_one
    )
    branch_grad = first_grad.astype(BF16)
    first_ref[...] = branch_grad
    sums[:width] += dot(attended_low, branch_grad, 0, 0)
    attended_grad = dot(branch_grad, wo[...], 1, 1)
    for h in range(HEADS):
        at = slice(h * HD, (h + 1) * HD)
        scaled = (attended_grad[:, at] * inverses[h]).astype(BF16)
        grad_ref[h] = scaled
        delta = jnp.sum(scaled.astype(F32) * attended[:, at], axis=-1, keepdims=True)
        delta_ref[h] = jnp.broadcast_to(delta, delta_ref.shape[1:])
    inner_sum = jnp.sum(inner_grad.astype(F32), axis=0)
    vectors = [
        gain_one_sum,
        shift_one_sum,
        gain_two_sum,
        shift_two_sum,
        jnp.sum(outer_grad.astype(F32), axis=0),
    ]
    vectors += [inner_sum[j : j + width] for j in range(0, hidden_width, width)]
    at = width + 2 * hidden_width
    for j, part in enumerate(vectors):
        sums[at + j : at + j + 1, :] += part[None, :]

    @pl.when(t == steps - 1)
    def _():
        bit = bit_ref[0]
        keep = pltpu.make_async_copy(
            sums.at[pl.ds(pl.multiple_of(bit * half, 16), half)],
            keep_ref.at[pl.ds(0, half)],
            arrived.at[0],
        )
        keep_vectors = pltpu.make_async_copy(
            sums.at[pl.ds(2 * half, vector_rows)],
            keep_ref.at[pl.ds(half, vector_rows)],
            arrived.at[1],
        )
        sending[:half] = sums[pl.ds(pl.multiple_of((1 - bit) * half, 16), half)].astype(BF16)
        sending[half:] = sums[2 * half :].astype(BF16)
        send = pltpu.make_async_copy(sending, send_ref, arrived.at[2])
        for copy in (keep, keep_vectors, send):
            copy.start()
        for copy in (*store, keep, keep_vectors, send):
            copy.wait()


def dense(bit, x, cots, attended, total_of, weights, steps=3):
    blocks, block, width = x.shape
    total = blocks * block
    rows = total // steps
    hidden = weights[1].shape[1]
    by_row = ((rows, width), lambda t: (t, 0))
    by_head = ((HEADS, rows, HD), lambda t: (0, t, 0))
    half = width // 2 + hidden
    *out, first_grad, grads, delta, keep, send = kernel_call(
        partial(dense_kernel, blocks, steps),
        (steps,),
        [(None, pltpu.SMEM), by_row, by_row, by_head]
        + [(w.shape, lambda t: (0, 0)) for w in weights]
        + [(None, pl.ANY)] * blocks,
        [(None, pl.ANY, (block, width), BF16)] * blocks
        + [
            (*by_row, (total, width), BF16),
            (*by_head, (HEADS, total, HD), BF16),
            (*by_head, (HEADS, total, HD), F32),
            (None, pl.ANY, (half + VECTORS, width), F32),
            (None, pl.ANY, (half + VECTORS, width), BF16),
        ],
        [
            pltpu.VMEM((2 * half + VECTORS, width), F32),
            pltpu.VMEM((half + VECTORS, width), BF16),
            pltpu.VMEM((total, width), BF16),
            pltpu.VMEM((total, width), BF16),
            pltpu.SemaphoreType.DMA((blocks,)),
            pltpu.SemaphoreType.DMA((blocks,)),
        ],
        6 * total * width * (width + 2 * hidden),
        32 * total * width + 8 * width * (width + 2 * hidden),
        bit,
        x.reshape(total, width),
        attended,
        total_of,
        *weights,
        *cots,
    )
    return out, first_grad, grads, delta, keep, send


def backward_kernel(scale_k, scale_q, carried, q_ref, g_ref, d_ref, p_ref, k_ref, v_ref, *refs):
    if carried:
        before, refs = refs[0], refs[1:]
    kv_ref, dq_ref, dq_sum, ds, q_t, g_t = refs
    c = pl.program_id(1)

    @pl.when(c == 0)
    def _():
        q_t[...] = q_ref[0].T
        g_t[...] = g_ref[0].T
        dq_sum[...] = before[0] if carried else jnp.zeros_like(dq_sum)

    keys, values = k_ref[0], v_ref[0]
    chunk = keys.shape[0]
    for start in range(0, p_ref.shape[1], ROWS_STEP):
        at = slice(start, start + ROWS_STEP)
        soft_grad = dot(g_ref[0, at, :], values, 1, 1)
        delta = jnp.concatenate([d_ref[0, at, :]] * (chunk // LANES), axis=1)
        score_grad = (p_ref[0, at, :].astype(F32) * (soft_grad - delta)).astype(BF16)
        ds[at, :] = score_grad
        dq_sum[at, :] += dot(score_grad, keys, 1, 0)
    dv = dot(g_t[...], p_ref[0], 1, 0).T
    dk = dot(q_t[...], ds[...], 1, 0).T * scale_k
    kv_ref[0, 0] = dk.astype(BF16)
    kv_ref[1, 0] = dv.astype(BF16)

    @pl.when(c == pl.num_programs(1) - 1)
    def _():
        dq_ref[0] = (dq_sum[...] * scale_q).astype(dq_ref.dtype)


def attention_backward(q, g, d, p, k, v, scale_k, scale_q, chunk, first, chunks, before=None):
    heads, total, hd = q.shape
    row = lambda h, c: (h, 0, 0)
    key = lambda h, c: (h, c + first, 0)
    by_row = ((1, total, hd), row)
    carried = before is not None
    return kernel_call(
        partial(backward_kernel, scale_k, scale_q, carried),
        (heads, chunks),
        [
            by_row,
            by_row,
            by_row,
            ((1, total, chunk), lambda h, c: (h, 0, c + first)),
            ((1, chunk, hd), key),
            ((1, chunk, hd), key),
        ]
        + [by_row] * carried,
        [
            ((2, 1, chunk, hd), lambda h, c: (0, h, c, 0), (2, heads, chunks * chunk, hd), BF16),
            (*by_row, (heads, total, hd), BF16 if carried else F32),
        ],
        [
            pltpu.VMEM((total, hd), F32),
            pltpu.VMEM((total, chunk), BF16),
            pltpu.VMEM((hd, total), BF16),
            pltpu.VMEM((hd, total), BF16),
        ],
        12 * heads * total * chunk * chunks * hd,
        2 * heads * total * chunk * chunks,
        q,
        g,
        d,
        p,
        k,
        v,
        *[before] * carried,
    )


def side_by_side(parts):
    return jnp.concatenate([part.astype(BF16) for part in parts], axis=1)


def weigh_kernel(
    bit_ref, x_ref, query_ref, own_ref, other_ref, keep_ref, send_ref, sums, sending, left
):
    s = pl.program_id(0)
    blocks, rows, width = x_ref.shape
    context = own_ref.shape[2] // blocks
    per = query_ref.shape[0]
    columns = per * HD
    x = x_ref[...].reshape(blocks * rows, width)
    above = x_ref[:, :context].reshape(blocks * context, width)
    three = [dot(x, side_by_side([query_ref[h] for h in range(per)]), 0, 0)]
    for j in range(2):
        whole = side_by_side(
            [own_ref[j, h].astype(F32) + other_ref[j, h].astype(F32) for h in range(per)]
        )
        three.append(dot(above, whole, 0, 0))
    steps = width // columns
    for j in range(steps):

        @pl.when(s == j)
        def _(j=j):
            for i, part in enumerate(three):
                sums[i * width : (i + 1) * width, j * columns : (j + 1) * columns] = part

    @pl.when(s == steps - 1)
    def _():
        bit = bit_ref[0]
        half = sending.shape[0]
        keep = pltpu.make_async_copy(
            sums.at[pl.ds(pl.multiple_of(bit * half, 16), half)], keep_ref, left.at[0]
        )
        keep.start()
        sending[...] = sums[pl.ds(pl.multiple_of((1 - bit) * half, 16), half)].astype(BF16)
        send = pltpu.make_async_copy(sending, send_ref, left.at[1])
        send.start()
        keep.wait()
        send.wait()


def weigh(bit, x, query_grad, own, other, per=2):
    blocks, rows, width = x.shape
    keys = own.shape[2]
    side = ((2, per, keys, HD), lambda s: (0, s, 0, 0))
    half = 3 * width // 2
    return kernel_call(
        weigh_kernel,
        (HEADS // per,),
        [
            (None, pltpu.SMEM),
            (x.shape, lambda s: (0, 0, 0)),
            ((per, blocks * rows, HD), lambda s: (s, 0, 0)),
            side,
            side,
        ],
        [(None, pl.ANY, (half, width), F32), (None, pl.ANY, (half, width), BF16)],
        [
            pltpu.VMEM((3 * width, width), F32),
            pltpu.VMEM((half, width), BF16),
            pltpu.SemaphoreType.DMA((2,)),
        ],
        2 * width * width * (blocks * rows + 2 * keys),
        2 * width * (2 * blocks * rows + 4 * keys),
        bit,
        x,
        query_grad,
        own,
        other,
    )


def finish_kernel(context, count, first_ref, query_ref, own, other, wq, wk, wv, *refs):
    token_refs, (tokens, left) = refs[:count], refs[count:]
    b = pl.program_id(0)
    query_grad = side_by_side([query_ref[h, 0] for h in range(HEADS)])
    key_grad, value_grad = (
        side_by_side(
            [own[j, h, 0].astype(F32) + other[j, h, 0].astype(F32) for h in range(HEADS)]
        )
        for j in range(2)
    )
    base = first_ref[0].astype(F32) + dot(query_grad, wq[...], 1, 1)
    back = dot(key_grad, wk[...], 1, 1) + dot(value_grad, wv[...], 1, 1)
    tokens[b, :context] = (base[:context] + back).astype(BF16)
    tokens[b, context:] = base[context:].astype(BF16)
    store = [
        pltpu.make_async_copy(tokens.at[j], ref, left.at[j]) for j, ref in enumerate(token_refs)
    ]
    for j, copy in enumerate(store):
        pl.when(b == j)(copy.start)

    @pl.when(b == count - 1)
    def _():
        for copy in store:
            copy.wait()


def finish(ahead, first_grad, own, other, query_grad, kinds, blocks):
    first, last = ahead[0], ahead[-1]
    count = len(ahead)
    at = lambda b: first + b * (last - first)
    total, width = first_grad.shape
    rows = total // blocks
    context = own.shape[2] // blocks
    side = ((2, HEADS, 1, context, HD), lambda b: (0, 0, at(b), 0, 0))
    return kernel_call(
        partial(finish_kernel, context, count),
        (count,),
        [
            ((1, rows, width), lambda b: (at(b), 0, 0)),
            ((HEADS, 1, rows, HD), lambda b: (0, at(b), 0, 0)),
            side,
            side,
        ]
        + [((width, width), lambda b: (0, 0))] * 3,
        [(None, pl.ANY, (rows, width), BF16)] * count,
        [pltpu.VMEM((count, rows, width), BF16), pltpu.SemaphoreType.DMA((count,))],
        2 * count * width * width * (rows + 2 * context),
        6 * count * width * (rows + 2 * context),
        first_grad.reshape(blocks, rows, width),
        query_grad.reshape(HEADS, blocks, rows, HD),
        own.reshape(2, HEADS, blocks, context, HD),
        other.reshape(2, HEADS, blocks, context, HD),
        *kinds,
    )


def unpack_kernel(counts, shares, place_ref, half_ref, *refs):
    outs, (early, late, left) = refs[:6], refs[6:]
    grad_query, grad_key, grad_value, grad_output, grad_inner, grad_outer = outs
    first, second = shares
    across, along = counts
    share = first + second
    for s in range(across):
        for u in range(along):
            at = (s * along + u) * share
            number = (place_ref[1] ^ s) * along + (place_ref[2] ^ u)
            early[pl.ds(pl.multiple_of(number * first, 16), first)] = half_ref[
                at : at + first
            ].astype(F32)
            late[pl.ds(pl.multiple_of(number * second, 16), second)] = half_ref[
                at + first : at + share
            ].astype(F32)
    width, hidden = grad_inner.shape

    def copy_out(pieces):
        copies = [
            pltpu.make_async_copy(source.at[pl.ds(start, size)], ref, left.at[j])
            for j, (source, start, size, ref) in enumerate(pieces)
        ]
        for copy in copies:
            copy.start()
        for copy in copies:
            copy.wait()

    late_refs = [grad_query, grad_key, grad_value]
    early_refs = [grad_output]
    early_refs += [grad_inner.at[:, pl.ds(j, width)] for j in range(0, hidden, width)]
    early_refs += [grad_outer.at[pl.ds(j, width)] for j in range(0, hidden, width)]

    def pieces(source, refs, start):
        end = start + source.shape[0]
        for j, ref in enumerate(refs):
            low, high = max(start, j * width), min(end, (j + 1) * width)
            if low < high:
                yield source, low - start, high - low, ref.at[pl.ds(low - j * width, high - low)]

    for core in range(2):

        @pl.when(place_ref[0] == core)
        def _(core=core):
            copy_out(
                [
                    *pieces(late, late_refs, core * late.shape[0]),
                    *pieces(early, early_refs, core * early.shape[0]),
                ]
            )


def unpack(places, half, counts, shares, hidden, into=()):
    width = half.shape[1]
    total = counts[0] * counts[1]
    shapes = [(width, width)] * 4 + [(width, hidden), (hidden, width)]
    return kernel_call(
        partial(unpack_kernel, counts, shares),
        (1,),
        [(None, pltpu.SMEM), (half.shape, lambda b: (0, 0))],
        [(None, pl.ANY, shape, F32) for shape in shapes],
        [
            pltpu.VMEM((total * shares[0], width), F32),
            pltpu.VMEM((total * shares[1], width), F32),
            pltpu.SemaphoreType.DMA((4 + 2 * hidden // width,)),
        ],
        0,
        6 * half.size,
        places,
        half,
        into=into,
    )


def summing(groups, members):
    grp, ctx = lax.axis_index("grp"), lax.axis_index("ctx")
    planes, along = groups // 2, members // 2
    places = [(g, c) for g in range(groups) for c in range(members)]
    number = lambda g, c: g * members + c
    stages = (
        (2, grp % 2, lambda g, c, s: (g ^ s, c)),
        (
            2 * planes,
            grp // 2 * 2 + ctx % 2,
            lambda g, c, s: (g ^ (s // 2 * 2), c ^ (s % 2)),
        ),
        (along, ctx // 2, lambda g, c, s: (g, c ^ (2 * s))),
    )

    def swap(array, move, s):
        return lax.ppermute(
            array, AXES, [(number(g, c), number(*move(g, c, s))) for g, c in places]
        )

    def reduce_pieces(stage, parts, below=0):
        count, index, _ = stage
        rows = parts[0].shape[0] - below
        piece = rows // count

        def take(s):
            at = (index ^ s) * piece
            taken = sum(lax.dynamic_slice_in_dim(part, at, piece).astype(F32) for part in parts)
            if not below:
                return taken
            return jnp.concatenate([taken, sum(part[rows:].astype(F32) for part in parts)])

        return [take(0)] + [take(s).astype(BF16) for s in range(1, count)]

    def reduce_join(stage, own, came):
        return [own, *came]

    def gather_pieces(stage, part):
        return [part.astype(BF16)] * stage[0]

    def gather_join(stage, own, came):
        return jnp.concatenate([own] + came)

    def send(stage, pieces):
        return [swap(piece, stage[2], s) for s, piece in enumerate(pieces) if s]

    return [
        (partial(reduce_pieces, stage), partial(send, stage), partial(reduce_join, stage))
        for stage in stages
    ] + [
        (partial(gather_pieces, stage), partial(send, stage), partial(gather_join, stage))
        for stage in reversed(stages)
    ], stages


def gathered_plan(
    tokens,
    query_counts,
    cotangent,
    query_weight,
    key_weight,
    value_weight,
    output_weight,
    inner_weight,
    inner_bias,
    outer_weight,
    outer_bias,
    first_gain,
    first_shift,
    second_gain,
    second_shift,
):
    blocks, rows, width = tokens.shape
    groups, members = lax.axis_size("grp"), lax.axis_size("ctx")
    member = lax.axis_index("ctx")
    place = member // 2
    context = CTX // members
    slots = QUERIES // members

    far = blocks // 2
    order = [r for r in range(1, blocks) if r != far] + [0, far]

    def route(r, back=False):
        pairs = []
        for g in range(groups):
            for c in range(members):
                to = (g - g % 2 + c % 2) * members + ((c // 2 + r) % blocks) * 2 + g % 2
                pairs.append((to, g * members + c) if back else (g * members + c, to))
        return pairs

    across = [
        (g * members + c, (g ^ 1) * members + c) for g in range(groups) for c in range(members)
    ]
    tie = lambda *arrays: lax.optimization_barrier(arrays)

    def block_of(array, r):
        return lax.dynamic_index_in_dim(array, lax.rem(place + r, blocks), 0, keepdims=False)

    def outward(block, r):
        return lax.ppermute(block, AXES, route(r))

    def homeward(block, r):
        return lax.ppermute(block, AXES, route(r, True))

    def put(whole, block, r):
        return lax.dynamic_update_index_in_dim(whole, block, lax.rem(place + r, blocks), 0)

    slot = member * slots + jnp.arange(rows, dtype=jnp.int32) - context
    live = (jnp.arange(rows) < context)[None, :] | (slot[None, :] < query_counts[:, None])
    live = live[:, :, None]
    masked = jnp.where(live, cotangent, 0).astype(BF16)

    scale = HD**-0.5
    log2e = 1.4426950408889634
    kinds = (query_weight, key_weight, value_weight)
    *own, own_far = [outward(block_of(tokens, r), r) for r in order]
    other = [lax.ppermute(block, AXES, across) for block in own]
    qkvx = ()
    for j in range(blocks - 1):
        qkvx = project(own[j], other[j], j, blocks, context, kinds, scale * log2e, qkvx)
    own_far, *kvqx = tie(own_far, *qkvx)
    other_far = lax.ppermute(own_far, AXES, across)
    *kv, q, x = project(own_far, None, blocks - 1, blocks, context, kinds, scale * log2e, kvqx)
    other_far, *kv = tie(other_far, *kv)
    k, v = project(None, other_far, blocks - 1, blocks, context, kinds, scale * log2e, kv)
    k, v = (array.reshape(HEADS, 2 * blocks * context, HD) for array in (k, v))

    *cots, q = tie(*[block_of(masked, r) for r in order], q)
    cots = [outward(block, r) for block, r in zip(cots, order, strict=True)]
    p, attended, totals = attention_forward(q, [k], [v], blocks)
    *cots, p = tie(*cots, p)

    lifted = lambda vector: vector.reshape(1, -1)
    weights = (
        output_weight,
        inner_weight,
        lifted(inner_bias),
        outer_weight,
        lifted(outer_bias),
        lifted(first_gain),
        lifted(first_shift),
        lifted(second_gain),
        lifted(second_shift),
    )
    bit = lax.rem(lax.axis_index("grp"), 2).astype(jnp.int32).reshape(1)
    out, first_grad, grads, delta, keep, given = dense(bit, x, cots, attended, totals, weights)

    stages, stages_of = summing(groups, members)
    scale_k = 1.0 / log2e
    chunk = blocks * context // 2

    added = lambda parts: sum(part.astype(F32) for part in parts)

    def start(stage, *part):
        pieces_of, send, join = stage
        mine, *pieces = pieces_of(*part)
        return pieces, lambda pieces: send([mine] + pieces), partial(join, mine)

    *out, given, grads = tie(*out, given, grads)
    came = lax.ppermute(given, AXES, across)
    home = [homeward(out[j], r) for j, r in enumerate(order[:-2])]
    kv_other, dq = attention_backward(q, grads, delta, p, k, v, scale_k, 1.0, chunk, 2, 2)
    *home, came, kv_other, grads = tie(*home, came, kv_other, grads)
    pieces, send, early_join = start(stages[1], [keep, came], VECTORS)
    *pieces, kv_other, far_out, grads = tie(*pieces, kv_other, out[-1], grads)
    kv_came = lax.ppermute(kv_other, AXES, across)
    early_came = send(pieces)
    home.append(homeward(far_out, far))
    kv_own, dq = attention_backward(q, grads, delta, p, k, v, scale_k, scale, chunk, 0, 2, dq)
    *early_came, home[-1], kv_came, kv_own = tie(*early_came, home[-1], kv_came, kv_own)

    token_of = lambda places, after: finish(
        places, after, kv_own, kv_came, dq, kinds, blocks
    )
    three = token_of([1], first_grad)[0]
    three, first_grad = tie(three, first_grad)
    three = homeward(three, order[1])
    one, two = token_of([2, 0], first_grad)
    one, two, x = tie(one, two, x)
    keep, given = weigh(bit, x, dq, kv_own, kv_came)
    three, given, first_grad = tie(three, given, first_grad)
    came = lax.ppermute(given, AXES, across)
    last = token_of([3], first_grad)[0]
    came, last = tie(came, last)

    pieces, send, join = start(stages[1], [keep, came])
    *pieces, two = tie(*pieces, two)
    came = send(pieces)
    two = homeward(two, order[0])
    *came, two = tie(*came, two)
    late = added(join(came))
    early = added(early_join(early_came))

    along = members // 2
    shares = ((early.shape[0] - VECTORS) // along, late.shape[0] // along)
    both = jnp.concatenate(
        [
            early[:-VECTORS].reshape(along, shares[0], width),
            late.reshape(along, shares[1], width),
            jnp.broadcast_to(early[-VECTORS:], (along, VECTORS, width)),
        ],
        axis=1,
    ).reshape(-1, width)
    pieces, send, join = start(stages[2], [both])
    *pieces, zero_out = tie(*pieces, out[-2])
    came = send(pieces)
    zero_home = homeward(zero_out, order[-2])
    grad_tokens = jnp.zeros((blocks, rows, width), F32)
    grad_tokens = put(grad_tokens, three.astype(F32), order[1])
    *came, zero_home, grad_tokens, one = tie(*came, zero_home, grad_tokens, one)
    home.insert(blocks - 2, zero_home)
    both = added(join(came))
    both, vectors = both[:-VECTORS], both[-VECTORS:]

    pieces, send, join = start(stages[3], both)
    *home, live, one, pieces[0] = tie(*home, live, one, pieces[0])
    came = send(pieces)
    one = homeward(one, order[2])
    grad_tokens = put(grad_tokens, two.astype(F32), order[0])
    *came, one, grad_tokens = tie(*came, one, grad_tokens)
    both = join(came)

    pieces, send, join = start(stages[4], both)
    *pieces, last = tie(*pieces, last)
    came = send(pieces)
    last = homeward(last, far)
    grad_tokens = put(grad_tokens, one.astype(F32), order[2])
    layer_out = jnp.zeros((blocks, rows, width), BF16)
    for block, r in zip(home, order, strict=True):
        layer_out = put(layer_out, jnp.where(block_of(live, r), block, 0).astype(BF16), r)
    *came, last, layer_out, grad_tokens = tie(*came, last, layer_out, grad_tokens)
    both = join(came)
    hidden = inner_weight.shape[1]
    counts = (groups, members // 2)
    mine = [index.astype(jnp.int32) for _, index, _ in stages_of]
    came = lax.ppermute(both, AXES, across)
    sums = unpack(jnp.stack(mine), both, counts, shares, hidden)
    grad_tokens = put(grad_tokens, last.astype(F32), far)
    came, grad_tokens, *sums = tie(came, grad_tokens, *sums)
    theirs = jnp.stack([1 - mine[0], *mine[1:]])
    sums = unpack(theirs, came, counts, shares, hidden, sums)
    return (
        layer_out,
        grad_tokens,
        *sums[:5],
        vectors[5 : 5 + hidden // width].reshape(hidden),
        sums[5],
        vectors[4],
        vectors[0],
        vectors[1],
        vectors[2],
        vectors[3],
    )


def solution(mesh):
    return jax.shard_map(
        gathered_plan if one_chip_each(mesh) else spread_plan,
        mesh=mesh,
        in_specs=(
            P("grp", "ctx", None),
            P("grp"),
            P("grp", "ctx", None),
            P(),
            P(),
            P(),
            P(),
            P(),
            P(),
            P(),
            P(),
            P(),
            P(),
            P(),
            P(),
        ),
        out_specs=(
            P("grp", "ctx", None),
            P("grp", "ctx", None),
            P(),
            P(),
            P(),
            P(),
            P(),
            P(),
            P(),
            P(),
            P(),
            P(),
            P(),
            P(),
        ),
        check_vma=False,
    )
```

```python
from functools import partial

import jax
import jax.numpy as jnp
from jax import lax
from jax.experimental import pallas as pl
from jax.experimental.pallas import tpu as pltpu
from jax.sharding import PartitionSpec as P

HEADS = 4
CTX = 4096
QUERIES = 128
NBLK = 4
HD = 128


EPSILON = 1e-05


def product(left, right):
    return jnp.dot(left, right, preferred_element_type=jnp.float32)


def contract_rows(left, right):
    return lax.dot_general(
        left, right, (((0,), (0,)), ((), ())), preferred_element_type=jnp.float32
    )


def contract_last(left, right):
    return lax.dot_general(
        left, right, (((1,), (1,)), ((), ())), preferred_element_type=jnp.float32
    )


def norm_forward(values, gain, shift):
    center = values - jnp.mean(values, axis=-1, keepdims=True)
    inverse = lax.rsqrt(jnp.mean(center * center, axis=-1, keepdims=True) + EPSILON)
    normed = center * inverse
    return (normed * gain + shift, normed, inverse)


def norm_backward(upstream, normed, inverse, gain):
    scaled = upstream * gain
    plain_mean = jnp.mean(scaled, axis=-1, keepdims=True)
    cross_mean = jnp.mean(scaled * normed, axis=-1, keepdims=True)
    value_grad = inverse * (scaled - plain_mean - normed * cross_mean)
    return (value_grad, jnp.sum(upstream * normed, axis=0), jnp.sum(upstream, axis=0))


def spread_plan(
    tokens,
    query_counts,
    cotangent,
    query_weight,
    key_weight,
    value_weight,
    output_weight,
    inner_weight,
    inner_bias,
    outer_weight,
    outer_bias,
    first_gain,
    first_shift,
    second_gain,
    second_shift,
):
    member = lax.axis_index("ctx")
    ctx_count = lax.axis_size("ctx")
    context_dev = CTX // ctx_count
    query_dev = QUERIES // ctx_count
    nb_dev = tokens.shape[0]
    rows_dev = tokens.shape[1]
    width = tokens.shape[2]
    heads_count = HEADS
    head_width = HD
    block_count = nb_dev // NBLK
    scale = head_width ** (-0.5)
    total_rows = nb_dev * rows_dev
    tokens_flat = tokens.reshape(total_rows, width)
    context_rows = tokens[:, :context_dev]
    context_flat = context_rows.reshape(nb_dev * context_dev, width)
    queries = (
        product(tokens_flat, query_weight).astype(jnp.bfloat16).reshape(nb_dev, rows_dev, width)
    )
    keys_own = (
        product(context_flat, key_weight).astype(jnp.bfloat16).reshape(nb_dev, context_dev, width)
    )
    values_own = (
        product(context_flat, value_weight).astype(jnp.bfloat16).reshape(nb_dev, context_dev, width)
    )
    sources = (keys_own, values_own)

    def to_blocks(array):
        return array.reshape((block_count, NBLK) + array.shape[1:])

    def fetch(source):
        keys_mine, values_mine = source
        keys_flat, values_flat = (
            lax.all_gather(keys_mine, "ctx", axis=1, tiled=True),
            lax.all_gather(values_mine, "ctx", axis=1, tiled=True),
        )
        return (keys_flat, values_flat, keys_mine, values_mine)

    def split_heads(array):
        return array.reshape(array.shape[0], array.shape[1], heads_count, head_width)

    def attend(carry, operands):
        queries_blk, source = operands
        keys_flat, values_flat, keys_mine, values_mine = fetch(source)
        query_heads = split_heads(queries_blk)
        scores = (
            jnp.einsum(
                "nrhd,nkhd->nhrk",
                query_heads,
                split_heads(keys_flat),
                preferred_element_type=jnp.float32,
            )
            * scale
        )
        log_total = jax.nn.logsumexp(scores, axis=-1, keepdims=True)
        soft_low = jnp.exp(scores - log_total).astype(jnp.bfloat16)
        mixed = jnp.einsum(
            "nhrk,nkhd->nrhd",
            soft_low,
            split_heads(values_flat),
            preferred_element_type=jnp.float32,
        )
        attended_blk = mixed.reshape(NBLK, rows_dev, width).astype(jnp.bfloat16)
        return (carry, (attended_blk, log_total[..., 0]))

    zero = jnp.zeros((), jnp.float32)
    _, (attended_b, lse_b) = lax.scan(
        attend, zero, (to_blocks(queries), jax.tree.map(to_blocks, sources))
    )
    attended_flat = attended_b.reshape(total_rows, width)
    slot_local = jnp.arange(rows_dev, dtype=jnp.int32) - context_dev
    slot_global = member * query_dev + slot_local
    live_rows = jnp.logical_or(
        slot_local[None, :] < 0, slot_global[None, :] < query_counts[:, None]
    )
    live_flat = live_rows.astype(jnp.float32).reshape(total_rows, 1)
    inner_bias_f = inner_bias.astype(jnp.float32)
    outer_bias_f = outer_bias.astype(jnp.float32)
    first_gain_f = first_gain.astype(jnp.float32)
    second_gain_f = second_gain.astype(jnp.float32)
    first_sum = tokens_flat.astype(jnp.float32) + product(attended_flat, output_weight)
    hidden, normed_one, inverse_one = norm_forward(
        first_sum, first_gain_f, first_shift.astype(jnp.float32)
    )
    hidden_low = hidden.astype(jnp.bfloat16)
    inner = product(hidden_low, inner_weight) + inner_bias_f
    gelu_value, gelu_back = jax.vjp(partial(jax.nn.gelu, approximate=False), inner)
    activated = gelu_value.astype(jnp.bfloat16)
    second_sum = hidden + product(activated, outer_weight) + outer_bias_f
    result, normed_two, inverse_two = norm_forward(
        second_sum, second_gain_f, second_shift.astype(jnp.float32)
    )
    layer_out = (result * live_flat).astype(jnp.bfloat16).reshape(nb_dev, rows_dev, width)
    upstream = cotangent.reshape(total_rows, width).astype(jnp.float32) * live_flat
    second_grad, grad_second_gain, grad_second_shift = norm_backward(
        upstream, normed_two, inverse_two, second_gain_f
    )
    outer_grad = second_grad.astype(jnp.bfloat16)
    grad_outer = contract_rows(activated, outer_grad)
    grad_outer_bias = jnp.sum(outer_grad.astype(jnp.float32), axis=0)
    inner_grad = gelu_back(contract_last(outer_grad, outer_weight))[0].astype(jnp.bfloat16)
    grad_inner = contract_rows(hidden_low, inner_grad)
    grad_inner_bias = jnp.sum(inner_grad.astype(jnp.float32), axis=0)
    hidden_grad = second_grad + contract_last(inner_grad, inner_weight)
    first_grad, grad_first_gain, grad_first_shift = norm_backward(
        hidden_grad, normed_one, inverse_one, first_gain_f
    )
    branch_grad = first_grad.astype(jnp.bfloat16)
    grad_output = contract_rows(attended_flat, branch_grad)
    attended_grad = (
        contract_last(branch_grad, output_weight)
        .astype(jnp.bfloat16)
        .reshape(nb_dev, rows_dev, width)
    )

    def attend_back(carry, operands):
        queries_blk, grads_blk, lse_blk, source = operands
        keys_flat, values_flat, keys_mine, values_mine = fetch(source)
        query_heads = split_heads(queries_blk)
        grad_heads = split_heads(grads_blk)
        key_heads = split_heads(keys_flat)
        value_heads = split_heads(values_flat)
        scores = (
            jnp.einsum(
                "nrhd,nkhd->nhrk", query_heads, key_heads, preferred_element_type=jnp.float32
            )
            * scale
        )
        soft = jnp.exp(scores - lse_blk[..., None])
        soft_grad = jnp.einsum(
            "nrhd,nkhd->nhrk", grad_heads, value_heads, preferred_element_type=jnp.float32
        )
        row_delta = jnp.sum(soft * soft_grad, axis=-1)
        score_grad = (soft * (soft_grad - row_delta[..., None])).astype(jnp.bfloat16)
        query_grad = (
            jnp.einsum("nhrk,nkhd->nrhd", score_grad, key_heads, preferred_element_type=jnp.float32)
            * scale
        )
        query_grad = query_grad.reshape(NBLK, rows_dev, width).astype(jnp.bfloat16)
        soft_low = soft.astype(jnp.bfloat16)
        key_part = (
            jnp.einsum(
                "nhrk,nrhd->nkhd", score_grad, query_heads, preferred_element_type=jnp.float32
            )
            * scale
        )
        value_part = jnp.einsum(
            "nhrk,nrhd->nkhd", soft_low, grad_heads, preferred_element_type=jnp.float32
        )
        key_sum, value_sum = (
            lax.psum_scatter(
                key_part.reshape(NBLK, -1, width), "ctx", scatter_dimension=1, tiled=True
            ),
            lax.psum_scatter(
                value_part.reshape(NBLK, -1, width), "ctx", scatter_dimension=1, tiled=True
            ),
        )
        key_grad = key_sum.astype(jnp.bfloat16)
        value_grad = value_sum.astype(jnp.bfloat16)
        return (carry, (query_grad, key_grad, value_grad))

    _, (query_grad_b, key_grad_b, value_grad_b) = lax.scan(
        attend_back,
        zero,
        (to_blocks(queries), to_blocks(attended_grad), lse_b, jax.tree.map(to_blocks, sources)),
    )
    query_grad = query_grad_b.reshape(total_rows, width)
    key_grad = key_grad_b.reshape(nb_dev * context_dev, width)
    value_grad = value_grad_b.reshape(nb_dev * context_dev, width)
    grad_query = contract_rows(tokens_flat, query_grad)
    grad_key = contract_rows(context_flat, key_grad)
    grad_value = contract_rows(context_flat, value_grad)
    token_grad = (first_grad + contract_last(query_grad, query_weight)).reshape(
        nb_dev, rows_dev, width
    )
    context_back = (
        contract_last(key_grad, key_weight) + contract_last(value_grad, value_weight)
    ).reshape(nb_dev, context_dev, width)
    grad_tokens = jnp.concatenate(
        [token_grad[:, :context_dev] + context_back, token_grad[:, context_dev:]], axis=1
    )
    finals = lax.psum(
        (
            grad_query,
            grad_key,
            grad_value,
            grad_output,
            grad_inner,
            grad_inner_bias,
            grad_outer,
            grad_outer_bias,
            grad_first_gain,
            grad_first_shift,
            grad_second_gain,
            grad_second_shift,
        ),
        ("grp", "ctx"),
    )
    return (layer_out, grad_tokens) + tuple(finals)


BF16, F32 = jnp.bfloat16, jnp.float32
MIB = 2**20
AXES = ("grp", "ctx")
LANES = 128
VECTORS = 16
ROWS_STEP = 528


def one_chip_each(mesh):
    return mesh.shape["grp"] % 2 == 0 and mesh.shape["ctx"] == 2 * NBLK


def dot(left, right, over_left, over_right):
    return lax.dot_general(
        left, right, (((over_left,), (over_right,)), ((), ())), preferred_element_type=F32
    )


def kernel_call(body, grid, ins, outs, scratch, flops, moved, *operands, exps=0, into=()):
    given = len(ins)

    def run(*refs):
        body(*refs[:given], *refs[given + len(into) :])

    return pl.pallas_call(
        run,
        grid=grid,
        in_specs=[
            pl.BlockSpec(memory_space=index) if shape is None else pl.BlockSpec(shape, index)
            for shape, index in ins
        ]
        + [pl.BlockSpec(memory_space=pl.ANY)] * len(into),
        out_specs=[
            pl.BlockSpec(memory_space=index) if shape is None else pl.BlockSpec(shape, index)
            for shape, index, _, _ in outs
        ],
        out_shape=[jax.ShapeDtypeStruct(shape, kind) for _, _, shape, kind in outs],
        scratch_shapes=scratch,
        input_output_aliases={given + j: j for j in range(len(into))},
        cost_estimate=pl.CostEstimate(flops=flops, bytes_accessed=moved, transcendentals=exps),
        compiler_params=pltpu.CompilerParams(vmem_limit_bytes=60 * MIB),
    )(*operands, *into)


def project_kernel(context, scale, with_own, *refs):
    if with_own:
        own, wq, refs = refs[0], refs[1], refs[2:]
        rows = own[...]
    others = len(refs) - 6 if with_own else len(refs) - 4
    other_refs, (wk, wv), refs = refs[:others], refs[others : others + 2], refs[others + 2 :]
    k_out, v_out = refs[:2]
    sides = []
    if with_own:
        q_out, x_out = refs[2:]
        x_out[0] = rows
        queries = (dot(rows, wq[...], 1, 0) * scale).astype(BF16)
        for h in range(HEADS):
            q_out[h] = queries[:, h * HD : (h + 1) * HD]
        sides.append(rows[:context])
    sides += [ref[:context] for ref in other_refs]
    for side, keys_of in enumerate(sides):
        keys = dot(keys_of, wk[...], 1, 0).astype(BF16)
        values = dot(keys_of, wv[...], 1, 0).astype(BF16)
        for h in range(HEADS):
            k_out[h, side, 0] = keys[:, h * HD : (h + 1) * HD]
            v_out[h, side, 0] = values[:, h * HD : (h + 1) * HD]


def project(own, other, place, blocks, context, kinds, scale, into):
    given = [array for array in (own, other) if array is not None]
    rows, width = given[0].shape
    fixed = lambda b: (0, 0)
    whole = ((width, width), fixed)
    sides = len(given)
    key_spec = (
        (HEADS, sides, 1, context, HD),
        lambda b: (0, int(own is None), place, 0, 0),
        (HEADS, 2, blocks, context, HD),
        BF16,
    )
    row_specs = [
        ((HEADS, rows, HD), lambda b: (0, place, 0), (HEADS, blocks * rows, HD), BF16),
        ((1, rows, width), lambda b: (place, 0, 0), (blocks, rows, width), BF16),
    ]
    row_in = [((rows, width), fixed)]
    with_own = own is not None
    wq, wk, wv = kinds
    return kernel_call(
        partial(project_kernel, context, scale, with_own),
        (1,),
        (row_in + [whole]) * with_own + row_in * (other is not None) + [whole] * 2,
        [key_spec] * 2 + row_specs * with_own,
        [],
        2 * width * width * (rows + 4 * context),
        4 * width * (rows + 3 * context),
        *([own, wq] if with_own else []),
        *([other] if other is not None else []),
        wk,
        wv,
        into=into,
    )


def forward_kernel(sets, steps, row_blocks, chunk, q_ref, *refs):
    k_refs, v_refs, refs = refs[:sets], refs[sets : 2 * sets], refs[2 * sets :]
    p_ref, o_ref, sum_ref, s_even, s_odd, top_even, top_odd, v_wide = refs
    t = pl.program_id(0)
    rows, hd = q_ref.shape[-2:]
    keys = p_ref.shape[-1]

    @pl.when(t == 0)
    def _():
        v_wide[:, hd:] = jnp.ones((keys, hd), BF16)

    @pl.when((t > 0) & (lax.rem(t - 1, row_blocks) == 0))
    def _():
        start = 0
        for v_ref in v_refs:
            v_wide[start : start + v_ref.shape[1], :hd] = v_ref[0]
            start += v_ref.shape[1]

    places = []
    for k_ref in k_refs:
        places += [(k_ref, slice(c, c + chunk)) for c in range(0, k_ref.shape[1], chunk)]

    def body(score, weigh, s_now, s_before, top_now, top_before):
        if score:
            q = q_ref[0]
            high = None
        if weigh:
            peak = jnp.max(top_before[...], axis=-1, keepdims=True)
            total = jnp.zeros((rows, 2 * hd), F32)
        for c, (k_ref, within) in enumerate(places):
            at = slice(c * chunk, (c + 1) * chunk)
            if score:
                scores = dot(q, k_ref[0, within, :], 1, 1)
                s_now[:, at] = scores
                for j in range(chunk // LANES):
                    part = scores[:, j * LANES : (j + 1) * LANES]
                    high = part if high is None else jnp.maximum(high, part)
            if weigh:
                soft = jnp.exp2(s_before[:, at] - peak).astype(BF16)
                p_ref[0, :, at] = soft
                total = total + dot(soft, v_wide[at, :], 1, 0)
        if score:
            top_now[...] = high
        if weigh:
            o_ref[...] = total[:, :hd]
            sum_ref[0] = total[:, hd:]

    even = (s_even, s_odd, top_even, top_odd)
    odd = (s_odd, s_even, top_odd, top_even)
    inside = (t > 0) & (t < steps)
    pl.when(inside & (lax.rem(t, 2) == 0))(lambda: body(True, True, *even))
    pl.when(inside & (lax.rem(t, 2) == 1))(lambda: body(True, True, *odd))
    pl.when(t == 0)(lambda: body(True, False, *even))
    pl.when(t == steps)(lambda: body(False, True, *(odd if steps % 2 else even)))


def attention_forward(q, ks, vs, row_blocks, chunk=512):
    heads, total, hd = q.shape
    keys = sum(k.shape[1] for k in ks)
    rows = total // row_blocks
    steps = heads * row_blocks
    ahead = lambda t: jnp.minimum(t, steps - 1)
    behind = lambda t: jnp.maximum(t - 1, 0)
    by_row = lambda t: (behind(t) // row_blocks, behind(t) % row_blocks, 0)
    per_row = ((1, rows, hd), by_row, (heads, total, hd), F32)
    return kernel_call(
        partial(forward_kernel, len(ks), steps, row_blocks, chunk),
        (steps + 1,),
        [((1, rows, hd), lambda t: (ahead(t) // row_blocks, ahead(t) % row_blocks, 0))]
        + [((1, k.shape[1], hd), lambda t: (ahead(t) // row_blocks, 0, 0)) for k in ks]
        + [((1, v.shape[1], hd), lambda t: (behind(t) // row_blocks, 0, 0)) for v in vs],
        [
            ((1, rows, keys), by_row, (heads, total, keys), BF16),
            (
                (rows, hd),
                lambda t: (behind(t) % row_blocks, behind(t) // row_blocks),
                (total, heads * hd),
                F32,
            ),
            per_row,
        ],
        [
            pltpu.VMEM((rows, keys), F32),
            pltpu.VMEM((rows, keys), F32),
            pltpu.VMEM((rows, LANES), F32),
            pltpu.VMEM((rows, LANES), F32),
            pltpu.VMEM((keys, 2 * hd), BF16),
        ],
        8 * heads * total * keys * hd,
        2 * heads * total * keys,
        q,
        *ks,
        *vs,
        exps=heads * total * keys,
    )


def gelu_pair(inner):
    size = jnp.abs(inner) * (0.5**0.5)
    rate = 1.0 / (1.0 + 0.3275911 * size)
    bell = jnp.exp(-(size * size))
    tail = rate * (
        0.254829592
        + rate * (-0.284496736 + rate * (1.421413741 + rate * (-1.453152027 + rate * 1.061405429)))
    )
    tail = 0.5 * tail * bell
    below = jnp.where(inner < 0, tail, 1.0 - tail)
    return inner * below, below + inner * bell * 0.3989422804014327


def dense_kernel(
    blocks, steps, bit_ref, x_ref, o_ref, total_ref, wo, w1, b1, w2, b2, g1, s1, g2, s2, *refs
):
    cot_refs, refs = refs[:blocks], refs[blocks:]
    out_refs, refs = refs[:blocks], refs[blocks:]
    first_ref, grad_ref, delta_ref, keep_ref, send_ref = refs[:5]
    sums, sending, cot, out, arrived, left = refs[5:]
    t = pl.program_id(0)
    width, hidden_width = w1.shape
    rows, half = x_ref.shape[0], (width + 2 * hidden_width) // 2
    vector_rows = sums.shape[0] - 2 * half
    block = cot.shape[0] // blocks
    load = [
        pltpu.make_async_copy(ref, cot.at[pl.ds(j * block, block)], arrived.at[j])
        for j, ref in enumerate(cot_refs)
    ]
    store = [
        pltpu.make_async_copy(out.at[pl.ds(j * block, block)], ref, left.at[j])
        for j, ref in enumerate(out_refs)
    ]

    @pl.when(t == 0)
    def _():
        for copy in load:
            copy.start()
        sums[...] = jnp.zeros_like(sums)

    for j, copy in enumerate(load):
        pl.when(t == j * block // rows)(copy.wait)
    here = pl.ds(pl.multiple_of(t * rows, 16), rows)
    gain_one, gain_two = g1[...].astype(F32), g2[...].astype(F32)
    inverses = [1.0 / total_ref[h] for h in range(HEADS)]
    attended = jnp.concatenate(
        [o_ref[:, h * HD : (h + 1) * HD] * inverses[h] for h in range(HEADS)], axis=1
    )
    attended_low = attended.astype(BF16)
    first_sum = x_ref[...].astype(F32) + dot(attended_low, wo[...], 1, 0)
    hidden, normed_one, inverse_one = norm_forward(first_sum, gain_one, s1[...].astype(F32))
    hidden_low = hidden.astype(BF16)
    inner = dot(hidden_low, w1[...], 1, 0) + b1[...].astype(F32)
    activated, slope = gelu_pair(inner)
    activated = activated.astype(BF16)
    second_sum = hidden + dot(activated, w2[...], 1, 0) + b2[...].astype(F32)
    result, normed_two, inverse_two = norm_forward(second_sum, gain_two, s2[...].astype(F32))
    out[here, :] = result.astype(BF16)
    for j, copy in enumerate(store):
        pl.when(t == ((j + 1) * block - 1) // rows)(copy.start)
    upstream = cot[here, :].astype(F32)
    second_grad, gain_two_sum, shift_two_sum = norm_backward(
        upstream, normed_two, inverse_two, gain_two
    )
    outer_grad = second_grad.astype(BF16)
    at = width + hidden_width
    sums[at : at + hidden_width] += dot(activated, outer_grad, 0, 0)
    inner_grad = (dot(outer_grad, w2[...], 1, 1) * slope).astype(BF16)
    inner_sums = dot(hidden_low, inner_grad, 0, 0)
    for j in range(0, hidden_width, width):
        sums[width + j : 2 * width + j] += inner_sums[:, j : j + width]
    hidden_grad = second_grad + dot(inner_grad, w1[...], 1, 1)
    first_grad, gain_one_sum, shift_one_sum = norm_backward(
        hidden_grad, normed_one, inverse_one, gain_one
    )
    branch_grad = first_grad.astype(BF16)
    first_ref[...] = branch_grad
    sums[:width] += dot(attended_low, branch_grad, 0, 0)
    attended_grad = dot(branch_grad, wo[...], 1, 1)
    for h in range(HEADS):
        at = slice(h * HD, (h + 1) * HD)
        scaled = (attended_grad[:, at] * inverses[h]).astype(BF16)
        grad_ref[h] = scaled
        delta = jnp.sum(scaled.astype(F32) * attended[:, at], axis=-1, keepdims=True)
        delta_ref[h] = jnp.broadcast_to(delta, delta_ref.shape[1:])
    inner_sum = jnp.sum(inner_grad.astype(F32), axis=0)
    vectors = [
        gain_one_sum,
        shift_one_sum,
        gain_two_sum,
        shift_two_sum,
        jnp.sum(outer_grad.astype(F32), axis=0),
    ]
    vectors += [inner_sum[j : j + width] for j in range(0, hidden_width, width)]
    at = width + 2 * hidden_width
    for j, part in enumerate(vectors):
        sums[at + j : at + j + 1, :] += part[None, :]

    @pl.when(t == steps - 1)
    def _():
        bit = bit_ref[0]
        keep = pltpu.make_async_copy(
            sums.at[pl.ds(pl.multiple_of(bit * half, 16), half)],
            keep_ref.at[pl.ds(0, half)],
            arrived.at[0],
        )
        keep_vectors = pltpu.make_async_copy(
            sums.at[pl.ds(2 * half, vector_rows)],
            keep_ref.at[pl.ds(half, vector_rows)],
            arrived.at[1],
        )
        sending[:half] = sums[pl.ds(pl.multiple_of((1 - bit) * half, 16), half)].astype(BF16)
        sending[half:] = sums[2 * half :].astype(BF16)
        send = pltpu.make_async_copy(sending, send_ref, arrived.at[2])
        for copy in (keep, keep_vectors, send):
            copy.start()
        for copy in (*store, keep, keep_vectors, send):
            copy.wait()


def dense(bit, x, cots, attended, total_of, weights, steps=3):
    blocks, block, width = x.shape
    total = blocks * block
    rows = total // steps
    hidden = weights[1].shape[1]
    by_row = ((rows, width), lambda t: (t, 0))
    by_head = ((HEADS, rows, HD), lambda t: (0, t, 0))
    half = width // 2 + hidden
    *out, first_grad, grads, delta, keep, send = kernel_call(
        partial(dense_kernel, blocks, steps),
        (steps,),
        [(None, pltpu.SMEM), by_row, by_row, by_head]
        + [(w.shape, lambda t: (0, 0)) for w in weights]
        + [(None, pl.ANY)] * blocks,
        [(None, pl.ANY, (block, width), BF16)] * blocks
        + [
            (*by_row, (total, width), BF16),
            (*by_head, (HEADS, total, HD), BF16),
            (*by_head, (HEADS, total, HD), F32),
            (None, pl.ANY, (half + VECTORS, width), F32),
            (None, pl.ANY, (half + VECTORS, width), BF16),
        ],
        [
            pltpu.VMEM((2 * half + VECTORS, width), F32),
            pltpu.VMEM((half + VECTORS, width), BF16),
            pltpu.VMEM((total, width), BF16),
            pltpu.VMEM((total, width), BF16),
            pltpu.SemaphoreType.DMA((blocks,)),
            pltpu.SemaphoreType.DMA((blocks,)),
        ],
        6 * total * width * (width + 2 * hidden),
        32 * total * width + 8 * width * (width + 2 * hidden),
        bit,
        x.reshape(total, width),
        attended,
        total_of,
        *weights,
        *cots,
    )
    return out, first_grad, grads, delta, keep, send


def backward_kernel(scale_k, scale_q, carried, q_ref, g_ref, d_ref, p_ref, k_ref, v_ref, *refs):
    if carried:
        before, refs = refs[0], refs[1:]
    kv_ref, dq_ref, ds = refs
    keys, values = k_ref[0], v_ref[0]
    for start in range(0, p_ref.shape[1], ROWS_STEP):
        at = slice(start, start + ROWS_STEP)
        soft_grad = dot(g_ref[0, at, :], values, 1, 1)
        delta = jnp.concatenate([d_ref[0, at, :]] * (keys.shape[0] // LANES), axis=1)
        score_grad = (p_ref[0, at, :].astype(F32) * (soft_grad - delta)).astype(BF16)
        ds[at, :] = score_grad
        query_grad = dot(score_grad, keys, 1, 0)
        if carried:
            query_grad = query_grad + before[0, at, :]
        dq_ref[0, at, :] = (query_grad * scale_q).astype(dq_ref.dtype)
    dv = dot(g_ref[0].T, p_ref[0], 1, 0).T
    dk = dot(q_ref[0].T, ds[...], 1, 0).T * scale_k
    kv_ref[0, 0] = dk.astype(BF16)
    kv_ref[1, 0] = dv.astype(BF16)


def attention_backward(q, g, d, p, k, v, scale_k, scale_q, half, before=None):
    heads, total, hd = q.shape
    keys = k.shape[1] // 2
    row = lambda h: (h, 0, 0)
    key = lambda h: (h, half, 0)
    by_row = ((1, total, hd), row)
    carried = before is not None
    return kernel_call(
        partial(backward_kernel, scale_k, scale_q, carried),
        (heads,),
        [
            by_row,
            by_row,
            by_row,
            ((1, total, keys), lambda h: (h, 0, half)),
            ((1, keys, hd), key),
            ((1, keys, hd), key),
        ]
        + [by_row] * carried,
        [
            ((2, 1, keys, hd), lambda h: (0, h, 0, 0), (2, heads, keys, hd), BF16),
            (*by_row, (heads, total, hd), BF16 if carried else F32),
        ],
        [pltpu.VMEM((total, keys), BF16)],
        12 * heads * total * keys * hd,
        2 * heads * total * keys,
        q,
        g,
        d,
        p,
        k,
        v,
        *[before] * carried,
    )


def side_by_side(parts):
    return jnp.concatenate([part.astype(BF16) for part in parts], axis=1)


def weigh_kernel(
    bit_ref, x_ref, query_ref, own_ref, other_ref, keep_ref, send_ref, sums, sending, left
):
    s = pl.program_id(0)
    blocks, rows, width = x_ref.shape
    context = own_ref.shape[2] // blocks
    per = query_ref.shape[0]
    columns = per * HD
    x = x_ref[...].reshape(blocks * rows, width)
    above = x_ref[:, :context].reshape(blocks * context, width)
    three = [dot(x, side_by_side([query_ref[h] for h in range(per)]), 0, 0)]
    for j in range(2):
        whole = side_by_side(
            [own_ref[j, h].astype(F32) + other_ref[j, h].astype(F32) for h in range(per)]
        )
        three.append(dot(above, whole, 0, 0))
    steps = width // columns
    for j in range(steps):

        @pl.when(s == j)
        def _(j=j):
            for i, part in enumerate(three):
                sums[i * width : (i + 1) * width, j * columns : (j + 1) * columns] = part

    @pl.when(s == steps - 1)
    def _():
        bit = bit_ref[0]
        half = sending.shape[0]
        keep = pltpu.make_async_copy(
            sums.at[pl.ds(pl.multiple_of(bit * half, 16), half)], keep_ref, left.at[0]
        )
        keep.start()
        sending[...] = sums[pl.ds(pl.multiple_of((1 - bit) * half, 16), half)].astype(BF16)
        send = pltpu.make_async_copy(sending, send_ref, left.at[1])
        send.start()
        keep.wait()
        send.wait()


def weigh(bit, x, query_grad, own, other, per=2):
    blocks, rows, width = x.shape
    keys = own.shape[2]
    side = ((2, per, keys, HD), lambda s: (0, s, 0, 0))
    half = 3 * width // 2
    return kernel_call(
        weigh_kernel,
        (HEADS // per,),
        [
            (None, pltpu.SMEM),
            (x.shape, lambda s: (0, 0, 0)),
            ((per, blocks * rows, HD), lambda s: (s, 0, 0)),
            side,
            side,
        ],
        [(None, pl.ANY, (half, width), F32), (None, pl.ANY, (half, width), BF16)],
        [
            pltpu.VMEM((3 * width, width), F32),
            pltpu.VMEM((half, width), BF16),
            pltpu.SemaphoreType.DMA((2,)),
        ],
        2 * width * width * (blocks * rows + 2 * keys),
        2 * width * (2 * blocks * rows + 4 * keys),
        bit,
        x,
        query_grad,
        own,
        other,
    )


def finish_kernel(context, count, first_ref, query_ref, own, other, wq, wk, wv, *refs):
    token_refs, (tokens, left) = refs[:count], refs[count:]
    b = pl.program_id(0)
    query_grad = side_by_side([query_ref[h, 0] for h in range(HEADS)])
    key_grad, value_grad = (
        side_by_side(
            [own[j, h, 0].astype(F32) + other[j, h, 0].astype(F32) for h in range(HEADS)]
        )
        for j in range(2)
    )
    base = first_ref[0].astype(F32) + dot(query_grad, wq[...], 1, 1)
    back = dot(key_grad, wk[...], 1, 1) + dot(value_grad, wv[...], 1, 1)
    tokens[b, :context] = (base[:context] + back).astype(BF16)
    tokens[b, context:] = base[context:].astype(BF16)
    store = [
        pltpu.make_async_copy(tokens.at[j], ref, left.at[j]) for j, ref in enumerate(token_refs)
    ]
    for j, copy in enumerate(store):
        pl.when(b == j)(copy.start)

    @pl.when(b == count - 1)
    def _():
        for copy in store:
            copy.wait()


def finish(ahead, first_grad, own, other, query_grad, kinds, blocks):
    first, last = ahead[0], ahead[-1]
    count = len(ahead)
    at = lambda b: first + b * (last - first)
    total, width = first_grad.shape
    rows = total // blocks
    context = own.shape[2] // blocks
    side = ((2, HEADS, 1, context, HD), lambda b: (0, 0, at(b), 0, 0))
    return kernel_call(
        partial(finish_kernel, context, count),
        (count,),
        [
            ((1, rows, width), lambda b: (at(b), 0, 0)),
            ((HEADS, 1, rows, HD), lambda b: (0, at(b), 0, 0)),
            side,
            side,
        ]
        + [((width, width), lambda b: (0, 0))] * 3,
        [(None, pl.ANY, (rows, width), BF16)] * count,
        [pltpu.VMEM((count, rows, width), BF16), pltpu.SemaphoreType.DMA((count,))],
        2 * count * width * width * (rows + 2 * context),
        6 * count * width * (rows + 2 * context),
        first_grad.reshape(blocks, rows, width),
        query_grad.reshape(HEADS, blocks, rows, HD),
        own.reshape(2, HEADS, blocks, context, HD),
        other.reshape(2, HEADS, blocks, context, HD),
        *kinds,
    )


def unpack_kernel(counts, shares, place_ref, half_ref, *refs):
    outs, (early, late, left) = refs[:6], refs[6:]
    grad_query, grad_key, grad_value, grad_output, grad_inner, grad_outer = outs
    first, second = shares
    across, along = counts
    share = first + second
    for s in range(across):
        for u in range(along):
            at = (s * along + u) * share
            number = (place_ref[1] ^ s) * along + (place_ref[2] ^ u)
            early[pl.ds(pl.multiple_of(number * first, 16), first)] = half_ref[
                at : at + first
            ].astype(F32)
            late[pl.ds(pl.multiple_of(number * second, 16), second)] = half_ref[
                at + first : at + share
            ].astype(F32)
    width, hidden = grad_inner.shape

    def copy_out(pieces):
        copies = [
            pltpu.make_async_copy(source.at[pl.ds(start, size)], ref, left.at[j])
            for j, (source, start, size, ref) in enumerate(pieces)
        ]
        for copy in copies:
            copy.start()
        for copy in copies:
            copy.wait()

    late_refs = [grad_query, grad_key, grad_value]
    early_refs = [grad_output]
    early_refs += [grad_inner.at[:, pl.ds(j, width)] for j in range(0, hidden, width)]
    early_refs += [grad_outer.at[pl.ds(j, width)] for j in range(0, hidden, width)]

    def pieces(source, refs, start):
        end = start + source.shape[0]
        for j, ref in enumerate(refs):
            low, high = max(start, j * width), min(end, (j + 1) * width)
            if low < high:
                yield source, low - start, high - low, ref.at[pl.ds(low - j * width, high - low)]

    for core in range(2):

        @pl.when(place_ref[0] == core)
        def _(core=core):
            copy_out(
                [
                    *pieces(late, late_refs, core * late.shape[0]),
                    *pieces(early, early_refs, core * early.shape[0]),
                ]
            )


def unpack(places, half, counts, shares, hidden, into=()):
    width = half.shape[1]
    total = counts[0] * counts[1]
    shapes = [(width, width)] * 4 + [(width, hidden), (hidden, width)]
    return kernel_call(
        partial(unpack_kernel, counts, shares),
        (1,),
        [(None, pltpu.SMEM), (half.shape, lambda b: (0, 0))],
        [(None, pl.ANY, shape, F32) for shape in shapes],
        [
            pltpu.VMEM((total * shares[0], width), F32),
            pltpu.VMEM((total * shares[1], width), F32),
            pltpu.SemaphoreType.DMA((4 + 2 * hidden // width,)),
        ],
        0,
        6 * half.size,
        places,
        half,
        into=into,
    )


def summing(groups, members):
    grp, ctx = lax.axis_index("grp"), lax.axis_index("ctx")
    planes, along = groups // 2, members // 2
    places = [(g, c) for g in range(groups) for c in range(members)]
    number = lambda g, c: g * members + c
    stages = (
        (2, grp % 2, lambda g, c, s: (g ^ s, c)),
        (
            2 * planes,
            grp // 2 * 2 + ctx % 2,
            lambda g, c, s: (g ^ (s // 2 * 2), c ^ (s % 2)),
        ),
        (along, ctx // 2, lambda g, c, s: (g, c ^ (2 * s))),
    )

    def swap(array, move, s):
        return lax.ppermute(
            array, AXES, [(number(g, c), number(*move(g, c, s))) for g, c in places]
        )

    def reduce_pieces(stage, parts, below=0):
        count, index, _ = stage
        rows = parts[0].shape[0] - below
        piece = rows // count

        def take(s):
            at = (index ^ s) * piece
            taken = sum(lax.dynamic_slice_in_dim(part, at, piece).astype(F32) for part in parts)
            if not below:
                return taken
            return jnp.concatenate([taken, sum(part[rows:].astype(F32) for part in parts)])

        return [take(0)] + [take(s).astype(BF16) for s in range(1, count)]

    def reduce_join(stage, own, came):
        return [own, *came]

    def gather_pieces(stage, part):
        return [part.astype(BF16)] * stage[0]

    def gather_join(stage, own, came):
        return jnp.concatenate([own] + came)

    def send(stage, pieces):
        return [swap(piece, stage[2], s) for s, piece in enumerate(pieces) if s]

    return [
        (partial(reduce_pieces, stage), partial(send, stage), partial(reduce_join, stage))
        for stage in stages
    ] + [
        (partial(gather_pieces, stage), partial(send, stage), partial(gather_join, stage))
        for stage in reversed(stages)
    ], stages


def gathered_plan(
    tokens,
    query_counts,
    cotangent,
    query_weight,
    key_weight,
    value_weight,
    output_weight,
    inner_weight,
    inner_bias,
    outer_weight,
    outer_bias,
    first_gain,
    first_shift,
    second_gain,
    second_shift,
):
    blocks, rows, width = tokens.shape
    groups, members = lax.axis_size("grp"), lax.axis_size("ctx")
    member = lax.axis_index("ctx")
    place = member // 2
    context = CTX // members
    slots = QUERIES // members

    far = blocks // 2
    order = [r for r in range(1, blocks) if r != far] + [0, far]

    def route(r, back=False):
        pairs = []
        for g in range(groups):
            for c in range(members):
                to = (g - g % 2 + c % 2) * members + ((c // 2 + r) % blocks) * 2 + g % 2
                pairs.append((to, g * members + c) if back else (g * members + c, to))
        return pairs

    across = [
        (g * members + c, (g ^ 1) * members + c) for g in range(groups) for c in range(members)
    ]
    tie = lambda *arrays: lax.optimization_barrier(arrays)

    def block_of(array, r):
        return lax.dynamic_index_in_dim(array, lax.rem(place + r, blocks), 0, keepdims=False)

    def outward(block, r):
        return lax.ppermute(block, AXES, route(r))

    def homeward(block, r):
        return lax.ppermute(block, AXES, route(r, True))

    def put(whole, block, r):
        return lax.dynamic_update_index_in_dim(whole, block, lax.rem(place + r, blocks), 0)

    slot = member * slots + jnp.arange(rows, dtype=jnp.int32) - context
    live = (jnp.arange(rows) < context)[None, :] | (slot[None, :] < query_counts[:, None])
    live = live[:, :, None]
    masked = jnp.where(live, cotangent, 0).astype(BF16)

    scale = HD**-0.5
    log2e = 1.4426950408889634
    kinds = (query_weight, key_weight, value_weight)
    *own, own_far = [outward(block_of(tokens, r), r) for r in order]
    other = [lax.ppermute(block, AXES, across) for block in own]
    qkvx = ()
    for j in range(blocks - 1):
        qkvx = project(own[j], other[j], j, blocks, context, kinds, scale * log2e, qkvx)
    own_far, *kvqx = tie(own_far, *qkvx)
    other_far = lax.ppermute(own_far, AXES, across)
    *kv, q, x = project(own_far, None, blocks - 1, blocks, context, kinds, scale * log2e, kvqx)
    other_far, *kv = tie(other_far, *kv)
    k, v = project(None, other_far, blocks - 1, blocks, context, kinds, scale * log2e, kv)
    k, v = (array.reshape(HEADS, 2 * blocks * context, HD) for array in (k, v))

    *cots, q = tie(*[block_of(masked, r) for r in order], q)
    cots = [outward(block, r) for block, r in zip(cots, order, strict=True)]
    p, attended, totals = attention_forward(q, [k], [v], blocks)
    *cots, p = tie(*cots, p)

    lifted = lambda vector: vector.reshape(1, -1)
    weights = (
        output_weight,
        inner_weight,
        lifted(inner_bias),
        outer_weight,
        lifted(outer_bias),
        lifted(first_gain),
        lifted(first_shift),
        lifted(second_gain),
        lifted(second_shift),
    )
    bit = lax.rem(lax.axis_index("grp"), 2).astype(jnp.int32).reshape(1)
    out, first_grad, grads, delta, keep, given = dense(bit, x, cots, attended, totals, weights)

    stages, stages_of = summing(groups, members)
    scale_k = 1.0 / log2e

    added = lambda parts: sum(part.astype(F32) for part in parts)

    def start(stage, *part):
        pieces_of, send, join = stage
        mine, *pieces = pieces_of(*part)
        return pieces, lambda pieces: send([mine] + pieces), partial(join, mine)

    *out, given, grads = tie(*out, given, grads)
    came = lax.ppermute(given, AXES, across)
    home = [homeward(out[j], r) for j, r in enumerate(order[:-2])]
    kv_other, dq = attention_backward(q, grads, delta, p, k, v, scale_k, 1.0, 1)
    *home, came, kv_other, grads = tie(*home, came, kv_other, grads)
    early_parts = [keep, came]
    pieces, send, _ = start(stages[1], early_parts, VECTORS)
    *pieces, kv_other, far_out, grads = tie(*pieces, kv_other, out[-1], grads)
    kv_came = lax.ppermute(kv_other, AXES, across)
    early_came = send(pieces)
    home.append(homeward(far_out, far))
    kv_own, dq = attention_backward(q, grads, delta, p, k, v, scale_k, scale, 0, dq)
    *early_came, home[-1], kv_came, kv_own, keep, came = tie(
        *early_came, home[-1], kv_came, kv_own, *early_parts
    )
    early_parts = [keep, came]

    token_of = lambda places, after: finish(
        places, after, kv_own, kv_came, dq, kinds, blocks
    )
    three = token_of([1], first_grad)[0]
    three, first_grad = tie(three, first_grad)
    three = homeward(three, order[1])
    one, two = token_of([2, 0], first_grad)
    one, two, x = tie(one, two, x)
    keep, given = weigh(bit, x, dq, kv_own, kv_came)
    three, given, first_grad = tie(three, given, first_grad)
    came = lax.ppermute(given, AXES, across)
    last = token_of([3], first_grad)[0]
    came, last = tie(came, last)

    pieces, send, join = start(stages[1], [keep, came])
    *pieces, two = tie(*pieces, two)
    came = send(pieces)
    two = homeward(two, order[0])
    *came, two = tie(*came, two)
    late = added(join(came))
    early = added([stages[1][0](list(early_parts), VECTORS)[0], *early_came])

    along = members // 2
    shares = ((early.shape[0] - VECTORS) // along, late.shape[0] // along)
    both = jnp.concatenate(
        [
            early[:-VECTORS].reshape(along, shares[0], width),
            late.reshape(along, shares[1], width),
            jnp.broadcast_to(early[-VECTORS:], (along, VECTORS, width)),
        ],
        axis=1,
    ).reshape(-1, width)
    pieces, send, join = start(stages[2], [both])
    *pieces, zero_out = tie(*pieces, out[-2])
    came = send(pieces)
    zero_home = homeward(zero_out, order[-2])
    grad_tokens = jnp.zeros((blocks, rows, width), F32)
    grad_tokens = put(grad_tokens, three.astype(F32), order[1])
    *came, zero_home, grad_tokens, one = tie(*came, zero_home, grad_tokens, one)
    home.insert(blocks - 2, zero_home)
    both = added(join(came))
    both, vectors = both[:-VECTORS], both[-VECTORS:]

    pieces, send, join = start(stages[3], both)
    *home, live, one, pieces[0] = tie(*home, live, one, pieces[0])
    came = send(pieces)
    one = homeward(one, order[2])
    grad_tokens = put(grad_tokens, two.astype(F32), order[0])
    *came, one, grad_tokens = tie(*came, one, grad_tokens)
    both = join(came)

    pieces, send, join = start(stages[4], both)
    *pieces, last = tie(*pieces, last)
    came = send(pieces)
    last = homeward(last, far)
    grad_tokens = put(grad_tokens, one.astype(F32), order[2])
    layer_out = jnp.zeros((blocks, rows, width), BF16)
    for block, r in zip(home, order, strict=True):
        layer_out = put(layer_out, jnp.where(block_of(live, r), block, 0).astype(BF16), r)
    *came, last, layer_out, grad_tokens = tie(*came, last, layer_out, grad_tokens)
    both = join(came)
    hidden = inner_weight.shape[1]
    counts = (groups, members // 2)
    mine = [index.astype(jnp.int32) for _, index, _ in stages_of]
    came = lax.ppermute(both, AXES, across)
    sums = unpack(jnp.stack(mine), both, counts, shares, hidden)
    grad_tokens = put(grad_tokens, last.astype(F32), far)
    came, grad_tokens, *sums = tie(came, grad_tokens, *sums)
    theirs = jnp.stack([1 - mine[0], *mine[1:]])
    sums = unpack(theirs, came, counts, shares, hidden, sums)
    return (
        layer_out,
        grad_tokens,
        *sums[:5],
        vectors[5 : 5 + hidden // width].reshape(hidden),
        sums[5],
        vectors[4],
        vectors[0],
        vectors[1],
        vectors[2],
        vectors[3],
    )


def solution(mesh):
    return jax.shard_map(
        gathered_plan if one_chip_each(mesh) else spread_plan,
        mesh=mesh,
        in_specs=(
            P("grp", "ctx", None),
            P("grp"),
            P("grp", "ctx", None),
            P(),
            P(),
            P(),
            P(),
            P(),
            P(),
            P(),
            P(),
            P(),
            P(),
            P(),
            P(),
        ),
        out_specs=(
            P("grp", "ctx", None),
            P("grp", "ctx", None),
            P(),
            P(),
            P(),
            P(),
            P(),
            P(),
            P(),
            P(),
            P(),
            P(),
            P(),
            P(),
        ),
        check_vma=False,
    )
```

```python
from functools import partial

import jax
import jax.numpy as jnp
from jax import lax
from jax.experimental import pallas as pl
from jax.experimental.pallas import tpu as pltpu
from jax.sharding import PartitionSpec as P

HEADS = 4
CTX = 4096
QUERIES = 128
NBLK = 4
HD = 128


EPSILON = 1e-05


def product(left, right):
    return jnp.dot(left, right, preferred_element_type=jnp.float32)


def contract_rows(left, right):
    return lax.dot_general(
        left, right, (((0,), (0,)), ((), ())), preferred_element_type=jnp.float32
    )


def contract_last(left, right):
    return lax.dot_general(
        left, right, (((1,), (1,)), ((), ())), preferred_element_type=jnp.float32
    )


def norm_forward(values, gain, shift):
    center = values - jnp.mean(values, axis=-1, keepdims=True)
    inverse = lax.rsqrt(jnp.mean(center * center, axis=-1, keepdims=True) + EPSILON)
    normed = center * inverse
    return (normed * gain + shift, normed, inverse)


def norm_backward(upstream, normed, inverse, gain):
    scaled = upstream * gain
    plain_mean = jnp.mean(scaled, axis=-1, keepdims=True)
    cross_mean = jnp.mean(scaled * normed, axis=-1, keepdims=True)
    value_grad = inverse * (scaled - plain_mean - normed * cross_mean)
    return (value_grad, jnp.sum(upstream * normed, axis=0), jnp.sum(upstream, axis=0))


def spread_plan(
    tokens,
    query_counts,
    cotangent,
    query_weight,
    key_weight,
    value_weight,
    output_weight,
    inner_weight,
    inner_bias,
    outer_weight,
    outer_bias,
    first_gain,
    first_shift,
    second_gain,
    second_shift,
):
    member = lax.axis_index("ctx")
    ctx_count = lax.axis_size("ctx")
    context_dev = CTX // ctx_count
    query_dev = QUERIES // ctx_count
    nb_dev = tokens.shape[0]
    rows_dev = tokens.shape[1]
    width = tokens.shape[2]
    heads_count = HEADS
    head_width = HD
    block_count = nb_dev // NBLK
    scale = head_width ** (-0.5)
    total_rows = nb_dev * rows_dev
    tokens_flat = tokens.reshape(total_rows, width)
    context_rows = tokens[:, :context_dev]
    context_flat = context_rows.reshape(nb_dev * context_dev, width)
    queries = (
        product(tokens_flat, query_weight).astype(jnp.bfloat16).reshape(nb_dev, rows_dev, width)
    )
    keys_own = (
        product(context_flat, key_weight).astype(jnp.bfloat16).reshape(nb_dev, context_dev, width)
    )
    values_own = (
        product(context_flat, value_weight).astype(jnp.bfloat16).reshape(nb_dev, context_dev, width)
    )
    sources = (keys_own, values_own)

    def to_blocks(array):
        return array.reshape((block_count, NBLK) + array.shape[1:])

    def fetch(source):
        keys_mine, values_mine = source
        keys_flat, values_flat = (
            lax.all_gather(keys_mine, "ctx", axis=1, tiled=True),
            lax.all_gather(values_mine, "ctx", axis=1, tiled=True),
        )
        return (keys_flat, values_flat, keys_mine, values_mine)

    def split_heads(array):
        return array.reshape(array.shape[0], array.shape[1], heads_count, head_width)

    def attend(carry, operands):
        queries_blk, source = operands
        keys_flat, values_flat, keys_mine, values_mine = fetch(source)
        query_heads = split_heads(queries_blk)
        scores = (
            jnp.einsum(
                "nrhd,nkhd->nhrk",
                query_heads,
                split_heads(keys_flat),
                preferred_element_type=jnp.float32,
            )
            * scale
        )
        log_total = jax.nn.logsumexp(scores, axis=-1, keepdims=True)
        soft_low = jnp.exp(scores - log_total).astype(jnp.bfloat16)
        mixed = jnp.einsum(
            "nhrk,nkhd->nrhd",
            soft_low,
            split_heads(values_flat),
            preferred_element_type=jnp.float32,
        )
        attended_blk = mixed.reshape(NBLK, rows_dev, width).astype(jnp.bfloat16)
        return (carry, (attended_blk, log_total[..., 0]))

    zero = jnp.zeros((), jnp.float32)
    _, (attended_b, lse_b) = lax.scan(
        attend, zero, (to_blocks(queries), jax.tree.map(to_blocks, sources))
    )
    attended_flat = attended_b.reshape(total_rows, width)
    slot_local = jnp.arange(rows_dev, dtype=jnp.int32) - context_dev
    slot_global = member * query_dev + slot_local
    live_rows = jnp.logical_or(
        slot_local[None, :] < 0, slot_global[None, :] < query_counts[:, None]
    )
    live_flat = live_rows.astype(jnp.float32).reshape(total_rows, 1)
    inner_bias_f = inner_bias.astype(jnp.float32)
    outer_bias_f = outer_bias.astype(jnp.float32)
    first_gain_f = first_gain.astype(jnp.float32)
    second_gain_f = second_gain.astype(jnp.float32)
    first_sum = tokens_flat.astype(jnp.float32) + product(attended_flat, output_weight)
    hidden, normed_one, inverse_one = norm_forward(
        first_sum, first_gain_f, first_shift.astype(jnp.float32)
    )
    hidden_low = hidden.astype(jnp.bfloat16)
    inner = product(hidden_low, inner_weight) + inner_bias_f
    gelu_value, gelu_back = jax.vjp(partial(jax.nn.gelu, approximate=False), inner)
    activated = gelu_value.astype(jnp.bfloat16)
    second_sum = hidden + product(activated, outer_weight) + outer_bias_f
    result, normed_two, inverse_two = norm_forward(
        second_sum, second_gain_f, second_shift.astype(jnp.float32)
    )
    layer_out = (result * live_flat).astype(jnp.bfloat16).reshape(nb_dev, rows_dev, width)
    upstream = cotangent.reshape(total_rows, width).astype(jnp.float32) * live_flat
    second_grad, grad_second_gain, grad_second_shift = norm_backward(
        upstream, normed_two, inverse_two, second_gain_f
    )
    outer_grad = second_grad.astype(jnp.bfloat16)
    grad_outer = contract_rows(activated, outer_grad)
    grad_outer_bias = jnp.sum(outer_grad.astype(jnp.float32), axis=0)
    inner_grad = gelu_back(contract_last(outer_grad, outer_weight))[0].astype(jnp.bfloat16)
    grad_inner = contract_rows(hidden_low, inner_grad)
    grad_inner_bias = jnp.sum(inner_grad.astype(jnp.float32), axis=0)
    hidden_grad = second_grad + contract_last(inner_grad, inner_weight)
    first_grad, grad_first_gain, grad_first_shift = norm_backward(
        hidden_grad, normed_one, inverse_one, first_gain_f
    )
    branch_grad = first_grad.astype(jnp.bfloat16)
    grad_output = contract_rows(attended_flat, branch_grad)
    attended_grad = (
        contract_last(branch_grad, output_weight)
        .astype(jnp.bfloat16)
        .reshape(nb_dev, rows_dev, width)
    )

    def attend_back(carry, operands):
        queries_blk, grads_blk, lse_blk, source = operands
        keys_flat, values_flat, keys_mine, values_mine = fetch(source)
        query_heads = split_heads(queries_blk)
        grad_heads = split_heads(grads_blk)
        key_heads = split_heads(keys_flat)
        value_heads = split_heads(values_flat)
        scores = (
            jnp.einsum(
                "nrhd,nkhd->nhrk", query_heads, key_heads, preferred_element_type=jnp.float32
            )
            * scale
        )
        soft = jnp.exp(scores - lse_blk[..., None])
        soft_grad = jnp.einsum(
            "nrhd,nkhd->nhrk", grad_heads, value_heads, preferred_element_type=jnp.float32
        )
        row_delta = jnp.sum(soft * soft_grad, axis=-1)
        score_grad = (soft * (soft_grad - row_delta[..., None])).astype(jnp.bfloat16)
        query_grad = (
            jnp.einsum("nhrk,nkhd->nrhd", score_grad, key_heads, preferred_element_type=jnp.float32)
            * scale
        )
        query_grad = query_grad.reshape(NBLK, rows_dev, width).astype(jnp.bfloat16)
        soft_low = soft.astype(jnp.bfloat16)
        key_part = (
            jnp.einsum(
                "nhrk,nrhd->nkhd", score_grad, query_heads, preferred_element_type=jnp.float32
            )
            * scale
        )
        value_part = jnp.einsum(
            "nhrk,nrhd->nkhd", soft_low, grad_heads, preferred_element_type=jnp.float32
        )
        key_sum, value_sum = (
            lax.psum_scatter(
                key_part.reshape(NBLK, -1, width), "ctx", scatter_dimension=1, tiled=True
            ),
            lax.psum_scatter(
                value_part.reshape(NBLK, -1, width), "ctx", scatter_dimension=1, tiled=True
            ),
        )
        key_grad = key_sum.astype(jnp.bfloat16)
        value_grad = value_sum.astype(jnp.bfloat16)
        return (carry, (query_grad, key_grad, value_grad))

    _, (query_grad_b, key_grad_b, value_grad_b) = lax.scan(
        attend_back,
        zero,
        (to_blocks(queries), to_blocks(attended_grad), lse_b, jax.tree.map(to_blocks, sources)),
    )
    query_grad = query_grad_b.reshape(total_rows, width)
    key_grad = key_grad_b.reshape(nb_dev * context_dev, width)
    value_grad = value_grad_b.reshape(nb_dev * context_dev, width)
    grad_query = contract_rows(tokens_flat, query_grad)
    grad_key = contract_rows(context_flat, key_grad)
    grad_value = contract_rows(context_flat, value_grad)
    token_grad = (first_grad + contract_last(query_grad, query_weight)).reshape(
        nb_dev, rows_dev, width
    )
    context_back = (
        contract_last(key_grad, key_weight) + contract_last(value_grad, value_weight)
    ).reshape(nb_dev, context_dev, width)
    grad_tokens = jnp.concatenate(
        [token_grad[:, :context_dev] + context_back, token_grad[:, context_dev:]], axis=1
    )
    finals = lax.psum(
        (
            grad_query,
            grad_key,
            grad_value,
            grad_output,
            grad_inner,
            grad_inner_bias,
            grad_outer,
            grad_outer_bias,
            grad_first_gain,
            grad_first_shift,
            grad_second_gain,
            grad_second_shift,
        ),
        ("grp", "ctx"),
    )
    return (layer_out, grad_tokens) + tuple(finals)


BF16, F32 = jnp.bfloat16, jnp.float32
MIB = 2**20
AXES = ("grp", "ctx")
LANES = 128
VECTORS = 16
ROWS_STEP = 528


def one_chip_each(mesh):
    return mesh.shape["grp"] % 2 == 0 and mesh.shape["ctx"] == 2 * NBLK


def dot(left, right, over_left, over_right):
    return lax.dot_general(
        left, right, (((over_left,), (over_right,)), ((), ())), preferred_element_type=F32
    )


def kernel_call(body, grid, ins, outs, scratch, flops, moved, *operands, exps=0, into=()):
    given = len(ins)

    def run(*refs):
        body(*refs[:given], *refs[given + len(into) :])

    return pl.pallas_call(
        run,
        grid=grid,
        in_specs=[
            pl.BlockSpec(memory_space=index) if shape is None else pl.BlockSpec(shape, index)
            for shape, index in ins
        ]
        + [pl.BlockSpec(memory_space=pl.ANY)] * len(into),
        out_specs=[
            pl.BlockSpec(memory_space=index) if shape is None else pl.BlockSpec(shape, index)
            for shape, index, _, _ in outs
        ],
        out_shape=[jax.ShapeDtypeStruct(shape, kind) for _, _, shape, kind in outs],
        scratch_shapes=scratch,
        input_output_aliases={given + j: j for j in range(len(into))},
        cost_estimate=pl.CostEstimate(flops=flops, bytes_accessed=moved, transcendentals=exps),
        compiler_params=pltpu.CompilerParams(vmem_limit_bytes=60 * MIB),
    )(*operands, *into)


def project_kernel(context, scale, with_own, *refs):
    if with_own:
        own, wq, refs = refs[0], refs[1], refs[2:]
        rows = own[...]
    others = len(refs) - 6 if with_own else len(refs) - 4
    other_refs, (wk, wv), refs = refs[:others], refs[others : others + 2], refs[others + 2 :]
    k_out, v_out = refs[:2]
    sides = []
    if with_own:
        q_out, x_out = refs[2:]
        x_out[0] = rows
        queries = (dot(rows, wq[...], 1, 0) * scale).astype(BF16)
        for h in range(HEADS):
            q_out[h] = queries[:, h * HD : (h + 1) * HD]
        sides.append(rows[:context])
    sides += [ref[:context] for ref in other_refs]
    for side, keys_of in enumerate(sides):
        keys = dot(keys_of, wk[...], 1, 0).astype(BF16)
        values = dot(keys_of, wv[...], 1, 0).astype(BF16)
        for h in range(HEADS):
            k_out[h, side, 0] = keys[:, h * HD : (h + 1) * HD]
            v_out[h, side, 0] = values[:, h * HD : (h + 1) * HD]


def project(own, other, place, blocks, context, kinds, scale, into):
    given = [array for array in (own, other) if array is not None]
    rows, width = given[0].shape
    fixed = lambda b: (0, 0)
    whole = ((width, width), fixed)
    sides = len(given)
    key_spec = (
        (HEADS, sides, 1, context, HD),
        lambda b: (0, int(own is None), place, 0, 0),
        (HEADS, 2, blocks, context, HD),
        BF16,
    )
    row_specs = [
        ((HEADS, rows, HD), lambda b: (0, place, 0), (HEADS, blocks * rows, HD), BF16),
        ((1, rows, width), lambda b: (place, 0, 0), (blocks, rows, width), BF16),
    ]
    row_in = [((rows, width), fixed)]
    with_own = own is not None
    wq, wk, wv = kinds
    return kernel_call(
        partial(project_kernel, context, scale, with_own),
        (1,),
        (row_in + [whole]) * with_own + row_in * (other is not None) + [whole] * 2,
        [key_spec] * 2 + row_specs * with_own,
        [],
        2 * width * width * (rows + 4 * context),
        4 * width * (rows + 3 * context),
        *([own, wq] if with_own else []),
        *([other] if other is not None else []),
        wk,
        wv,
        into=into,
    )


def forward_kernel(sets, steps, row_blocks, chunk, q_ref, *refs):
    k_refs, v_refs, refs = refs[:sets], refs[sets : 2 * sets], refs[2 * sets :]
    p_ref, o_ref, sum_ref, s_even, s_odd, top_even, top_odd, v_wide = refs
    t = pl.program_id(0)
    rows, hd = q_ref.shape[-2:]
    keys = p_ref.shape[-1]

    @pl.when(t == 0)
    def _():
        v_wide[:, hd:] = jnp.ones((keys, hd), BF16)

    @pl.when((t > 0) & (lax.rem(t - 1, row_blocks) == 0))
    def _():
        start = 0
        for v_ref in v_refs:
            v_wide[start : start + v_ref.shape[1], :hd] = v_ref[0]
            start += v_ref.shape[1]

    places = []
    for k_ref in k_refs:
        places += [(k_ref, slice(c, c + chunk)) for c in range(0, k_ref.shape[1], chunk)]

    def body(score, weigh, s_now, s_before, top_now, top_before):
        if score:
            q = q_ref[0]
            high = None
        if weigh:
            peak = jnp.max(top_before[...], axis=-1, keepdims=True)
            total = jnp.zeros((rows, 2 * hd), F32)
        for c, (k_ref, within) in enumerate(places):
            at = slice(c * chunk, (c + 1) * chunk)
            if score:
                scores = dot(q, k_ref[0, within, :], 1, 1)
                s_now[:, at] = scores
                for j in range(chunk // LANES):
                    part = scores[:, j * LANES : (j + 1) * LANES]
                    high = part if high is None else jnp.maximum(high, part)
            if weigh:
                soft = jnp.exp2(s_before[:, at] - peak).astype(BF16)
                p_ref[0, :, at] = soft
                total = total + dot(soft, v_wide[at, :], 1, 0)
        if score:
            top_now[...] = high
        if weigh:
            o_ref[...] = total[:, :hd]
            sum_ref[0] = total[:, hd:]

    even = (s_even, s_odd, top_even, top_odd)
    odd = (s_odd, s_even, top_odd, top_even)
    inside = (t > 0) & (t < steps)
    pl.when(inside & (lax.rem(t, 2) == 0))(lambda: body(True, True, *even))
    pl.when(inside & (lax.rem(t, 2) == 1))(lambda: body(True, True, *odd))
    pl.when(t == 0)(lambda: body(True, False, *even))
    pl.when(t == steps)(lambda: body(False, True, *(odd if steps % 2 else even)))


def attention_forward(q, ks, vs, row_blocks, chunk=512):
    heads, total, hd = q.shape
    keys = sum(k.shape[1] for k in ks)
    rows = total // row_blocks
    steps = heads * row_blocks
    ahead = lambda t: jnp.minimum(t, steps - 1)
    behind = lambda t: jnp.maximum(t - 1, 0)
    by_row = lambda t: (behind(t) // row_blocks, behind(t) % row_blocks, 0)
    per_row = ((1, rows, hd), by_row, (heads, total, hd), F32)
    return kernel_call(
        partial(forward_kernel, len(ks), steps, row_blocks, chunk),
        (steps + 1,),
        [((1, rows, hd), lambda t: (ahead(t) // row_blocks, ahead(t) % row_blocks, 0))]
        + [((1, k.shape[1], hd), lambda t: (ahead(t) // row_blocks, 0, 0)) for k in ks]
        + [((1, v.shape[1], hd), lambda t: (behind(t) // row_blocks, 0, 0)) for v in vs],
        [
            ((1, rows, keys), by_row, (heads, total, keys), BF16),
            (
                (rows, hd),
                lambda t: (behind(t) % row_blocks, behind(t) // row_blocks),
                (total, heads * hd),
                F32,
            ),
            per_row,
        ],
        [
            pltpu.VMEM((rows, keys), F32),
            pltpu.VMEM((rows, keys), F32),
            pltpu.VMEM((rows, LANES), F32),
            pltpu.VMEM((rows, LANES), F32),
            pltpu.VMEM((keys, 2 * hd), BF16),
        ],
        8 * heads * total * keys * hd,
        2 * heads * total * keys,
        q,
        *ks,
        *vs,
        exps=heads * total * keys,
    )


def gelu_pair(inner):
    size = jnp.abs(inner) * (0.5**0.5)
    rate = 1.0 / (1.0 + 0.3275911 * size)
    bell = jnp.exp(-(size * size))
    tail = rate * (
        0.254829592
        + rate * (-0.284496736 + rate * (1.421413741 + rate * (-1.453152027 + rate * 1.061405429)))
    )
    tail = 0.5 * tail * bell
    below = jnp.where(inner < 0, tail, 1.0 - tail)
    return inner * below, below + inner * bell * 0.3989422804014327


def dense_kernel(
    blocks, steps, bit_ref, x_ref, o_ref, total_ref, wo, w1, b1, w2, b2, g1, s1, g2, s2, *refs
):
    cot_refs, refs = refs[:blocks], refs[blocks:]
    out_refs, refs = refs[:blocks], refs[blocks:]
    first_ref, grad_ref, delta_ref, keep_ref, send_ref = refs[:5]
    sums, sending, cot, out, arrived, left = refs[5:]
    t = pl.program_id(0)
    width, hidden_width = w1.shape
    rows, half = x_ref.shape[0], (width + 2 * hidden_width) // 2
    vector_rows = sums.shape[0] - 2 * half
    block = cot.shape[0] // blocks
    load = [
        pltpu.make_async_copy(ref, cot.at[pl.ds(j * block, block)], arrived.at[j])
        for j, ref in enumerate(cot_refs)
    ]
    store = [
        pltpu.make_async_copy(out.at[pl.ds(j * block, block)], ref, left.at[j])
        for j, ref in enumerate(out_refs)
    ]

    @pl.when(t == 0)
    def _():
        for copy in load:
            copy.start()
        sums[...] = jnp.zeros_like(sums)

    for j, copy in enumerate(load):
        pl.when(t == j * block // rows)(copy.wait)
    here = pl.ds(pl.multiple_of(t * rows, 16), rows)
    gain_one, gain_two = g1[...].astype(F32), g2[...].astype(F32)
    inverses = [1.0 / total_ref[h] for h in range(HEADS)]
    attended = jnp.concatenate(
        [o_ref[:, h * HD : (h + 1) * HD] * inverses[h] for h in range(HEADS)], axis=1
    )
    attended_low = attended.astype(BF16)
    first_sum = x_ref[...].astype(F32) + dot(attended_low, wo[...], 1, 0)
    hidden, normed_one, inverse_one = norm_forward(first_sum, gain_one, s1[...].astype(F32))
    hidden_low = hidden.astype(BF16)
    inner = dot(hidden_low, w1[...], 1, 0) + b1[...].astype(F32)
    activated, slope = gelu_pair(inner)
    activated = activated.astype(BF16)
    second_sum = hidden + dot(activated, w2[...], 1, 0) + b2[...].astype(F32)
    result, normed_two, inverse_two = norm_forward(second_sum, gain_two, s2[...].astype(F32))
    out[here, :] = result.astype(BF16)
    for j, copy in enumerate(store):
        pl.when(t == ((j + 1) * block - 1) // rows)(copy.start)
    upstream = cot[here, :].astype(F32)
    second_grad, gain_two_sum, shift_two_sum = norm_backward(
        upstream, normed_two, inverse_two, gain_two
    )
    outer_grad = second_grad.astype(BF16)
    at = width + hidden_width
    sums[at : at + hidden_width] += dot(activated, outer_grad, 0, 0)
    inner_grad = (dot(outer_grad, w2[...], 1, 1) * slope).astype(BF16)
    inner_sums = dot(hidden_low, inner_grad, 0, 0)
    for j in range(0, hidden_width, width):
        sums[width + j : 2 * width + j] += inner_sums[:, j : j + width]
    hidden_grad = second_grad + dot(inner_grad, w1[...], 1, 1)
    first_grad, gain_one_sum, shift_one_sum = norm_backward(
        hidden_grad, normed_one, inverse_one, gain_one
    )
    branch_grad = first_grad.astype(BF16)
    first_ref[...] = branch_grad
    sums[:width] += dot(attended_low, branch_grad, 0, 0)
    attended_grad = dot(branch_grad, wo[...], 1, 1)
    for h in range(HEADS):
        at = slice(h * HD, (h + 1) * HD)
        scaled = (attended_grad[:, at] * inverses[h]).astype(BF16)
        grad_ref[h] = scaled
        delta = jnp.sum(scaled.astype(F32) * attended[:, at], axis=-1, keepdims=True)
        delta_ref[h] = jnp.broadcast_to(delta, delta_ref.shape[1:])
    inner_sum = jnp.sum(inner_grad.astype(F32), axis=0)
    vectors = [
        gain_one_sum,
        shift_one_sum,
        gain_two_sum,
        shift_two_sum,
        jnp.sum(outer_grad.astype(F32), axis=0),
    ]
    vectors += [inner_sum[j : j + width] for j in range(0, hidden_width, width)]
    at = width + 2 * hidden_width
    for j, part in enumerate(vectors):
        sums[at + j : at + j + 1, :] += part[None, :]

    @pl.when(t == steps - 1)
    def _():
        bit = bit_ref[0]
        keep = pltpu.make_async_copy(
            sums.at[pl.ds(pl.multiple_of(bit * half, 16), half)],
            keep_ref.at[pl.ds(0, half)],
            arrived.at[0],
        )
        keep_vectors = pltpu.make_async_copy(
            sums.at[pl.ds(2 * half, vector_rows)],
            keep_ref.at[pl.ds(half, vector_rows)],
            arrived.at[1],
        )
        sending[:half] = sums[pl.ds(pl.multiple_of((1 - bit) * half, 16), half)].astype(BF16)
        sending[half:] = sums[2 * half :].astype(BF16)
        send = pltpu.make_async_copy(sending, send_ref, arrived.at[2])
        for copy in (keep, keep_vectors, send):
            copy.start()
        for copy in (*store, keep, keep_vectors, send):
            copy.wait()


def dense(bit, x, cots, attended, total_of, weights, steps=3):
    blocks, block, width = x.shape
    total = blocks * block
    rows = total // steps
    hidden = weights[1].shape[1]
    by_row = ((rows, width), lambda t: (t, 0))
    by_head = ((HEADS, rows, HD), lambda t: (0, t, 0))
    half = width // 2 + hidden
    *out, first_grad, grads, delta, keep, send = kernel_call(
        partial(dense_kernel, blocks, steps),
        (steps,),
        [(None, pltpu.SMEM), by_row, by_row, by_head]
        + [(w.shape, lambda t: (0, 0)) for w in weights]
        + [(None, pl.ANY)] * blocks,
        [(None, pl.ANY, (block, width), BF16)] * blocks
        + [
            (*by_row, (total, width), BF16),
            (*by_head, (HEADS, total, HD), BF16),
            (*by_head, (HEADS, total, HD), F32),
            (None, pl.ANY, (half + VECTORS, width), F32),
            (None, pl.ANY, (half + VECTORS, width), BF16),
        ],
        [
            pltpu.VMEM((2 * half + VECTORS, width), F32),
            pltpu.VMEM((half + VECTORS, width), BF16),
            pltpu.VMEM((total, width), BF16),
            pltpu.VMEM((total, width), BF16),
            pltpu.SemaphoreType.DMA((blocks,)),
            pltpu.SemaphoreType.DMA((blocks,)),
        ],
        6 * total * width * (width + 2 * hidden),
        32 * total * width + 8 * width * (width + 2 * hidden),
        bit,
        x.reshape(total, width),
        attended,
        total_of,
        *weights,
        *cots,
    )
    return out, first_grad, grads, delta, keep, send


def backward_kernel(scale_k, scale_q, carried, q_ref, g_ref, d_ref, p_ref, k_ref, v_ref, *refs):
    if carried:
        before, refs = refs[0], refs[1:]
    kv_ref, dq_ref, ds = refs
    keys, values = k_ref[0], v_ref[0]
    for start in range(0, p_ref.shape[1], ROWS_STEP):
        at = slice(start, start + ROWS_STEP)
        soft_grad = dot(g_ref[0, at, :], values, 1, 1)
        delta = jnp.concatenate([d_ref[0, at, :]] * (keys.shape[0] // LANES), axis=1)
        score_grad = (p_ref[0, at, :].astype(F32) * (soft_grad - delta)).astype(BF16)
        ds[at, :] = score_grad
        query_grad = dot(score_grad, keys, 1, 0)
        if carried:
            query_grad = query_grad + before[0, at, :]
        dq_ref[0, at, :] = (query_grad * scale_q).astype(dq_ref.dtype)
    dv = dot(g_ref[0].T, p_ref[0], 1, 0).T
    dk = dot(q_ref[0].T, ds[...], 1, 0).T * scale_k
    kv_ref[0, 0] = dk.astype(BF16)
    kv_ref[1, 0] = dv.astype(BF16)


def attention_backward(q, g, d, p, k, v, scale_k, scale_q, half, before=None):
    heads, total, hd = q.shape
    keys = k.shape[1] // 2
    row = lambda h: (h, 0, 0)
    key = lambda h: (h, half, 0)
    by_row = ((1, total, hd), row)
    carried = before is not None
    return kernel_call(
        partial(backward_kernel, scale_k, scale_q, carried),
        (heads,),
        [
            by_row,
            by_row,
            by_row,
            ((1, total, keys), lambda h: (h, 0, half)),
            ((1, keys, hd), key),
            ((1, keys, hd), key),
        ]
        + [by_row] * carried,
        [
            ((2, 1, keys, hd), lambda h: (0, h, 0, 0), (2, heads, keys, hd), BF16),
            (*by_row, (heads, total, hd), BF16 if carried else F32),
        ],
        [pltpu.VMEM((total, keys), BF16)],
        12 * heads * total * keys * hd,
        2 * heads * total * keys,
        q,
        g,
        d,
        p,
        k,
        v,
        *[before] * carried,
    )


def side_by_side(parts):
    return jnp.concatenate([part.astype(BF16) for part in parts], axis=1)


def weigh_kernel(
    bit_ref, x_ref, query_ref, own_ref, other_ref, keep_ref, send_ref, sums, sending, left
):
    s = pl.program_id(0)
    blocks, rows, width = x_ref.shape
    context = own_ref.shape[2] // blocks
    per = query_ref.shape[0]
    columns = per * HD
    x = x_ref[...].reshape(blocks * rows, width)
    above = x_ref[:, :context].reshape(blocks * context, width)
    three = [dot(x, side_by_side([query_ref[h] for h in range(per)]), 0, 0)]
    for j in range(2):
        whole = side_by_side(
            [own_ref[j, h].astype(F32) + other_ref[j, h].astype(F32) for h in range(per)]
        )
        three.append(dot(above, whole, 0, 0))
    steps = width // columns
    for j in range(steps):

        @pl.when(s == j)
        def _(j=j):
            for i, part in enumerate(three):
                sums[i * width : (i + 1) * width, j * columns : (j + 1) * columns] = part

    @pl.when(s == steps - 1)
    def _():
        bit = bit_ref[0]
        half = sending.shape[0]
        keep = pltpu.make_async_copy(
            sums.at[pl.ds(pl.multiple_of(bit * half, 16), half)], keep_ref, left.at[0]
        )
        keep.start()
        sending[...] = sums[pl.ds(pl.multiple_of((1 - bit) * half, 16), half)].astype(BF16)
        send = pltpu.make_async_copy(sending, send_ref, left.at[1])
        send.start()
        keep.wait()
        send.wait()


def weigh(bit, x, query_grad, own, other, per=2):
    blocks, rows, width = x.shape
    keys = own.shape[2]
    side = ((2, per, keys, HD), lambda s: (0, s, 0, 0))
    half = 3 * width // 2
    return kernel_call(
        weigh_kernel,
        (HEADS // per,),
        [
            (None, pltpu.SMEM),
            (x.shape, lambda s: (0, 0, 0)),
            ((per, blocks * rows, HD), lambda s: (s, 0, 0)),
            side,
            side,
        ],
        [(None, pl.ANY, (half, width), F32), (None, pl.ANY, (half, width), BF16)],
        [
            pltpu.VMEM((3 * width, width), F32),
            pltpu.VMEM((half, width), BF16),
            pltpu.SemaphoreType.DMA((2,)),
        ],
        2 * width * width * (blocks * rows + 2 * keys),
        2 * width * (2 * blocks * rows + 4 * keys),
        bit,
        x,
        query_grad,
        own,
        other,
    )


def finish_kernel(context, count, first_ref, query_ref, own, other, wq, wk, wv, *refs):
    token_refs, (tokens, left) = refs[:count], refs[count:]
    b = pl.program_id(0)
    query_grad = side_by_side([query_ref[h, 0] for h in range(HEADS)])
    key_grad, value_grad = (
        side_by_side(
            [own[j, h, 0].astype(F32) + other[j, h, 0].astype(F32) for h in range(HEADS)]
        )
        for j in range(2)
    )
    base = first_ref[0].astype(F32) + dot(query_grad, wq[...], 1, 1)
    back = dot(key_grad, wk[...], 1, 1) + dot(value_grad, wv[...], 1, 1)
    tokens[b, :context] = (base[:context] + back).astype(BF16)
    tokens[b, context:] = base[context:].astype(BF16)
    store = [
        pltpu.make_async_copy(tokens.at[j], ref, left.at[j]) for j, ref in enumerate(token_refs)
    ]
    for j, copy in enumerate(store):
        pl.when(b == j)(copy.start)

    @pl.when(b == count - 1)
    def _():
        for copy in store:
            copy.wait()


def finish(ahead, first_grad, own, other, query_grad, kinds, blocks):
    first, last = ahead[0], ahead[-1]
    count = len(ahead)
    at = lambda b: first + b * (last - first)
    total, width = first_grad.shape
    rows = total // blocks
    context = own.shape[2] // blocks
    side = ((2, HEADS, 1, context, HD), lambda b: (0, 0, at(b), 0, 0))
    return kernel_call(
        partial(finish_kernel, context, count),
        (count,),
        [
            ((1, rows, width), lambda b: (at(b), 0, 0)),
            ((HEADS, 1, rows, HD), lambda b: (0, at(b), 0, 0)),
            side,
            side,
        ]
        + [((width, width), lambda b: (0, 0))] * 3,
        [(None, pl.ANY, (rows, width), BF16)] * count,
        [pltpu.VMEM((count, rows, width), BF16), pltpu.SemaphoreType.DMA((count,))],
        2 * count * width * width * (rows + 2 * context),
        6 * count * width * (rows + 2 * context),
        first_grad.reshape(blocks, rows, width),
        query_grad.reshape(HEADS, blocks, rows, HD),
        own.reshape(2, HEADS, blocks, context, HD),
        other.reshape(2, HEADS, blocks, context, HD),
        *kinds,
    )


def unpack_kernel(counts, shares, place_ref, half_ref, *refs):
    outs, (early, late, left) = refs[:6], refs[6:]
    grad_query, grad_key, grad_value, grad_output, grad_inner, grad_outer = outs
    first, second = shares
    across, along = counts
    share = first + second
    for s in range(across):
        for u in range(along):
            at = (s * along + u) * share
            number = (place_ref[1] ^ s) * along + (place_ref[2] ^ u)
            early[pl.ds(pl.multiple_of(number * first, 16), first)] = half_ref[
                at : at + first
            ].astype(F32)
            late[pl.ds(pl.multiple_of(number * second, 16), second)] = half_ref[
                at + first : at + share
            ].astype(F32)
    width, hidden = grad_inner.shape

    def copy_out(pieces):
        copies = [
            pltpu.make_async_copy(source.at[pl.ds(start, size)], ref, left.at[j])
            for j, (source, start, size, ref) in enumerate(pieces)
        ]
        for copy in copies:
            copy.start()
        for copy in copies:
            copy.wait()

    late_refs = [grad_query, grad_key, grad_value]
    early_refs = [grad_output]
    early_refs += [grad_inner.at[:, pl.ds(j, width)] for j in range(0, hidden, width)]
    early_refs += [grad_outer.at[pl.ds(j, width)] for j in range(0, hidden, width)]

    def pieces(source, refs, start):
        end = start + source.shape[0]
        for j, ref in enumerate(refs):
            low, high = max(start, j * width), min(end, (j + 1) * width)
            if low < high:
                yield source, low - start, high - low, ref.at[pl.ds(low - j * width, high - low)]

    for core in range(2):

        @pl.when(place_ref[0] == core)
        def _(core=core):
            copy_out(
                [
                    *pieces(late, late_refs, core * late.shape[0]),
                    *pieces(early, early_refs, core * early.shape[0]),
                ]
            )


def unpack(places, half, counts, shares, hidden, into=()):
    width = half.shape[1]
    total = counts[0] * counts[1]
    shapes = [(width, width)] * 4 + [(width, hidden), (hidden, width)]
    return kernel_call(
        partial(unpack_kernel, counts, shares),
        (1,),
        [(None, pltpu.SMEM), (half.shape, lambda b: (0, 0))],
        [(None, pl.ANY, shape, F32) for shape in shapes],
        [
            pltpu.VMEM((total * shares[0], width), F32),
            pltpu.VMEM((total * shares[1], width), F32),
            pltpu.SemaphoreType.DMA((4 + 2 * hidden // width,)),
        ],
        0,
        6 * half.size,
        places,
        half,
        into=into,
    )


def summing(groups, members):
    grp, ctx = lax.axis_index("grp"), lax.axis_index("ctx")
    planes, along = groups // 2, members // 2
    places = [(g, c) for g in range(groups) for c in range(members)]
    number = lambda g, c: g * members + c
    stages = (
        (2, grp % 2, lambda g, c, s: (g ^ s, c)),
        (
            2 * planes,
            grp // 2 * 2 + ctx % 2,
            lambda g, c, s: (g ^ (s // 2 * 2), c ^ (s % 2)),
        ),
        (along, ctx // 2, lambda g, c, s: (g, c ^ (2 * s))),
    )

    def swap(array, move, s):
        return lax.ppermute(
            array, AXES, [(number(g, c), number(*move(g, c, s))) for g, c in places]
        )

    def reduce_pieces(stage, parts, below=0):
        count, index, _ = stage
        rows = parts[0].shape[0] - below
        piece = rows // count

        def take(s):
            at = (index ^ s) * piece
            taken = sum(lax.dynamic_slice_in_dim(part, at, piece).astype(F32) for part in parts)
            if not below:
                return taken
            return jnp.concatenate([taken, sum(part[rows:].astype(F32) for part in parts)])

        return [take(0)] + [take(s).astype(BF16) for s in range(1, count)]

    def reduce_join(stage, own, came):
        return [own, *came]

    def gather_pieces(stage, part):
        return [part.astype(BF16)] * stage[0]

    def gather_join(stage, own, came):
        return jnp.concatenate([own] + came)

    def send(stage, pieces):
        return [swap(piece, stage[2], s) for s, piece in enumerate(pieces) if s]

    return [
        (partial(reduce_pieces, stage), partial(send, stage), partial(reduce_join, stage))
        for stage in stages
    ] + [
        (partial(gather_pieces, stage), partial(send, stage), partial(gather_join, stage))
        for stage in reversed(stages)
    ], stages


def gathered_plan(
    tokens,
    query_counts,
    cotangent,
    query_weight,
    key_weight,
    value_weight,
    output_weight,
    inner_weight,
    inner_bias,
    outer_weight,
    outer_bias,
    first_gain,
    first_shift,
    second_gain,
    second_shift,
):
    blocks, rows, width = tokens.shape
    groups, members = lax.axis_size("grp"), lax.axis_size("ctx")
    member = lax.axis_index("ctx")
    place = member // 2
    context = CTX // members
    slots = QUERIES // members

    far = blocks // 2
    order = [r for r in range(1, blocks) if r != far] + [0, far]

    def route(r, back=False):
        pairs = []
        for g in range(groups):
            for c in range(members):
                to = (g - g % 2 + c % 2) * members + ((c // 2 + r) % blocks) * 2 + g % 2
                pairs.append((to, g * members + c) if back else (g * members + c, to))
        return pairs

    across = [
        (g * members + c, (g ^ 1) * members + c) for g in range(groups) for c in range(members)
    ]
    tie = lambda *arrays: lax.optimization_barrier(arrays)

    def block_of(array, r):
        return lax.dynamic_index_in_dim(array, lax.rem(place + r, blocks), 0, keepdims=False)

    def outward(block, r):
        return lax.ppermute(block, AXES, route(r))

    def homeward(block, r):
        return lax.ppermute(block, AXES, route(r, True))

    def put(whole, block, r):
        return lax.dynamic_update_index_in_dim(whole, block, lax.rem(place + r, blocks), 0)

    slot = member * slots + jnp.arange(rows, dtype=jnp.int32) - context
    live = (jnp.arange(rows) < context)[None, :] | (slot[None, :] < query_counts[:, None])
    live = live[:, :, None]
    masked = jnp.where(live, cotangent, 0).astype(BF16)

    scale = HD**-0.5
    log2e = 1.4426950408889634
    kinds = (query_weight, key_weight, value_weight)
    *own, own_far = [outward(block_of(tokens, r), r) for r in order]
    other = [lax.ppermute(block, AXES, across) for block in own]
    qkvx = ()
    for j in range(blocks - 1):
        qkvx = project(own[j], other[j], j, blocks, context, kinds, scale * log2e, qkvx)
    own_far, *kvqx = tie(own_far, *qkvx)
    other_far = lax.ppermute(own_far, AXES, across)
    *kv, q, x = project(own_far, None, blocks - 1, blocks, context, kinds, scale * log2e, kvqx)
    other_far, *kv = tie(other_far, *kv)
    k, v = project(None, other_far, blocks - 1, blocks, context, kinds, scale * log2e, kv)
    k, v = (array.reshape(HEADS, 2 * blocks * context, HD) for array in (k, v))

    *cots, q = tie(*[block_of(masked, r) for r in order], q)
    cots = [outward(block, r) for block, r in zip(cots, order, strict=True)]
    p, attended, totals = attention_forward(q, [k], [v], blocks)
    *cots, p = tie(*cots, p)

    lifted = lambda vector: vector.reshape(1, -1)
    weights = (
        output_weight,
        inner_weight,
        lifted(inner_bias),
        outer_weight,
        lifted(outer_bias),
        lifted(first_gain),
        lifted(first_shift),
        lifted(second_gain),
        lifted(second_shift),
    )
    bit = lax.rem(lax.axis_index("grp"), 2).astype(jnp.int32).reshape(1)
    out, first_grad, grads, delta, keep, given = dense(bit, x, cots, attended, totals, weights)

    stages, stages_of = summing(groups, members)
    scale_k = 1.0 / log2e

    added = lambda parts: sum(part.astype(F32) for part in parts)

    def start(stage, *part):
        pieces_of, send, join = stage
        mine, *pieces = pieces_of(*part)
        return pieces, lambda pieces: send([mine] + pieces), partial(join, mine)

    *out, given, grads = tie(*out, given, grads)
    came = lax.ppermute(given, AXES, across)
    home = [homeward(out[j], r) for j, r in enumerate(order[:-2])]
    kv_other, dq = attention_backward(q, grads, delta, p, k, v, scale_k, 1.0, 1)
    *home, came, kv_other, grads = tie(*home, came, kv_other, grads)
    early_parts = [keep, came]
    pieces, send, _ = start(stages[1], early_parts, VECTORS)
    *pieces, kv_other, far_out, grads = tie(*pieces, kv_other, out[-1], grads)
    kv_came = lax.ppermute(kv_other, AXES, across)
    early_came = send(pieces)
    home.append(homeward(far_out, far))
    kv_own, dq = attention_backward(q, grads, delta, p, k, v, scale_k, scale, 0, dq)
    *early_came, home[-1], kv_came, kv_own, keep, came = tie(
        *early_came, home[-1], kv_came, kv_own, *early_parts
    )
    early_parts = [keep, came]

    token_of = lambda places, after: finish(
        places, after, kv_own, kv_came, dq, kinds, blocks
    )
    keep, given = weigh(bit, x, dq, kv_own, kv_came)
    given, first_grad = tie(given, first_grad)
    came = lax.ppermute(given, AXES, across)
    two, three = token_of([0, 1], first_grad)
    came, two, three, first_grad = tie(came, two, three, first_grad)

    pieces, send, join = start(stages[1], [keep, came])
    *pieces, two, three, first_grad = tie(*pieces, two, three, first_grad)
    came = send(pieces)
    two, three = homeward(two, order[0]), homeward(three, order[1])
    one, last = token_of([2, 3], first_grad)
    *came, two, three, one, last = tie(*came, two, three, one, last)
    late = added(join(came))
    early = added([stages[1][0](list(early_parts), VECTORS)[0], *early_came])

    along = members // 2
    shares = ((early.shape[0] - VECTORS) // along, late.shape[0] // along)
    both = jnp.concatenate(
        [
            early[:-VECTORS].reshape(along, shares[0], width),
            late.reshape(along, shares[1], width),
            jnp.broadcast_to(early[-VECTORS:], (along, VECTORS, width)),
        ],
        axis=1,
    ).reshape(-1, width)
    pieces, send, join = start(stages[2], [both])
    *pieces, zero_out = tie(*pieces, out[-2])
    came = send(pieces)
    zero_home = homeward(zero_out, order[-2])
    grad_tokens = jnp.zeros((blocks, rows, width), F32)
    grad_tokens = put(grad_tokens, three.astype(F32), order[1])
    *came, zero_home, grad_tokens, one = tie(*came, zero_home, grad_tokens, one)
    home.insert(blocks - 2, zero_home)
    both = added(join(came))
    both, vectors = both[:-VECTORS], both[-VECTORS:]

    pieces, send, join = start(stages[3], both)
    *home, live, one, pieces[0] = tie(*home, live, one, pieces[0])
    came = send(pieces)
    one = homeward(one, order[2])
    grad_tokens = put(grad_tokens, two.astype(F32), order[0])
    *came, one, grad_tokens = tie(*came, one, grad_tokens)
    both = join(came)

    pieces, send, join = start(stages[4], both)
    *pieces, last = tie(*pieces, last)
    came = send(pieces)
    last = homeward(last, far)
    grad_tokens = put(grad_tokens, one.astype(F32), order[2])
    layer_out = jnp.zeros((blocks, rows, width), BF16)
    for block, r in zip(home, order, strict=True):
        layer_out = put(layer_out, jnp.where(block_of(live, r), block, 0).astype(BF16), r)
    *came, last, layer_out, grad_tokens = tie(*came, last, layer_out, grad_tokens)
    both = join(came)
    hidden = inner_weight.shape[1]
    counts = (groups, members // 2)
    mine = [index.astype(jnp.int32) for _, index, _ in stages_of]
    came = lax.ppermute(both, AXES, across)
    sums = unpack(jnp.stack(mine), both, counts, shares, hidden)
    grad_tokens = put(grad_tokens, last.astype(F32), far)
    came, grad_tokens, *sums = tie(came, grad_tokens, *sums)
    theirs = jnp.stack([1 - mine[0], *mine[1:]])
    sums = unpack(theirs, came, counts, shares, hidden, sums)
    return (
        layer_out,
        grad_tokens,
        *sums[:5],
        vectors[5 : 5 + hidden // width].reshape(hidden),
        sums[5],
        vectors[4],
        vectors[0],
        vectors[1],
        vectors[2],
        vectors[3],
    )


def solution(mesh):
    return jax.shard_map(
        gathered_plan if one_chip_each(mesh) else spread_plan,
        mesh=mesh,
        in_specs=(
            P("grp", "ctx", None),
            P("grp"),
            P("grp", "ctx", None),
            P(),
            P(),
            P(),
            P(),
            P(),
            P(),
            P(),
            P(),
            P(),
            P(),
            P(),
            P(),
        ),
        out_specs=(
            P("grp", "ctx", None),
            P("grp", "ctx", None),
            P(),
            P(),
            P(),
            P(),
            P(),
            P(),
            P(),
            P(),
            P(),
            P(),
            P(),
            P(),
        ),
        check_vma=False,
    )
```
